32 devices in a mesh: fsdp: 8 (over z, x), factor: 4 (over y, core).
Axes of the slice: x: 2, y: 2, z: 4, core: 2. Of those that a mesh axis runs over, the one named last changes fastest.
Arguments:
- activations: bfloat16 [32, 16, 16, 512], P(('fsdp', 'factor')), may hold values from -12 to 12
- cotangent: bfloat16 [32, 16, 16, 512], P(('fsdp', 'factor')), may hold values from -0.6684369 to 0.6684369
- weight: bfloat16 [4608, 512], P('fsdp'), may hold values from -0.09375 to 0.09375
- a_factor_old: float32 [4608, 4608], P('factor', 'fsdp'), may hold values from -0.11785113 to 5, as said below
- g_factor_old: float32 [512, 512], P('factor'), may hold values from -0.35355339 to 5, as said below
- a_inverse: float32 [4608, 4608], P('fsdp', 'factor'), may hold values from -0.09375 to 0.09375
- g_inverse: float32 [512, 512], replicated, may hold values from -0.25 to 0.25
Outputs:
- conv_out: bfloat16 [32, 16, 16, 512], P(('fsdp', 'factor'))
- a_factor: float32 [4608, 4608], P('factor', 'fsdp')
- g_factor: float32 [512, 512], P('factor')
- natural_grad: bfloat16 [4608, 512], P('fsdp', 'factor')
The draws below stay inside these ranges and needn't reach their ends.
Inputs may be any that keep to these rules, and one draw needn't show every extreme that they name: `a_factor_old`: a symmetric matrix. `g_factor_old`: a symmetric matrix.
All inputs are finite; a program needn't handle non-finite values.
Results may differ from the reference program's by a relative error of at most 0.0017.
Values may be sent and summed in bfloat16 or wider, within the bound.
No kernel may reach another device: no remote copies, remote signals or barrier semaphores. Data moves between devices by JAX's collectives and lax.ppermute only.
A program may use at most 192 MiB of HBM per device.

```python
import math
import jax
import jax.numpy as jnp
from jax import lax

C = 512
FAN = 4608
S = 16
BATCH = 32
N_FACTOR = 4


def box_smooth(noise):
    side = noise.shape[1] - 2
    total = noise[:, 0:side, 0:side, :]
    for row_off in range(3):
        for col_off in range(3):
            if row_off + col_off > 0:
                total = total + noise[:, row_off:row_off + side, col_off:col_off + side, :]
    return total / 3.0


def textured_maps(key):
    keys = jax.random.split(key, 3)
    shape = (BATCH, S + 2, S + 2, C)
    noise = jax.random.normal(keys[0], shape, jnp.float32)
    field = box_smooth(noise)
    partner = jax.random.permutation(keys[1], C)
    mixed_field = (field + 0.6 * field[:, :, :, partner]) / math.sqrt(1.36)
    channel_scale = jnp.exp(jax.random.uniform(keys[2], (C,), jnp.float32, math.log(0.3), math.log(3.0)))
    result = mixed_field * channel_scale
    return jnp.clip(result, -12.0, 12.0)


def covariance_like(key, order):
    keys = jax.random.split(key, 2)
    diag_values = jnp.exp(jax.random.uniform(keys[0], (order,), jnp.float32, math.log(0.2), math.log(5.0)))
    raw = jax.random.normal(keys[1], (order, order), jnp.float32)
    spread = 1.2 / math.sqrt(order)
    symmetric = jnp.clip((raw + raw.T) * 0.70710678, -6.0, 6.0) * spread
    rows = jax.lax.broadcasted_iota(jnp.int32, (order, order), 0)
    cols = jax.lax.broadcasted_iota(jnp.int32, (order, order), 1)
    on_diag = rows == cols
    return jnp.where(on_diag, diag_values[:, None] * jnp.ones((1, order), jnp.float32), symmetric)


def draw_activations(key, part):
    return textured_maps(jax.random.fold_in(key, 11)).astype(jnp.bfloat16)


def draw_cotangent(key, part):
    maps = textured_maps(jax.random.fold_in(key, 23))
    image_ids = jax.lax.broadcasted_iota(jnp.int32, (BATCH, 1, 1, C), 0)
    channel_ids = jax.lax.broadcasted_iota(jnp.int32, (BATCH, 1, 1, C), 3)
    block_width = C // N_FACTOR
    owned = channel_ids // block_width == image_ids % N_FACTOR
    boost = jnp.where(owned, 5.0, 1.0).astype(jnp.float32)
    return (maps * boost / (S * math.sqrt(BATCH))).astype(jnp.bfloat16)


def draw_a_factor_old(key, part):
    return covariance_like(jax.random.fold_in(key, 37), 9 * C)


def draw_g_factor_old(key, part):
    return covariance_like(jax.random.fold_in(key, 41), C)


def levels(own_key, dims, cuts, smallest, largest):
    gain, own = 1.0, jax.random.fold_in(own_key, 6)
    for axis_at, blocks in cuts:
        steps = jnp.exp(jax.random.uniform(jax.random.fold_in(own, axis_at), (blocks,), jnp.float32, smallest / len(cuts), largest / len(cuts)))
        gain = gain * jnp.repeat(steps, dims[axis_at] // blocks).reshape([-1 if axis == axis_at else 1 for axis in range(len(dims))])
    return gain


def centred(own_key, shape, width, reach, shards=(), held_as=jnp.bfloat16):
    entries = width * jax.random.normal(own_key, shape, jnp.float32)
    if shards:
        entries = entries * levels(own_key, shape, shards, -0.22, 0.18)
    return jnp.clip(entries, -reach, reach).astype(held_as)


def setup_inputs(seed: int = 0) -> dict:
    splits = jax.random.split(jax.random.key(seed), 8)
    activations = draw_activations(jax.random.fold_in(splits[7], 71), 0)
    cotangent = draw_cotangent(jax.random.fold_in(splits[7], 71), 0)
    weight = centred(splits[2], (FAN, C), FAN ** -0.5, 0.09375, ((0, 8),))
    a_factor_old = draw_a_factor_old(jax.random.fold_in(splits[7], 71), 0)
    g_factor_old = draw_g_factor_old(jax.random.fold_in(splits[7], 71), 0)
    a_inverse = centred(splits[5], (FAN, FAN), FAN ** -0.5, 0.09375, ((0, 8), (1, 4)), jnp.float32)
    g_inverse = centred(splits[6], (C, C), C ** -0.5, 0.25, (), jnp.float32)
    return dict(activations=activations, cotangent=cotangent, weight=weight, a_factor_old=a_factor_old, g_factor_old=g_factor_old, a_inverse=a_inverse, g_inverse=g_inverse)


def unfold(images):
    padded = jnp.pad(images, ((0, 0), (1, 1), (1, 1), (0, 0)))
    tap_list = [padded[:, row_off:row_off + S, col_off:col_off + S, :] for row_off in range(3) for col_off in range(3)]
    return jnp.concatenate(tap_list, axis=3).reshape(-1, 9 * C)


def reference(activations, cotangent, weight, a_factor_old, g_factor_old, a_inverse, g_inverse):
    blocks = BATCH // 16
    act_blocks = activations.reshape(blocks, 16, S, S, C)
    cot_blocks = cotangent.reshape(blocks, 16, S, S, C)

    def block_step(carry, pieces):
        a_acc, grad_acc, g_acc = carry
        patches = unfold(pieces[0])
        cot_flat = pieces[1].reshape(-1, C)
        outputs = jnp.dot(patches, weight, preferred_element_type=jnp.float32).astype(jnp.bfloat16)
        a_acc = a_acc + jnp.dot(patches.T, patches, preferred_element_type=jnp.float32)
        grad_acc = grad_acc + jnp.dot(patches.T, cot_flat, preferred_element_type=jnp.float32)
        g_acc = g_acc + jnp.dot(cot_flat.T, cot_flat, preferred_element_type=jnp.float32)
        return (a_acc, grad_acc, g_acc), outputs.reshape(16, S, S, C)

    start_carry = (jnp.zeros((9 * C, 9 * C), jnp.float32), jnp.zeros((9 * C, C), jnp.float32), jnp.zeros((C, C), jnp.float32))
    (a_acc, grad_acc, g_acc), conv_blocks = lax.scan(block_step, start_carry, (act_blocks, cot_blocks))
    conv_out = conv_blocks.reshape(BATCH, S, S, C)
    pixel_total = float(BATCH * S * S)
    a_factor = 0.5 * a_factor_old + 0.5 * (a_acc / pixel_total)
    g_factor = 0.5 * g_factor_old + 0.5 * g_acc
    mixed = jnp.dot(grad_acc, g_inverse, precision=lax.Precision.HIGHEST, preferred_element_type=jnp.float32)
    natural_grad = jnp.dot(a_inverse, mixed, precision=lax.Precision.HIGHEST, preferred_element_type=jnp.float32).astype(jnp.bfloat16)
    return (conv_out, a_factor, g_factor, natural_grad)
```

```python
import jax
import jax.numpy as jnp
from jax import lax
from jax.sharding import PartitionSpec as P


def by_rows(first_op, second_op):
    return lax.dot_general(
        first_op, second_op, (((0,), (0,)), ((), ())), preferred_element_type=jnp.float32
    )


def moved(array, axis, target):
    count = lax.axis_size(axis)
    return lax.ppermute(array, axis, [(at, target(at) % count) for at in range(count)])


def tile_of_patches(images, start, width):
    side, channels = images.shape[1], images.shape[3]
    padded = jnp.pad(images, ((0, 0), (1, 1), (1, 1), (0, 0)))
    first_tap, offset = start // channels, start % channels
    rolled = lax.dynamic_slice_in_dim(
        jnp.concatenate([padded, padded], axis=3), offset, channels, 3
    )
    lane = lax.broadcasted_iota(jnp.int32, (1, 1, 1, channels), 3)

    def tap(index):
        index = jnp.minimum(index, 8)
        return lax.dynamic_slice(
            rolled, (0, index // 3, index % 3, 0), (images.shape[0], side, side, channels)
        )

    pieces = []
    for at in range(0, width, channels):
        step = at // channels
        piece = jnp.where(lane < channels - offset, tap(first_tap + step), tap(first_tap + step + 1))
        pieces.append(piece[..., : min(channels, width - at)])
    return jnp.concatenate(pieces, axis=3).reshape(-1, width)


def per_device(activations, cotangent, weight, a_factor_old, g_factor_old, a_inverse, g_inverse):
    channels = activations.shape[3]
    n_fsdp, n_factor = lax.axis_size("fsdp"), lax.axis_size("factor")
    n_layer, n_pair = n_fsdp // 2, n_factor // 2
    fsdp_at, factor_at = lax.axis_index("fsdp"), lax.axis_index("factor")
    core_at, pair_at = factor_at % 2, factor_at // 2
    rows, cols = a_factor_old.shape
    strip = channels // n_fsdp
    block = channels // n_factor

    def over_layer(array, step):
        return moved(array, "fsdp", lambda at: at + 2 * step)

    def over_side(array):
        return moved(array, "fsdp", lambda at: at ^ 1)

    def over_pair(array, step):
        return moved(array, "factor", lambda at: at + 2 * step)

    def over_core(array):
        return moved(array, "factor", lambda at: at ^ 1)

    own_cot = cotangent.reshape(-1, channels)
    strips = lax.all_to_all(
        own_cot.T.reshape(n_fsdp, strip, own_cot.shape[0]), "fsdp", split_axis=0, concat_axis=0
    )
    strips_by_pair = [strips] + [over_pair(strips, step) for step in range(1, n_pair)]

    layers = [activations] + [over_layer(activations, step) for step in range(1, n_layer)]
    cov_pair = jnp.zeros((cols, 2 * rows), jnp.float32)
    grad_pair = jnp.zeros((strip, 2 * rows), jnp.float32)
    group_images = []
    for step, layer in enumerate(layers):
        near = [layer] + [over_pair(layer, pair) for pair in range(1, n_pair)]
        if step % 2 == 0:
            aside = over_side(layer)
            far = [aside] + [over_pair(aside, pair) for pair in range(1, n_pair)]
        else:
            far = [over_side(image) for image in near]
        if step == 0:
            group_images = near
        images = jnp.concatenate(near + far, axis=0)
        row_tile = tile_of_patches(images, pair_at * (2 * rows), 2 * rows)
        col_tile = tile_of_patches(images, fsdp_at * cols, cols)
        owner = (fsdp_at - 2 * step) % n_fsdp
        cot_list = [
            lax.dynamic_index_in_dim(strips_by_pair[pair], which, 0, keepdims=False)
            for which in (owner, owner ^ 1)
            for pair in range(n_pair)
        ]
        cov_pair = cov_pair + by_rows(col_tile, row_tile)
        grad_pair = grad_pair + jnp.dot(
            jnp.concatenate(cot_list, axis=1), row_tile, preferred_element_type=jnp.float32
        )

    def own_half(array):
        halves = array.reshape(array.shape[0], 2, rows)
        mine = lax.dynamic_index_in_dim(halves, core_at, 1, keepdims=False)
        theirs = lax.dynamic_index_in_dim(halves, 1 - core_at, 1, keepdims=False)
        return mine + over_core(theirs)

    grad_own = own_half(grad_pair)
    cov_own = own_half(cov_pair)
    pixel_total = float(
        activations.shape[0] * activations.shape[1] * activations.shape[2] * n_fsdp * n_factor
    )
    a_factor = 0.5 * a_factor_old + (0.5 / pixel_total) * cov_own.T

    grad_layers = [grad_own] + [over_layer(grad_own, step) for step in range(1, n_layer)]
    near_grads = jnp.concatenate(grad_layers, axis=0)
    grad_cols = jnp.concatenate([near_grads, over_side(near_grads)], axis=0)
    came_from = (fsdp_at - 2 * jnp.arange(n_layer)) % n_fsdp
    came_from = jnp.concatenate([came_from, came_from ^ 1])
    inverse_rows = g_inverse.reshape(n_fsdp, strip, channels)[came_from].reshape(channels, channels)
    partial = lax.dot_general(
        a_inverse,
        grad_cols,
        (((1,), (1,)), ((), ())),
        precision=lax.Precision.HIGH,
        preferred_element_type=jnp.float32,
    )
    partial = jnp.dot(
        partial, inverse_rows, precision=lax.Precision.HIGH, preferred_element_type=jnp.float32
    )
    by_block = partial.reshape(-1, n_pair, 2, block)
    mine = lax.dynamic_index_in_dim(by_block, core_at, 2, keepdims=False)
    theirs = lax.dynamic_index_in_dim(by_block, 1 - core_at, 2, keepdims=False)
    by_pair = mine + over_core(theirs)
    result = lax.dynamic_index_in_dim(by_pair, pair_at, 1, keepdims=False)
    for step in range(1, n_pair):
        away = lax.dynamic_index_in_dim(by_pair, (pair_at + step) % n_pair, 1, keepdims=False)
        result = result + over_pair(away, step)
    natural_grad = result.astype(jnp.bfloat16)

    weight_part = lax.dynamic_slice_in_dim(weight, factor_at * block, block, 1)
    kernel = lax.all_gather(weight_part, "fsdp", axis=0, tiled=True).reshape(3, 3, channels, block)
    near_images = jnp.concatenate(group_images, axis=0)
    maps = lax.conv_general_dilated(
        jnp.concatenate([near_images, over_core(near_images)], axis=0),
        kernel,
        (1, 1),
        "SAME",
        dimension_numbers=("NHWC", "HWIO", "NHWC"),
        preferred_element_type=jnp.float32,
    ).astype(jnp.bfloat16)
    maps = maps.reshape((2, n_pair) + activations.shape[:3] + (block,))
    own_maps = []
    for pair in range(n_pair):
        for other in range(2):
            own_maps.append(
                maps[other, pair]
                if pair + other == 0
                else moved(
                    maps[other, pair], "factor", lambda at, o=other, p=pair: (at ^ o) - 2 * p
                )
            )
    own_maps = jnp.stack(own_maps)
    conv_out = jnp.concatenate(
        [
            lax.dynamic_index_in_dim(
                own_maps,
                2 * ((at // 2 - pair_at) % n_pair) + (at + core_at) % 2,
                0,
                keepdims=False,
            )
            for at in range(n_factor)
        ],
        axis=3,
    )

    g_partial = lax.psum_scatter(
        by_rows(own_cot, own_cot), "factor", scatter_dimension=0, tiled=True
    )
    g_factor = 0.5 * g_factor_old + 0.5 * lax.psum(g_partial, "fsdp")
    return (conv_out, a_factor, g_factor, natural_grad)


def solution(mesh):
    images = P(("fsdp", "factor"), None, None, None)
    return jax.shard_map(
        per_device,
        mesh=mesh,
        in_specs=(
            images,
            images,
            P("fsdp", None),
            P("factor", "fsdp"),
            P("factor", None),
            P("fsdp", "factor"),
            P(),
        ),
        out_specs=(
            images,
            P("factor", "fsdp"),
            P("factor", None),
            P("fsdp", "factor"),
        ),
        check_vma=False,
    )
```

```python
import jax
import jax.numpy as jnp
from jax import lax
from jax.experimental import pallas as pl
from jax.experimental.pallas import tpu as pltpu
from jax.sharding import PartitionSpec as P

LANES = 128


def by_rows(first_op, second_op):
    return lax.dot_general(
        first_op, second_op, (((0,), (0,)), ((), ())), preferred_element_type=jnp.float32
    )


def moved(array, axis, target):
    count = lax.axis_size(axis)
    return lax.ppermute(array, axis, [(at, target(at) % count) for at in range(count)])


def tile_of_patches(images, start, width):
    side, channels = images.shape[1], images.shape[3]
    padded = jnp.pad(images, ((0, 0), (1, 1), (1, 1), (0, 0)))
    first_tap, offset = start // channels, start % channels
    rolled = lax.dynamic_slice_in_dim(
        jnp.concatenate([padded, padded], axis=3), offset, channels, 3
    )
    lane = lax.broadcasted_iota(jnp.int32, (1, 1, 1, channels), 3)

    def tap(index):
        index = jnp.minimum(index, 8)
        return lax.dynamic_slice(
            rolled, (0, index // 3, index % 3, 0), (images.shape[0], side, side, channels)
        )

    pieces = []
    for at in range(0, width, channels):
        step = at // channels
        piece = jnp.where(lane < channels - offset, tap(first_tap + step), tap(first_tap + step + 1))
        pieces.append(piece[..., : min(channels, width - at)])
    return jnp.concatenate(pieces, axis=3).reshape(-1, width)


def products_kernel(n_pair, first, *refs):
    place = refs[0]
    image_refs = refs[1 : 1 + 2 * n_pair]
    strip_refs = refs[1 + 2 * n_pair : 1 + 3 * n_pair]
    refs = refs[1 + 3 * n_pair :]
    before, refs = (None, refs) if first else (refs[:4], refs[4:])
    totals, (shifted, turned, left) = refs[:4], refs[4:]
    n_images, side, channels = len(image_refs), image_refs[0].shape[1], image_refs[0].shape[3]
    spots = side * side
    cols, rows = totals[0].shape
    strip = totals[1].shape[0]
    fsdp_at = place[2]

    spot = lax.broadcasted_iota(jnp.int32, (spots, LANES), 0) % side
    empty = jnp.zeros((side, channels), jnp.bfloat16)
    for at, ref in enumerate(image_refs):
        for col_off in range(3):
            shifted[col_off, at, 0] = empty
            shifted[col_off, at, side + 1] = empty
        shifted[1, at, 1 : side + 1] = ref[0]
        for lane in range(0, channels, LANES):
            part = ref[0, :, :, lane : lane + LANES].reshape(spots, LANES).astype(jnp.float32)
            before_it = jnp.where(spot == 0, 0.0, pltpu.roll(part, 1, 0))
            after_it = jnp.where(spot == side - 1, 0.0, pltpu.roll(part, spots - 1, 0))
            for col_off, moved_part in ((0, before_it), (2, after_it)):
                shifted[col_off, at, 1 : side + 1, :, lane : lane + LANES] = moved_part.astype(
                    jnp.bfloat16
                ).reshape(side, side, LANES)

    def lanes_of_tap(tap, lane):
        piece = shifted[tap % 3, :, pl.ds(tap // 3, side), :, pl.ds(pl.multiple_of(lane, LANES), LANES)]
        return piece.reshape(n_images * spots, LANES)

    first_tap = (fsdp_at * cols) // channels
    for step in range(2):
        tap = jnp.minimum(first_tap + step, 8)
        for lane in range(0, channels, LANES):
            turned[step, lane : lane + LANES, :] = lanes_of_tap(tap, lane).T
    for at in range(cols // strip):
        start = fsdp_at * cols + at * strip
        left[at * strip : (at + 1) * strip, :] = turned[
            start // channels - first_tap, pl.ds(pl.multiple_of(start % channels, strip), strip), :
        ]
    for far in range(2):
        for pair in range(n_pair):
            at = far * n_pair + pair
            left[cols : cols + strip, at * spots : (at + 1) * spots] = strip_refs[pair][place[3 + far]]

    tiles_per = rows // LANES

    def lanes_at(index):
        whose = jnp.where(index >= tiles_per, 1, 0)
        start = (place[whose] * tiles_per + index - whose * tiles_per) * LANES
        return lanes_of_tap(start // channels, start % channels)

    def product(first_index, count):
        right = jnp.concatenate([lanes_at(first_index + k) for k in range(count)], axis=1)
        return jnp.dot(left[...], right, preferred_element_type=jnp.float32)

    def keep(whose, lane, count, value):
        at = pl.ds(pl.multiple_of(lane, LANES), count * LANES)
        for kind, part in ((0, value[:cols]), (1, value[cols:])):
            if not first:
                part = part + before[2 * whose + kind][:, at]
            totals[2 * whose + kind][:, at] = part

    half = tiles_per // 2

    @pl.loop(0, half)
    def _(step):
        keep(0, step * 2 * LANES, 2, product(2 * step, 2))

    if tiles_per % 2:
        both = product(2 * half, 2)
        keep(0, 2 * half * LANES, 1, both[:, :LANES])
        keep(1, 0, 1, both[:, LANES:])

    odd = tiles_per % 2

    @pl.loop(0, half)
    def _(step):
        keep(1, (odd + 2 * step) * LANES, 2, product(tiles_per + odd + 2 * step, 2))


def add_products(place, images, strips, before, cols, rows):
    n_images, channels, strip = len(images), images[0].shape[3], strips[0].shape[1]
    spots = images[0].shape[1] * images[0].shape[2]
    shapes = [jax.ShapeDtypeStruct((height, rows), jnp.float32) for height in (cols, strip)] * 2
    whole = pl.BlockSpec(memory_space=pltpu.VMEM)
    operands = [place, *images, *strips, *(before or [])]
    n_front = 1 + n_images + len(strips)
    return pl.pallas_call(
        lambda *refs: products_kernel(len(strips), before is None, *refs),
        out_shape=shapes,
        in_specs=[pl.BlockSpec(memory_space=pltpu.SMEM)] + [whole] * (len(operands) - 1),
        out_specs=[whole] * 4,
        scratch_shapes=[
            pltpu.VMEM((3, n_images, images[0].shape[1] + 2, images[0].shape[2], channels), jnp.bfloat16),
            pltpu.VMEM((2, channels, n_images * spots), jnp.bfloat16),
            pltpu.VMEM((cols + strip, n_images * spots), jnp.bfloat16),
        ],
        input_output_aliases={} if before is None else {n_front + k: k for k in range(4)},
        compiler_params=pltpu.CompilerParams(vmem_limit_bytes=40 * 1024 * 1024),
        cost_estimate=pl.CostEstimate(
            flops=4 * (cols + strip) * rows * n_images * spots,
            bytes_accessed=4 * 4 * (cols + strip) * rows,
            transcendentals=0,
        ),
    )(*operands)


def per_device(activations, cotangent, weight, a_factor_old, g_factor_old, a_inverse, g_inverse):
    channels = activations.shape[3]
    n_fsdp, n_factor = lax.axis_size("fsdp"), lax.axis_size("factor")
    n_layer, n_pair = n_fsdp // 2, n_factor // 2
    fsdp_at, factor_at = lax.axis_index("fsdp"), lax.axis_index("factor")
    core_at, pair_at = factor_at % 2, factor_at // 2
    rows, cols = a_factor_old.shape
    strip = channels // n_fsdp
    block = channels // n_factor

    def over_layer(array, step):
        return moved(array, "fsdp", lambda at: at + 2 * step)

    def over_side(array):
        return moved(array, "fsdp", lambda at: at ^ 1)

    def over_pair(array, step):
        return moved(array, "factor", lambda at: at + 2 * step)

    def over_core(array):
        return moved(array, "factor", lambda at: at ^ 1)

    own_cot = cotangent.reshape(-1, channels)
    strips = lax.all_to_all(
        own_cot.T.reshape(n_fsdp, strip, own_cot.shape[0]), "fsdp", split_axis=0, concat_axis=0
    )
    strips_by_pair = [strips] + [over_pair(strips, step) for step in range(1, n_pair)]

    layers = [activations] + [over_layer(activations, step) for step in range(1, n_layer)]
    aligned = rows % LANES == 0 and channels % LANES == 0 and activations.shape[0] == 1
    totals = None
    group_images = []
    for step, layer in enumerate(layers):
        near = [layer] + [over_pair(layer, pair) for pair in range(1, n_pair)]
        if step % 2 == 0:
            aside = over_side(layer)
            far = [aside] + [over_pair(aside, pair) for pair in range(1, n_pair)]
        else:
            far = [over_side(image) for image in near]
        if step == 0:
            group_images = near
        owner = (fsdp_at - 2 * step) % n_fsdp
        if aligned:
            place = jnp.stack([factor_at ^ 1, factor_at, fsdp_at, owner, owner ^ 1])
            totals = add_products(place, near + far, strips_by_pair, totals, cols, rows)
            continue
        images = jnp.concatenate(near + far, axis=0)
        col_tile = tile_of_patches(images, fsdp_at * cols, cols)
        cot_tile = jnp.concatenate(
            [
                lax.dynamic_index_in_dim(strips_by_pair[pair], which, 0, keepdims=False)
                for which in (owner, owner ^ 1)
                for pair in range(n_pair)
            ],
            axis=1,
        )
        more = []
        for tile in (factor_at ^ 1, factor_at):
            row_tile = tile_of_patches(images, tile * rows, rows)
            more.append(by_rows(col_tile, row_tile))
            more.append(jnp.dot(cot_tile, row_tile, preferred_element_type=jnp.float32))
        totals = more if totals is None else [total + new for total, new in zip(totals, more)]

    grad_own = totals[3] + over_core(totals[1])
    cov_own = totals[2] + over_core(totals[0])
    pixel_total = float(
        activations.shape[0] * activations.shape[1] * activations.shape[2] * n_fsdp * n_factor
    )
    a_factor = 0.5 * a_factor_old + (0.5 / pixel_total) * cov_own.T

    grad_layers = [grad_own] + [over_layer(grad_own, step) for step in range(1, n_layer)]
    near_grads = jnp.concatenate(grad_layers, axis=0)
    grad_cols = jnp.concatenate([near_grads, over_side(near_grads)], axis=0)
    came_from = (fsdp_at - 2 * jnp.arange(n_layer)) % n_fsdp
    came_from = jnp.concatenate([came_from, came_from ^ 1])
    order = [
        (2 * ((pair_at + step) % n_pair) + (core_at + other) % 2) * block
        for other in (1, 0)
        for step in range(n_pair)
    ]
    inverse = jnp.concatenate(
        [lax.dynamic_slice_in_dim(g_inverse, at, block, 1) for at in order], axis=1
    )
    inverse = inverse.reshape(n_fsdp, strip, channels)
    inverse = jnp.concatenate(
        [lax.dynamic_index_in_dim(inverse, came_from[at], 0, keepdims=False) for at in range(n_fsdp)]
    )
    partial = lax.dot_general(
        a_inverse,
        grad_cols,
        (((1,), (1,)), ((), ())),
        precision=lax.Precision.HIGH,
        preferred_element_type=jnp.float32,
    )
    partial = jnp.dot(
        partial, inverse, precision=lax.Precision.HIGH, preferred_element_type=jnp.float32
    )
    by_pair = partial[:, channels // 2 :] + over_core(partial[:, : channels // 2])
    result = by_pair[:, :block]
    for step in range(1, n_pair):
        result = result + over_pair(by_pair[:, step * block : (step + 1) * block], step)
    natural_grad = result.astype(jnp.bfloat16)

    weight_part = lax.dynamic_slice_in_dim(weight, factor_at * block, block, 1)
    kernel = lax.all_gather(weight_part, "fsdp", axis=0, tiled=True).reshape(3, 3, channels, block)
    near_images = jnp.concatenate(group_images, axis=0)
    maps = lax.conv_general_dilated(
        jnp.concatenate([near_images, over_core(near_images)], axis=0),
        kernel,
        (1, 1),
        "SAME",
        dimension_numbers=("NHWC", "HWIO", "NHWC"),
        preferred_element_type=jnp.float32,
    ).astype(jnp.bfloat16)
    maps = maps.reshape((2, n_pair) + activations.shape[:3] + (block,))
    own_maps = []
    for pair in range(n_pair):
        for other in range(2):
            own_maps.append(
                maps[other, pair]
                if pair + other == 0
                else moved(
                    maps[other, pair], "factor", lambda at, o=other, p=pair: (at ^ o) - 2 * p
                )
            )
    own_maps = jnp.stack(own_maps)
    conv_out = jnp.concatenate(
        [
            lax.dynamic_index_in_dim(
                own_maps,
                2 * ((at // 2 - pair_at) % n_pair) + (at + core_at) % 2,
                0,
                keepdims=False,
            )
            for at in range(n_factor)
        ],
        axis=3,
    )

    g_partial = [
        by_rows(lax.dynamic_slice_in_dim(own_cot, at, block, 1), own_cot) for at in order
    ]
    g_pairs = jnp.concatenate(g_partial[n_pair:]) + over_core(jnp.concatenate(g_partial[:n_pair]))
    g_sum = g_pairs[:block]
    for step in range(1, n_pair):
        g_sum = g_sum + over_pair(g_pairs[step * block : (step + 1) * block], step)
    distance = 1
    while distance < n_fsdp:
        g_sum = g_sum + moved(g_sum, "fsdp", lambda at, d=distance: at ^ d)
        distance *= 2
    g_factor = 0.5 * g_factor_old + 0.5 * g_sum
    return (conv_out, a_factor, g_factor, natural_grad)


def solution(mesh):
    images = P(("fsdp", "factor"), None, None, None)
    return jax.shard_map(
        per_device,
        mesh=mesh,
        in_specs=(
            images,
            images,
            P("fsdp", None),
            P("factor", "fsdp"),
            P("factor", None),
            P("fsdp", "factor"),
            P(),
        ),
        out_specs=(
            images,
            P("factor", "fsdp"),
            P("factor", None),
            P("fsdp", "factor"),
        ),
        check_vma=False,
    )
```

```python
import jax
import jax.numpy as jnp
from jax import lax
from jax.experimental import pallas as pl
from jax.experimental.pallas import tpu as pltpu
from jax.sharding import PartitionSpec as P

LANES = 128


def by_rows(first_op, second_op):
    return lax.dot_general(
        first_op, second_op, (((0,), (0,)), ((), ())), preferred_element_type=jnp.float32
    )


def moved(array, axis, target):
    count = lax.axis_size(axis)
    return lax.ppermute(array, axis, [(at, target(at) % count) for at in range(count)])


def tile_of_patches(images, start, width):
    side, channels = images.shape[1], images.shape[3]
    padded = jnp.pad(images, ((0, 0), (1, 1), (1, 1), (0, 0)))
    first_tap, offset = start // channels, start % channels
    rolled = lax.dynamic_slice_in_dim(
        jnp.concatenate([padded, padded], axis=3), offset, channels, 3
    )
    lane = lax.broadcasted_iota(jnp.int32, (1, 1, 1, channels), 3)

    def tap(index):
        index = jnp.minimum(index, 8)
        return lax.dynamic_slice(
            rolled, (0, index // 3, index % 3, 0), (images.shape[0], side, side, channels)
        )

    pieces = []
    for at in range(0, width, channels):
        step = at // channels
        piece = jnp.where(lane < channels - offset, tap(first_tap + step), tap(first_tap + step + 1))
        pieces.append(piece[..., : min(channels, width - at)])
    return jnp.concatenate(pieces, axis=3).reshape(-1, width)


def products_kernel(n_pair, first, *refs):
    place = refs[0]
    image_refs = refs[1 : 1 + 2 * n_pair]
    strip_refs = refs[1 + 2 * n_pair : 1 + 3 * n_pair]
    refs = refs[1 + 3 * n_pair :]
    before, refs = (None, refs) if first else (refs[:4], refs[4:])
    totals, (shifted, turned, left) = refs[:4], refs[4:]
    n_images, side, channels = len(image_refs), image_refs[0].shape[1], image_refs[0].shape[3]
    spots = side * side
    cols, rows = totals[0].shape
    strip = totals[1].shape[0]
    fsdp_at = place[2]

    spot = lax.broadcasted_iota(jnp.int32, (spots, LANES), 0) % side
    empty = jnp.zeros((side, channels), jnp.bfloat16)
    for at, ref in enumerate(image_refs):
        for col_off in range(3):
            shifted[col_off, at, 0] = empty
            shifted[col_off, at, side + 1] = empty
        shifted[1, at, 1 : side + 1] = ref[0]
        for lane in range(0, channels, LANES):
            part = ref[0, :, :, lane : lane + LANES].reshape(spots, LANES).astype(jnp.float32)
            before_it = jnp.where(spot == 0, 0.0, pltpu.roll(part, 1, 0))
            after_it = jnp.where(spot == side - 1, 0.0, pltpu.roll(part, spots - 1, 0))
            for col_off, moved_part in ((0, before_it), (2, after_it)):
                shifted[col_off, at, 1 : side + 1, :, lane : lane + LANES] = moved_part.astype(
                    jnp.bfloat16
                ).reshape(side, side, LANES)

    def lanes_of_tap(tap, lane):
        piece = shifted[tap % 3, :, pl.ds(tap // 3, side), :, pl.ds(pl.multiple_of(lane, LANES), LANES)]
        return piece.reshape(n_images * spots, LANES)

    start = fsdp_at * cols
    inside = start % LANES
    for at in range(0, turned.shape[0], LANES):
        lane = start - inside + at
        tap = jnp.minimum(lane // channels, 8)
        turned[at : at + LANES, :] = lanes_of_tap(tap, lane % channels).T
    left[:cols, :] = turned[pl.ds(pl.multiple_of(inside, strip), cols), :]
    for far in range(2):
        for pair in range(n_pair):
            at = far * n_pair + pair
            left[cols : cols + strip, at * spots : (at + 1) * spots] = strip_refs[pair][place[3 + far]]

    tiles_per = rows // LANES

    def lanes_at(index):
        whose = jnp.where(index >= tiles_per, 1, 0)
        start = (place[whose] * tiles_per + index - whose * tiles_per) * LANES
        return lanes_of_tap(start // channels, start % channels)

    def product(first_index, count):
        right = jnp.concatenate([lanes_at(first_index + k) for k in range(count)], axis=1)
        return jnp.dot(left[...], right, preferred_element_type=jnp.float32)

    def keep(whose, lane, count, value):
        at = pl.ds(pl.multiple_of(lane, LANES), count * LANES)
        for kind, part in ((0, value[:cols]), (1, value[cols:])):
            if not first:
                part = part + before[2 * whose + kind][:, at]
            totals[2 * whose + kind][:, at] = part

    half = tiles_per // 2

    @pl.loop(0, half)
    def _(step):
        keep(0, step * 2 * LANES, 2, product(2 * step, 2))

    if tiles_per % 2:
        both = product(2 * half, 2)
        keep(0, 2 * half * LANES, 1, both[:, :LANES])
        keep(1, 0, 1, both[:, LANES:])

    odd = tiles_per % 2

    @pl.loop(0, half)
    def _(step):
        keep(1, (odd + 2 * step) * LANES, 2, product(tiles_per + odd + 2 * step, 2))


def add_products(place, images, strips, before, cols, rows):
    n_images, channels, strip = len(images), images[0].shape[3], strips[0].shape[1]
    spots = images[0].shape[1] * images[0].shape[2]
    shapes = [jax.ShapeDtypeStruct((height, rows), jnp.float32) for height in (cols, strip)] * 2
    whole = pl.BlockSpec(memory_space=pltpu.VMEM)
    operands = [place, *images, *strips, *(before or [])]
    n_front = 1 + n_images + len(strips)
    return pl.pallas_call(
        lambda *refs: products_kernel(len(strips), before is None, *refs),
        out_shape=shapes,
        in_specs=[pl.BlockSpec(memory_space=pltpu.SMEM)] + [whole] * (len(operands) - 1),
        out_specs=[whole] * 4,
        scratch_shapes=[
            pltpu.VMEM((3, n_images, images[0].shape[1] + 2, images[0].shape[2], channels), jnp.bfloat16),
            pltpu.VMEM(((cols + strip + LANES - 1) // LANES * LANES, n_images * spots), jnp.bfloat16),
            pltpu.VMEM((cols + strip, n_images * spots), jnp.bfloat16),
        ],
        input_output_aliases={} if before is None else {n_front + k: k for k in range(4)},
        compiler_params=pltpu.CompilerParams(vmem_limit_bytes=40 * 1024 * 1024),
        cost_estimate=pl.CostEstimate(
            flops=4 * (cols + strip) * rows * n_images * spots,
            bytes_accessed=4 * 4 * (cols + strip) * rows,
            transcendentals=0,
        ),
    )(*operands)


def tail_kernel(strip, block, *refs):
    order, a_ref, g_ref = refs[:3]
    away_ref, kept_ref, columns, inverse = refs[-4:]
    strip_refs = refs[3:-4]
    channels = g_ref.shape[0]
    for at, ref in enumerate(strip_refs):
        columns[at * strip : (at + 1) * strip, :] = ref[...]
        rows = pl.ds(pl.multiple_of(order[at] * strip, strip), strip)
        for to in range(channels // block):
            lanes = pl.ds(pl.multiple_of(order[len(strip_refs) + to] * block, block), block)
            inverse[at * strip : (at + 1) * strip, to * block : (to + 1) * block] = g_ref[rows, lanes]
    first = lax.dot_general(
        a_ref[...],
        columns[...],
        (((1,), (1,)), ((), ())),
        precision=lax.Precision.HIGH,
        preferred_element_type=jnp.float32,
    )
    both = jnp.dot(
        first, inverse[...], precision=lax.Precision.HIGH, preferred_element_type=jnp.float32
    )
    away_ref[...] = both[:, : channels // 2]
    kept_ref[...] = both[:, channels // 2 :]


def tail_products(order, a_inverse, g_inverse, strips, block):
    channels, strip = g_inverse.shape[0], strips[0].shape[0]
    rows, depth = a_inverse.shape
    whole = pl.BlockSpec(memory_space=pltpu.VMEM)
    return pl.pallas_call(
        lambda *refs: tail_kernel(strip, block, *refs),
        out_shape=[jax.ShapeDtypeStruct((rows, channels // 2), jnp.float32)] * 2,
        in_specs=[pl.BlockSpec(memory_space=pltpu.SMEM)] + [whole] * (2 + len(strips)),
        out_specs=[whole] * 2,
        scratch_shapes=[
            pltpu.VMEM((channels, depth), jnp.float32),
            pltpu.VMEM((channels, channels), jnp.float32),
        ],
        compiler_params=pltpu.CompilerParams(vmem_limit_bytes=32 * 1024 * 1024),
        cost_estimate=pl.CostEstimate(
            flops=6 * rows * channels * (depth + channels),
            bytes_accessed=4 * rows * (depth + channels),
            transcendentals=0,
        ),
    )(order, a_inverse, g_inverse, *strips)


def per_device(activations, cotangent, weight, a_factor_old, g_factor_old, a_inverse, g_inverse):
    channels = activations.shape[3]
    n_fsdp, n_factor = lax.axis_size("fsdp"), lax.axis_size("factor")
    n_layer, n_pair = n_fsdp // 2, n_factor // 2
    fsdp_at, factor_at = lax.axis_index("fsdp"), lax.axis_index("factor")
    core_at, pair_at = factor_at % 2, factor_at // 2
    rows, cols = a_factor_old.shape
    strip = channels // n_fsdp
    block = channels // n_factor

    def over_layer(array, step):
        return moved(array, "fsdp", lambda at: at + 2 * step)

    def over_side(array):
        return moved(array, "fsdp", lambda at: at ^ 1)

    def over_pair(array, step):
        return moved(array, "factor", lambda at: at + 2 * step)

    def over_core(array):
        return moved(array, "factor", lambda at: at ^ 1)

    own_cot = cotangent.reshape(-1, channels)
    strips = lax.all_to_all(
        own_cot.T.reshape(n_fsdp, strip, own_cot.shape[0]), "fsdp", split_axis=0, concat_axis=0
    )
    strips_by_pair = [strips] + [over_pair(strips, step) for step in range(1, n_pair)]

    layers = [activations]
    source = activations
    for step in range(1, n_layer):
        layers.append(over_layer(source, step))
        source, _ = lax.optimization_barrier((source, layers[-1]))
    weight, _ = lax.optimization_barrier((weight, layers[-1]))
    aligned = rows % LANES == 0 and channels % LANES == 0 and activations.shape[0] == 1
    totals = None
    group_images = []
    for step, layer in enumerate(layers):
        near = [layer] + [over_pair(layer, pair) for pair in range(1, n_pair)]
        if step % 2 == 0:
            aside = over_side(layer)
            far = [aside] + [over_pair(aside, pair) for pair in range(1, n_pair)]
        else:
            far = [over_side(image) for image in near]
        if step == 0:
            group_images = near
        owner = (fsdp_at - 2 * step) % n_fsdp
        if aligned:
            place = jnp.stack([factor_at ^ 1, factor_at, fsdp_at, owner, owner ^ 1])
            totals = add_products(place, near + far, strips_by_pair, totals, cols, rows)
            continue
        images = jnp.concatenate(near + far, axis=0)
        col_tile = tile_of_patches(images, fsdp_at * cols, cols)
        cot_tile = jnp.concatenate(
            [
                lax.dynamic_index_in_dim(strips_by_pair[pair], which, 0, keepdims=False)
                for which in (owner, owner ^ 1)
                for pair in range(n_pair)
            ],
            axis=1,
        )
        more = []
        for tile in (factor_at ^ 1, factor_at):
            row_tile = tile_of_patches(images, tile * rows, rows)
            more.append(by_rows(col_tile, row_tile))
            more.append(jnp.dot(cot_tile, row_tile, preferred_element_type=jnp.float32))
        totals = more if totals is None else [total + new for total, new in zip(totals, more)]

    late_cot, late_g, late_images, _ = lax.optimization_barrier(
        (own_cot, g_factor_old, group_images, far[-1])
    )
    grad_own = totals[3] + over_core(totals[1])
    cov_own = totals[2] + over_core(totals[0])
    pixel_total = float(
        activations.shape[0] * activations.shape[1] * activations.shape[2] * n_fsdp * n_factor
    )
    a_factor = 0.5 * a_factor_old + (0.5 / pixel_total) * cov_own.T

    exponent = jnp.floor(jnp.log2(jnp.maximum(jnp.max(jnp.abs(grad_own)), 1e-30))) - 14.0
    packed = (grad_own * jnp.exp2(-exponent)).astype(jnp.float16)
    exponent = jnp.full((strip, LANES), exponent, jnp.float16)
    packed = jnp.concatenate([packed, exponent], axis=1)
    near_packed = [packed] + [over_layer(packed, step) for step in range(1, n_layer)]
    far_packed = [over_side(array) for array in near_packed]
    strips_of_grad = [
        array[:, :rows].astype(jnp.float32) * jnp.exp2(array[:, rows : rows + 1].astype(jnp.float32))
        for array in near_packed + far_packed
    ]
    came_from = [(fsdp_at - 2 * step) % n_fsdp for step in range(n_layer)]
    came_from = came_from + [at ^ 1 for at in came_from]
    order = [
        2 * ((pair_at + step) % n_pair) + (core_at + other) % 2
        for other in (1, 0)
        for step in range(n_pair)
    ]
    if aligned and block % LANES == 0:
        away, kept = tail_products(
            jnp.stack(came_from + order), a_inverse, g_inverse, strips_of_grad, block
        )
    else:
        inverse = jnp.concatenate(
            [lax.dynamic_slice_in_dim(g_inverse, at * block, block, 1) for at in order], axis=1
        )
        inverse = jnp.concatenate(
            [lax.dynamic_slice_in_dim(inverse, at * strip, strip, 0) for at in came_from]
        )
        partial = lax.dot_general(
            a_inverse,
            jnp.concatenate(strips_of_grad),
            (((1,), (1,)), ((), ())),
            precision=lax.Precision.HIGH,
            preferred_element_type=jnp.float32,
        )
        partial = jnp.dot(
            partial, inverse, precision=lax.Precision.HIGH, preferred_element_type=jnp.float32
        )
        away, kept = partial[:, : channels // 2], partial[:, channels // 2 :]
    by_pair = kept + over_core(away)
    result = by_pair[:, :block]
    for step in range(1, n_pair):
        result = result + over_pair(by_pair[:, step * block : (step + 1) * block], step)
    natural_grad = result.astype(jnp.bfloat16)

    weight_part = lax.dynamic_slice_in_dim(weight, factor_at * block, block, 1)
    near_parts = [weight_part] + [over_layer(weight_part, step) for step in range(1, n_layer)]
    near_parts = jnp.stack(near_parts)
    parts = jnp.stack([near_parts, over_side(near_parts)])
    kernel = jnp.concatenate(
        [
            lax.dynamic_slice(
                parts,
                ((fsdp_at + at) % 2, (fsdp_at // 2 - at // 2) % n_layer, 0, 0),
                (1, 1) + weight_part.shape,
            )[0, 0]
            for at in range(n_fsdp)
        ]
    ).reshape(3, 3, channels, block)
    near_images = jnp.concatenate(late_images, axis=0)
    maps = lax.conv_general_dilated(
        jnp.concatenate([near_images, over_core(near_images)], axis=0),
        kernel,
        (1, 1),
        "SAME",
        dimension_numbers=("NHWC", "HWIO", "NHWC"),
        preferred_element_type=jnp.float32,
    ).astype(jnp.bfloat16)
    maps = maps.reshape((2, n_pair) + activations.shape[:3] + (block,))
    own_maps = []
    for pair in range(n_pair):
        for other in range(2):
            own_maps.append(
                maps[other, pair]
                if pair + other == 0
                else moved(
                    maps[other, pair], "factor", lambda at, o=other, p=pair: (at ^ o) - 2 * p
                )
            )
    own_maps = jnp.stack(own_maps)
    conv_out = jnp.concatenate(
        [
            lax.dynamic_index_in_dim(
                own_maps,
                2 * ((at // 2 - pair_at) % n_pair) + (at + core_at) % 2,
                0,
                keepdims=False,
            )
            for at in range(n_factor)
        ],
        axis=3,
    )

    g_partial = by_rows(late_cot, late_cot).reshape(n_pair, 2, block, channels)
    g_pairs = lax.dynamic_index_in_dim(g_partial, core_at, 1, keepdims=False) + over_core(
        lax.dynamic_index_in_dim(g_partial, 1 - core_at, 1, keepdims=False)
    )
    g_sum = lax.dynamic_index_in_dim(g_pairs, pair_at, 0, keepdims=False)
    for step in range(1, n_pair):
        away = lax.dynamic_index_in_dim(g_pairs, (pair_at + step) % n_pair, 0, keepdims=False)
        g_sum = g_sum + over_pair(away, step)
    distance = 1
    while distance < n_fsdp:
        g_sum = g_sum + moved(g_sum, "fsdp", lambda at, d=distance: at ^ d)
        distance *= 2
    g_factor = 0.5 * late_g + 0.5 * g_sum
    return (conv_out, a_factor, g_factor, natural_grad)


def solution(mesh):
    images = P(("fsdp", "factor"), None, None, None)
    return jax.shard_map(
        per_device,
        mesh=mesh,
        in_specs=(
            images,
            images,
            P("fsdp", None),
            P("factor", "fsdp"),
            P("factor", None),
            P("fsdp", "factor"),
            P(),
        ),
        out_specs=(
            images,
            P("factor", "fsdp"),
            P("factor", None),
            P("fsdp", "factor"),
        ),
        check_vma=False,
    )
```

```python
import jax
import jax.numpy as jnp
from jax import lax
from jax.experimental import pallas as pl
from jax.experimental.pallas import tpu as pltpu
from jax.sharding import PartitionSpec as P

LANES = 128


def by_rows(first_op, second_op):
    return lax.dot_general(
        first_op, second_op, (((0,), (0,)), ((), ())), preferred_element_type=jnp.float32
    )


def moved(array, axis, target):
    count = lax.axis_size(axis)
    return lax.ppermute(array, axis, [(at, target(at) % count) for at in range(count)])


def tile_of_patches(images, start, width):
    side, channels = images.shape[1], images.shape[3]
    padded = jnp.pad(images, ((0, 0), (1, 1), (1, 1), (0, 0)))
    first_tap, offset = start // channels, start % channels
    rolled = lax.dynamic_slice_in_dim(
        jnp.concatenate([padded, padded], axis=3), offset, channels, 3
    )
    lane = lax.broadcasted_iota(jnp.int32, (1, 1, 1, channels), 3)

    def tap(index):
        index = jnp.minimum(index, 8)
        return lax.dynamic_slice(
            rolled, (0, index // 3, index % 3, 0), (images.shape[0], side, side, channels)
        )

    pieces = []
    for at in range(0, width, channels):
        step = at // channels
        piece = jnp.where(lane < channels - offset, tap(first_tap + step), tap(first_tap + step + 1))
        pieces.append(piece[..., : min(channels, width - at)])
    return jnp.concatenate(pieces, axis=3).reshape(-1, width)


def products_kernel(pairs, n_pair, first, *refs):
    place = refs[0]
    image_refs = refs[1 : 1 + len(pairs)]
    strip_refs = refs[1 + len(pairs) : 1 + len(pairs) + n_pair]
    refs = refs[1 + len(pairs) + n_pair :]
    before, refs = (None, refs) if first else (refs[:4], refs[4:])
    totals, (shifted, turned, left) = refs[:4], refs[4:]
    n_images, side, channels = len(image_refs), image_refs[0].shape[1], image_refs[0].shape[3]
    spots = side * side
    cols, rows = totals[0].shape
    strip = totals[1].shape[0]
    fsdp_at = place[2]

    spot = lax.broadcasted_iota(jnp.int32, (spots, LANES), 0) % side
    empty = jnp.zeros((side, channels), jnp.bfloat16)
    for at, ref in enumerate(image_refs):
        for col_off in range(3):
            shifted[col_off, at, 0] = empty
            shifted[col_off, at, side + 1] = empty
        shifted[1, at, 1 : side + 1] = ref[0]
        for lane in range(0, channels, LANES):
            part = ref[0, :, :, lane : lane + LANES].reshape(spots, LANES).astype(jnp.float32)
            before_it = jnp.where(spot == 0, 0.0, pltpu.roll(part, 1, 0))
            after_it = jnp.where(spot == side - 1, 0.0, pltpu.roll(part, spots - 1, 0))
            for col_off, moved_part in ((0, before_it), (2, after_it)):
                shifted[col_off, at, 1 : side + 1, :, lane : lane + LANES] = moved_part.astype(
                    jnp.bfloat16
                ).reshape(side, side, LANES)

    def lanes_of_tap(tap, lane):
        piece = shifted[tap % 3, :, pl.ds(tap // 3, side), :, pl.ds(pl.multiple_of(lane, LANES), LANES)]
        return piece.reshape(n_images * spots, LANES)

    start = fsdp_at * cols
    inside = start % LANES
    for at in range(0, turned.shape[0], LANES):
        lane = start - inside + at
        tap = jnp.minimum(lane // channels, 8)
        turned[at : at + LANES, :] = lanes_of_tap(tap, lane % channels).T
    left[:cols, :] = turned[pl.ds(pl.multiple_of(inside, strip), cols), :]
    for at, pair in enumerate(pairs):
        left[cols : cols + strip, at * spots : (at + 1) * spots] = strip_refs[pair][place[3 + at]]

    tiles_per = rows // LANES

    def lanes_at(index):
        whose = jnp.where(index >= tiles_per, 1, 0)
        start = (place[whose] * tiles_per + index - whose * tiles_per) * LANES
        return lanes_of_tap(start // channels, start % channels)

    def product(first_index, count):
        right = jnp.concatenate([lanes_at(first_index + k) for k in range(count)], axis=1)
        return jnp.dot(left[...], right, preferred_element_type=jnp.float32)

    def keep(whose, lane, count, value):
        at = pl.ds(pl.multiple_of(lane, LANES), count * LANES)
        for kind, part in ((0, value[:cols]), (1, value[cols:])):
            if not first:
                part = part + before[2 * whose + kind][:, at]
            totals[2 * whose + kind][:, at] = part

    half = tiles_per // 2

    @pl.loop(0, half)
    def _(step):
        keep(0, step * 2 * LANES, 2, product(2 * step, 2))

    if tiles_per % 2:
        both = product(2 * half, 2)
        keep(0, 2 * half * LANES, 1, both[:, :LANES])
        keep(1, 0, 1, both[:, LANES:])

    odd = tiles_per % 2

    @pl.loop(0, half)
    def _(step):
        keep(1, (odd + 2 * step) * LANES, 2, product(tiles_per + odd + 2 * step, 2))


def add_products(place, images, pairs, strips, before, cols, rows):
    n_images, channels, strip = len(images), images[0].shape[3], strips[0].shape[1]
    spots = images[0].shape[1] * images[0].shape[2]
    shapes = [jax.ShapeDtypeStruct((height, rows), jnp.float32) for height in (cols, strip)] * 2
    whole = pl.BlockSpec(memory_space=pltpu.VMEM)
    operands = [place, *images, *strips, *(before or [])]
    n_front = 1 + n_images + len(strips)
    return pl.pallas_call(
        lambda *refs: products_kernel(pairs, len(strips), before is None, *refs),
        out_shape=shapes,
        in_specs=[pl.BlockSpec(memory_space=pltpu.SMEM)] + [whole] * (len(operands) - 1),
        out_specs=[whole] * 4,
        scratch_shapes=[
            pltpu.VMEM((3, n_images, images[0].shape[1] + 2, images[0].shape[2], channels), jnp.bfloat16),
            pltpu.VMEM(((cols + strip + LANES - 1) // LANES * LANES, n_images * spots), jnp.bfloat16),
            pltpu.VMEM((cols + strip, n_images * spots), jnp.bfloat16),
        ],
        input_output_aliases={} if before is None else {n_front + k: k for k in range(4)},
        compiler_params=pltpu.CompilerParams(vmem_limit_bytes=40 * 1024 * 1024),
        cost_estimate=pl.CostEstimate(
            flops=4 * (cols + strip) * rows * n_images * spots,
            bytes_accessed=16 * (cols + strip) * rows,
            transcendentals=0,
        ),
    )(*operands)


def tail_kernel(strip, block, *refs):
    order, a_ref, g_ref = refs[:3]
    away_ref, kept_ref, columns, inverse = refs[-4:]
    strip_refs = refs[3:-4]
    channels = g_ref.shape[0]
    for at, ref in enumerate(strip_refs):
        columns[at * strip : (at + 1) * strip, :] = ref[...]
        rows = pl.ds(pl.multiple_of(order[at] * strip, strip), strip)
        for to in range(channels // block):
            lanes = pl.ds(pl.multiple_of(order[len(strip_refs) + to] * block, block), block)
            inverse[at * strip : (at + 1) * strip, to * block : (to + 1) * block] = g_ref[rows, lanes]
    first = lax.dot_general(
        a_ref[...],
        columns[...],
        (((1,), (1,)), ((), ())),
        precision=lax.Precision.HIGH,
        preferred_element_type=jnp.float32,
    )
    both = jnp.dot(
        first, inverse[...], precision=lax.Precision.HIGH, preferred_element_type=jnp.float32
    )
    away_ref[...] = both[:, : channels // 2]
    kept_ref[...] = both[:, channels // 2 :]


def tail_products(order, a_inverse, g_inverse, strips, block):
    channels, strip = g_inverse.shape[0], strips[0].shape[0]
    rows, depth = a_inverse.shape
    whole = pl.BlockSpec(memory_space=pltpu.VMEM)
    return pl.pallas_call(
        lambda *refs: tail_kernel(strip, block, *refs),
        out_shape=[jax.ShapeDtypeStruct((rows, channels // 2), jnp.float32)] * 2,
        in_specs=[pl.BlockSpec(memory_space=pltpu.SMEM)] + [whole] * (2 + len(strips)),
        out_specs=[whole] * 2,
        scratch_shapes=[
            pltpu.VMEM((channels, depth), jnp.float32),
            pltpu.VMEM((channels, channels), jnp.float32),
        ],
        compiler_params=pltpu.CompilerParams(vmem_limit_bytes=32 * 1024 * 1024),
        cost_estimate=pl.CostEstimate(
            flops=6 * rows * channels * (depth + channels),
            bytes_accessed=4 * rows * (depth + channels),
            transcendentals=0,
        ),
    )(order, a_inverse, g_inverse, *strips)


def gather_plan(n_layer, n_pair):
    far_layers = sorted(range(1, n_layer), key=lambda step: min(step, n_layer - step))
    by_side, by_pair = [], []
    for turn, layer in enumerate([0] + far_layers):
        by_side.append((("side", layer, 0), ("layer", layer, 0)))
        for pair in range(1, n_pair):
            by_pair.append((("pair", layer, pair), ("layer", layer, 0)))
            if turn % 2 == 0:
                by_pair.append((("both", layer, pair), ("side", layer, 0)))
            else:
                by_side.append((("both", layer, pair), ("pair", layer, pair)))
    by_layer = [(("layer", layer, 0), None) for layer in far_layers]
    for link in (by_side, by_pair):
        link.sort(key=lambda item: item[0][0] == "both")
    here, due, rounds = {None, ("layer", 0, 0)}, {}, []
    while by_layer or by_side or by_pair:
        here |= {item for item, when in due.items() if when <= len(rounds)}
        due = {item: when for item, when in due.items() if when > len(rounds)}
        now = []
        for link in (by_layer, by_side, by_pair):
            if link is by_layer and any(item[0] == "layer" for item in due):
                continue
            free = [item for item in link if item[1] in here]
            if free:
                link.remove(free[0])
                item, source = free[0]
                hops = min(item[1], n_layer - item[1]) if item[0] == "layer" else 1
                due[item] = len(rounds) + hops
                now.append((item, source, "pair" if link is by_pair else item[0], hops))
        rounds.append(now)
    return rounds


def per_device(activations, cotangent, weight, a_factor_old, g_factor_old, a_inverse, g_inverse):
    channels = activations.shape[3]
    n_fsdp, n_factor = lax.axis_size("fsdp"), lax.axis_size("factor")
    n_layer, n_pair = n_fsdp // 2, n_factor // 2
    fsdp_at, factor_at = lax.axis_index("fsdp"), lax.axis_index("factor")
    core_at, pair_at = factor_at % 2, factor_at // 2
    rows, cols = a_factor_old.shape
    strip = channels // n_fsdp
    block = channels // n_factor

    def over_layer(array, step):
        return moved(array, "fsdp", lambda at: at + 2 * step)

    def over_side(array):
        return moved(array, "fsdp", lambda at: at ^ 1)

    def over_pair(array, step):
        return moved(array, "factor", lambda at: at + 2 * step)

    def over_core(array):
        return moved(array, "factor", lambda at: at ^ 1)

    def after(arrays, events):
        return lax.optimization_barrier((arrays, events))[0]

    def transfer(array, item, how):
        if how == "layer":
            return over_layer(array, item[1])
        if how == "pair":
            return over_pair(array, item[2])
        return over_side(array)

    own_cot = cotangent.reshape(-1, channels)
    maps = {("layer", 0, 0): activations}
    plan = gather_plan(n_layer, n_pair)
    events, due = [[]], []
    for at, now in enumerate(plan):
        sources = [activations if source is None else maps[source] for _, source, _, _ in now]
        sources = after(sources, events[at])
        for array, (item, _, how, hops) in zip(sources, now):
            maps[item] = transfer(array, item, how)
            due.append((at + hops, maps[item]))
        events.append([array for when, array in due if when == at + 1])
    last = len(plan) - 1

    strips = after(own_cot, events[1]).T.reshape(n_fsdp, strip, own_cot.shape[0])
    strips = lax.all_to_all(strips, "fsdp", split_axis=0, concat_axis=0)
    strips_by_pair = [strips] + [
        over_pair(after(strips, events[3]), step) for step in range(1, n_pair)
    ]

    aligned = rows % LANES == 0 and channels % LANES == 0 and activations.shape[0] == 1
    arrived = {("layer", 0, 0): 0}
    for at, now in enumerate(plan):
        arrived.update({item: at + hops for item, _, _, hops in now})
    images = sorted(maps, key=lambda item: arrived[item])
    images.sort(
        key=lambda item: max(when for other, when in arrived.items() if other[1] == item[1])
    )
    half = len(images) // 2
    totals = None
    for batch in (images[:half], images[half:]):
        owners, pairs = [], []
        for kind, layer, pair in batch:
            owner = (fsdp_at - 2 * layer) % n_fsdp
            owners.append(owner ^ 1 if kind in ("side", "both") else owner)
            pairs.append(pair)
        if aligned:
            place = jnp.stack([factor_at ^ 1, factor_at, fsdp_at] + owners)
            totals = add_products(
                place, [maps[item] for item in batch], pairs, strips_by_pair, totals, cols, rows
            )
            continue
        for at in range(0, len(batch), 2 * n_pair):
            part = jnp.concatenate([maps[item] for item in batch[at : at + 2 * n_pair]], axis=0)
            col_tile = tile_of_patches(part, fsdp_at * cols, cols)
            cot_tile = jnp.concatenate(
                [
                    lax.dynamic_index_in_dim(strips_by_pair[pair], owner, 0, keepdims=False)
                    for pair, owner in list(zip(pairs, owners))[at : at + 2 * n_pair]
                ],
                axis=1,
            )
            more = []
            for tile in (factor_at ^ 1, factor_at):
                row_tile = tile_of_patches(part, tile * rows, rows)
                more.append(by_rows(col_tile, row_tile))
                more.append(jnp.dot(cot_tile, row_tile, preferred_element_type=jnp.float32))
            totals = more if totals is None else [old + new for old, new in zip(totals, more)]

    grad_own = totals[3] + over_core(totals[1])
    cov_own = totals[2] + over_core(totals[0])
    pixel_total = float(
        activations.shape[0] * activations.shape[1] * activations.shape[2] * n_fsdp * n_factor
    )
    a_factor = 0.5 * a_factor_old + (0.5 / pixel_total) * cov_own.T

    exponent = jnp.floor(jnp.log2(jnp.maximum(jnp.max(jnp.abs(grad_own)), 1e-30))) - 14.0
    packed = (grad_own * jnp.exp2(-exponent)).astype(jnp.float16)
    exponent = jnp.full((strip, LANES), exponent, jnp.float16)
    packed = jnp.concatenate([packed, exponent], axis=1)
    near_packed = [packed] + [over_layer(packed, step) for step in range(1, n_layer)]
    far_packed = [over_side(array) for array in near_packed]
    strips_of_grad = [
        array[:, :rows].astype(jnp.float32) * jnp.exp2(array[:, rows : rows + 1].astype(jnp.float32))
        for array in near_packed + far_packed
    ]
    came_from = [(fsdp_at - 2 * step) % n_fsdp for step in range(n_layer)]
    came_from = came_from + [at ^ 1 for at in came_from]
    order = [
        2 * ((pair_at + step) % n_pair) + (core_at + other) % 2
        for other in (1, 0)
        for step in range(n_pair)
    ]
    if aligned and block % LANES == 0:
        away, kept = tail_products(
            jnp.stack(came_from + order), a_inverse, g_inverse, strips_of_grad, block
        )
    else:
        inverse = jnp.concatenate(
            [lax.dynamic_slice_in_dim(g_inverse, at * block, block, 1) for at in order], axis=1
        )
        inverse = jnp.concatenate(
            [lax.dynamic_slice_in_dim(inverse, at * strip, strip, 0) for at in came_from]
        )
        partial = lax.dot_general(
            a_inverse,
            jnp.concatenate(strips_of_grad),
            (((1,), (1,)), ((), ())),
            precision=lax.Precision.HIGH,
            preferred_element_type=jnp.float32,
        )
        partial = jnp.dot(
            partial, inverse, precision=lax.Precision.HIGH, preferred_element_type=jnp.float32
        )
        away, kept = partial[:, : channels // 2], partial[:, channels // 2 :]
    by_pair = kept + over_core(away)
    result = by_pair[:, :block]
    for step in range(1, n_pair):
        result = result + over_pair(by_pair[:, step * block : (step + 1) * block], step)
    natural_grad = result.astype(jnp.bfloat16)

    weight_part = lax.dynamic_slice_in_dim(
        after(weight, events[last - 1]), factor_at * block, block, 1
    )
    near_parts = [weight_part] + [over_layer(weight_part, step) for step in range(1, n_layer)]
    near_parts = after(jnp.stack(near_parts), events[last + 1])
    parts = jnp.stack([near_parts, over_side(near_parts)])
    kernel = jnp.concatenate(
        [
            lax.dynamic_slice(
                parts,
                ((fsdp_at + at) % 2, (fsdp_at // 2 - at // 2) % n_layer, 0, 0),
                (1, 1) + weight_part.shape,
            )[0, 0]
            for at in range(n_fsdp)
        ]
    ).reshape(3, 3, channels, block)
    near_images = [activations] + [maps["pair", 0, step] for step in range(1, n_pair)]
    near_images = after(jnp.concatenate(near_images, axis=0), events[last - 1])
    outputs = lax.conv_general_dilated(
        jnp.concatenate([near_images, over_core(near_images)], axis=0),
        kernel,
        (1, 1),
        "SAME",
        dimension_numbers=("NHWC", "HWIO", "NHWC"),
        preferred_element_type=jnp.float32,
    ).astype(jnp.bfloat16)
    outputs = outputs.reshape((2, n_pair) + activations.shape[:3] + (block,))
    own_maps = []
    for pair in range(n_pair):
        for other in range(2):
            own_maps.append(
                outputs[other, pair]
                if pair + other == 0
                else moved(
                    outputs[other, pair], "factor", lambda at, o=other, p=pair: (at ^ o) - 2 * p
                )
            )
    own_maps = jnp.stack(own_maps)
    conv_out = jnp.concatenate(
        [
            lax.dynamic_index_in_dim(
                own_maps,
                2 * ((at // 2 - pair_at) % n_pair) + (at + core_at) % 2,
                0,
                keepdims=False,
            )
            for at in range(n_factor)
        ],
        axis=3,
    )

    late_cot = after(own_cot, events[2])
    g_partial = by_rows(late_cot, late_cot).reshape(n_pair, 2, block, channels)
    g_pairs = lax.dynamic_index_in_dim(g_partial, core_at, 1, keepdims=False) + over_core(
        lax.dynamic_index_in_dim(g_partial, 1 - core_at, 1, keepdims=False)
    )
    g_pairs = after(g_pairs, events[last + 1])
    g_sum = lax.dynamic_index_in_dim(g_pairs, pair_at, 0, keepdims=False)
    for step in range(1, n_pair):
        away = lax.dynamic_index_in_dim(g_pairs, (pair_at + step) % n_pair, 0, keepdims=False)
        g_sum = g_sum + over_pair(away, step)
    distance = 1
    while distance < n_fsdp:
        g_sum = g_sum + moved(g_sum, "fsdp", lambda at, d=distance: at ^ d)
        distance *= 2
    g_factor = 0.5 * g_factor_old + 0.5 * g_sum
    return (conv_out, a_factor, g_factor, natural_grad)


def solution(mesh):
    images = P(("fsdp", "factor"), None, None, None)
    return jax.shard_map(
        per_device,
        mesh=mesh,
        in_specs=(
            images,
            images,
            P("fsdp", None),
            P("factor", "fsdp"),
            P("factor", None),
            P("fsdp", "factor"),
            P(),
        ),
        out_specs=(
            images,
            P("factor", "fsdp"),
            P("factor", None),
            P("fsdp", "factor"),
        ),
        check_vma=False,
    )
```

```python
import jax
import jax.numpy as jnp
from jax import lax
from jax.experimental import pallas as pl
from jax.experimental.pallas import tpu as pltpu
from jax.sharding import PartitionSpec as P

LANES = 128


def by_rows(first_op, second_op):
    return lax.dot_general(
        first_op, second_op, (((0,), (0,)), ((), ())), preferred_element_type=jnp.float32
    )


def moved(array, axis, target):
    count = lax.axis_size(axis)
    return lax.ppermute(array, axis, [(at, target(at) % count) for at in range(count)])


def tile_of_patches(images, start, width):
    side, channels = images.shape[1], images.shape[3]
    padded = jnp.pad(images, ((0, 0), (1, 1), (1, 1), (0, 0)))
    first_tap, offset = start // channels, start % channels
    rolled = lax.dynamic_slice_in_dim(
        jnp.concatenate([padded, padded], axis=3), offset, channels, 3
    )
    lane = lax.broadcasted_iota(jnp.int32, (1, 1, 1, channels), 3)

    def tap(index):
        index = jnp.minimum(index, 8)
        return lax.dynamic_slice(
            rolled, (0, index // 3, index % 3, 0), (images.shape[0], side, side, channels)
        )

    pieces = []
    for at in range(0, width, channels):
        step = at // channels
        piece = jnp.where(lane < channels - offset, tap(first_tap + step), tap(first_tap + step + 1))
        pieces.append(piece[..., : min(channels, width - at)])
    return jnp.concatenate(pieces, axis=3).reshape(-1, width)


def fill_shifted(image_refs, shifted):
    side, channels = image_refs[0].shape[1], image_refs[0].shape[3]
    spots = side * side
    spot = lax.broadcasted_iota(jnp.int32, (spots, LANES), 0) % side
    empty = jnp.zeros((side, channels), jnp.bfloat16)
    for at, ref in enumerate(image_refs):
        for col_off in range(3):
            shifted[col_off, at, 0] = empty
            shifted[col_off, at, side + 1] = empty
        shifted[1, at, 1 : side + 1] = ref[0]
        for lane in range(0, channels, LANES):
            part = ref[0, :, :, lane : lane + LANES].reshape(spots, LANES).astype(jnp.float32)
            before_it = jnp.where(spot == 0, 0.0, pltpu.roll(part, 1, 0))
            after_it = jnp.where(spot == side - 1, 0.0, pltpu.roll(part, spots - 1, 0))
            for col_off, moved_part in ((0, before_it), (2, after_it)):
                shifted[col_off, at, 1 : side + 1, :, lane : lane + LANES] = moved_part.astype(
                    jnp.bfloat16
                ).reshape(side, side, LANES)


def products_kernel(pairs, n_pair, first, *refs):
    place = refs[0]
    image_refs = refs[1 : 1 + len(pairs)]
    strip_refs = refs[1 + len(pairs) : 1 + len(pairs) + n_pair]
    refs = refs[1 + len(pairs) + n_pair :]
    before, refs = (None, refs) if first else (refs[:4], refs[4:])
    totals, (shifted, turned, left) = refs[:4], refs[4:]
    n_images, side, channels = len(image_refs), image_refs[0].shape[1], image_refs[0].shape[3]
    spots = side * side
    cols, rows = totals[0].shape
    strip = totals[1].shape[0]
    fsdp_at = place[2]

    fill_shifted(image_refs, shifted)

    def lanes_of_tap(tap, lane):
        piece = shifted[tap % 3, :, pl.ds(tap // 3, side), :, pl.ds(pl.multiple_of(lane, LANES), LANES)]
        return piece.reshape(n_images * spots, LANES)

    start = fsdp_at * cols
    inside = start % LANES
    for at in range(0, turned.shape[0], LANES):
        lane = start - inside + at
        tap = jnp.minimum(lane // channels, 8)
        turned[at : at + LANES, :] = lanes_of_tap(tap, lane % channels).T
    left[:cols, :] = turned[pl.ds(pl.multiple_of(inside, strip), cols), :]
    for at, pair in enumerate(pairs):
        left[cols : cols + strip, at * spots : (at + 1) * spots] = strip_refs[pair][place[3 + at]]

    tiles_per = rows // LANES

    def lanes_at(index):
        whose = jnp.where(index >= tiles_per, 1, 0)
        start = (place[whose] * tiles_per + index - whose * tiles_per) * LANES
        return lanes_of_tap(start // channels, start % channels)

    def product(first_index, count):
        right = jnp.concatenate([lanes_at(first_index + k) for k in range(count)], axis=1)
        return jnp.dot(left[...], right, preferred_element_type=jnp.float32)

    def keep(whose, lane, count, value):
        at = pl.ds(pl.multiple_of(lane, LANES), count * LANES)
        for kind, part in ((0, value[:cols]), (1, value[cols:])):
            if not first:
                part = part + before[2 * whose + kind][:, at]
            totals[2 * whose + kind][:, at] = part

    half = tiles_per // 2

    @pl.loop(0, half)
    def _(step):
        keep(0, step * 2 * LANES, 2, product(2 * step, 2))

    if tiles_per % 2:
        both = product(2 * half, 2)
        keep(0, 2 * half * LANES, 1, both[:, :LANES])
        keep(1, 0, 1, both[:, LANES:])

    odd = tiles_per % 2

    @pl.loop(0, half)
    def _(step):
        keep(1, (odd + 2 * step) * LANES, 2, product(tiles_per + odd + 2 * step, 2))


def add_products(place, images, pairs, strips, before, cols, rows):
    n_images, channels, strip = len(images), images[0].shape[3], strips[0].shape[1]
    spots = images[0].shape[1] * images[0].shape[2]
    shapes = [jax.ShapeDtypeStruct((height, rows), jnp.float32) for height in (cols, strip)] * 2
    whole = pl.BlockSpec(memory_space=pltpu.VMEM)
    operands = [place, *images, *strips, *(before or [])]
    n_front = 1 + n_images + len(strips)
    return pl.pallas_call(
        lambda *refs: products_kernel(pairs, len(strips), before is None, *refs),
        out_shape=shapes,
        in_specs=[pl.BlockSpec(memory_space=pltpu.SMEM)] + [whole] * (len(operands) - 1),
        out_specs=[whole] * 4,
        scratch_shapes=[
            pltpu.VMEM((3, n_images, images[0].shape[1] + 2, images[0].shape[2], channels), jnp.bfloat16),
            pltpu.VMEM(((cols + strip + LANES - 1) // LANES * LANES, n_images * spots), jnp.bfloat16),
            pltpu.VMEM((cols + strip, n_images * spots), jnp.bfloat16),
        ],
        input_output_aliases={} if before is None else {n_front + k: k for k in range(4)},
        compiler_params=pltpu.CompilerParams(vmem_limit_bytes=40 * 1024 * 1024),
        cost_estimate=pl.CostEstimate(
            flops=4 * (cols + strip) * rows * n_images * spots,
            bytes_accessed=16 * (cols + strip) * rows,
            transcendentals=0,
        ),
    )(*operands)


def tail_kernel(strip, block, *refs):
    order, a_ref, g_ref = refs[:3]
    away_ref, kept_ref, columns, inverse = refs[-4:]
    strip_refs = refs[3:-4]
    channels = g_ref.shape[0]
    for at, ref in enumerate(strip_refs):
        columns[at * strip : (at + 1) * strip, :] = ref[...]
        rows = pl.ds(pl.multiple_of(order[at] * strip, strip), strip)
        for to in range(channels // block):
            lanes = pl.ds(pl.multiple_of(order[len(strip_refs) + to] * block, block), block)
            inverse[at * strip : (at + 1) * strip, to * block : (to + 1) * block] = g_ref[rows, lanes]
    first = lax.dot_general(
        a_ref[...],
        columns[...],
        (((1,), (1,)), ((), ())),
        precision=lax.Precision.HIGH,
        preferred_element_type=jnp.float32,
    )
    both = jnp.dot(
        first, inverse[...], precision=lax.Precision.HIGH, preferred_element_type=jnp.float32
    )
    away_ref[...] = both[:, : channels // 2]
    kept_ref[...] = both[:, channels // 2 :]


def tail_products(order, a_inverse, g_inverse, strips, block):
    channels, strip = g_inverse.shape[0], strips[0].shape[0]
    rows, depth = a_inverse.shape
    whole = pl.BlockSpec(memory_space=pltpu.VMEM)
    return pl.pallas_call(
        lambda *refs: tail_kernel(strip, block, *refs),
        out_shape=[jax.ShapeDtypeStruct((rows, channels // 2), jnp.float32)] * 2,
        in_specs=[pl.BlockSpec(memory_space=pltpu.SMEM)] + [whole] * (2 + len(strips)),
        out_specs=[whole] * 2,
        scratch_shapes=[
            pltpu.VMEM((channels, depth), jnp.float32),
            pltpu.VMEM((channels, channels), jnp.float32),
        ],
        compiler_params=pltpu.CompilerParams(vmem_limit_bytes=32 * 1024 * 1024),
        cost_estimate=pl.CostEstimate(
            flops=6 * rows * channels * (depth + channels),
            bytes_accessed=4 * rows * (depth + channels),
            transcendentals=0,
        ),
    )(order, a_inverse, g_inverse, *strips)


def conv_kernel(order, *refs):
    order_ref, refs = refs[0], refs[1:]
    n_images, n_parts = order
    image_refs, part_refs = refs[:n_images], refs[n_images : n_images + n_parts]
    out_refs = refs[n_images + n_parts : -2]
    shifted, weight = refs[-2:]
    side, channels = image_refs[0].shape[1], image_refs[0].shape[3]
    depth = part_refs[0].shape[0]
    fill_shifted(image_refs, shifted)
    for at, ref in enumerate(part_refs):
        weight[pl.ds(pl.multiple_of(order_ref[at] * depth, 64), depth), :] = ref[...]
    for at, ref in enumerate(out_refs):
        total = jnp.zeros((side * side, weight.shape[1]), jnp.float32)
        for tap in range(9):
            left = shifted[tap % 3, at, tap // 3 : tap // 3 + side].reshape(side * side, channels)
            total += jnp.dot(
                left,
                weight[tap * channels : (tap + 1) * channels, :],
                preferred_element_type=jnp.float32,
            )
        ref[0] = total.astype(jnp.bfloat16).reshape(side, side, weight.shape[1])


def convolve(order, images, parts):
    n_images, (_, side, _, channels) = len(images), images[0].shape
    depth, block = parts[0].shape
    whole = pl.BlockSpec(memory_space=pltpu.VMEM)
    return pl.pallas_call(
        lambda *refs: conv_kernel((n_images, len(parts)), *refs),
        out_shape=[jax.ShapeDtypeStruct((1, side, side, block), jnp.bfloat16)] * n_images,
        in_specs=[pl.BlockSpec(memory_space=pltpu.SMEM)] + [whole] * (n_images + len(parts)),
        out_specs=[whole] * n_images,
        scratch_shapes=[
            pltpu.VMEM((3, n_images, side + 2, side, channels), jnp.bfloat16),
            pltpu.VMEM((9 * channels, block), jnp.bfloat16),
        ],
        compiler_params=pltpu.CompilerParams(vmem_limit_bytes=24 * 1024 * 1024),
        cost_estimate=pl.CostEstimate(
            flops=36 * n_images * side * side * channels * block,
            bytes_accessed=2 * (9 * channels * block + n_images * side * side * channels),
            transcendentals=0,
        ),
    )(order, *images, *parts)


def side_by_side_kernel(order_ref, *refs):
    block = refs[0].shape[3]
    for at, ref in enumerate(refs[:-1]):
        refs[-1][:, :, :, pl.ds(pl.multiple_of(order_ref[at] * block, LANES), block)] = ref[...]


def side_by_side(order, blocks):
    whole = pl.BlockSpec(memory_space=pltpu.VMEM)
    shape = blocks[0].shape[:3] + (len(blocks) * blocks[0].shape[3],)
    return pl.pallas_call(
        side_by_side_kernel,
        out_shape=jax.ShapeDtypeStruct(shape, blocks[0].dtype),
        in_specs=[pl.BlockSpec(memory_space=pltpu.SMEM)] + [whole] * len(blocks),
        out_specs=whole,
    )(order, *blocks)


def gather_plan(n_layer, n_pair):
    far_layers = sorted(range(1, n_layer), key=lambda step: min(step, n_layer - step))
    by_side, by_pair = [], []
    for turn, layer in enumerate([0] + far_layers):
        by_side.append((("side", layer, 0), ("layer", layer, 0)))
        for pair in range(1, n_pair):
            by_pair.append((("pair", layer, pair), ("layer", layer, 0)))
            if turn % 2 == 0:
                by_pair.append((("both", layer, pair), ("side", layer, 0)))
            else:
                by_side.append((("both", layer, pair), ("pair", layer, pair)))
    by_layer = [(("layer", layer, 0), None) for layer in far_layers]
    for link in (by_side, by_pair):
        link.sort(key=lambda item: item[0][0] == "both")
    here, due, rounds = {None, ("layer", 0, 0)}, {}, []
    while by_layer or by_side or by_pair:
        here |= {item for item, when in due.items() if when <= len(rounds)}
        due = {item: when for item, when in due.items() if when > len(rounds)}
        now = []
        for link in (by_layer, by_side, by_pair):
            if link is by_layer and any(item[0] == "layer" for item in due):
                continue
            free = [item for item in link if item[1] in here]
            if free:
                link.remove(free[0])
                item, source = free[0]
                hops = min(item[1], n_layer - item[1]) if item[0] == "layer" else 1
                due[item] = len(rounds) + hops
                now.append((item, source, "pair" if link is by_pair else item[0], hops))
        rounds.append(now)
    return rounds


def per_device(activations, cotangent, weight, a_factor_old, g_factor_old, a_inverse, g_inverse):
    channels = activations.shape[3]
    n_fsdp, n_factor = lax.axis_size("fsdp"), lax.axis_size("factor")
    n_layer, n_pair = n_fsdp // 2, n_factor // 2
    fsdp_at, factor_at = lax.axis_index("fsdp"), lax.axis_index("factor")
    core_at, pair_at = factor_at % 2, factor_at // 2
    rows, cols = a_factor_old.shape
    strip = channels // n_fsdp
    block = channels // n_factor

    def over_layer(array, step):
        return moved(array, "fsdp", lambda at: at + 2 * step)

    def over_side(array):
        return moved(array, "fsdp", lambda at: at ^ 1)

    def over_pair(array, step):
        return moved(array, "factor", lambda at: at + 2 * step)

    def over_core(array):
        return moved(array, "factor", lambda at: at ^ 1)

    def after(arrays, events):
        return lax.optimization_barrier((arrays, events))[0]

    def transfer(array, item, how):
        if how == "layer":
            return over_layer(array, item[1])
        if how == "pair":
            return over_pair(array, item[2])
        return over_side(array)

    own_cot = cotangent.reshape(-1, channels)
    maps = {("layer", 0, 0): activations}
    plan = gather_plan(n_layer, n_pair)
    events, due = [[]], []
    strips_by_pair = []
    for at, now in enumerate(plan):
        if at == 1:
            strips = after(own_cot, events[1]).T.reshape(n_fsdp, strip, own_cot.shape[0])
            strips_by_pair.append(lax.all_to_all(strips, "fsdp", split_axis=0, concat_axis=0))
        if at == 3:
            strips = after(strips_by_pair[0], events[3])
            strips_by_pair += [over_pair(strips, step) for step in range(1, n_pair)]
            due += [(4, strips) for strips in strips_by_pair]
        sources = [activations if source is None else maps[source] for _, source, _, _ in now]
        sources = after(sources, events[at])
        for array, (item, _, how, hops) in zip(sources, now):
            maps[item] = transfer(array, item, how)
            due.append((at + hops, maps[item]))
        events.append([array for when, array in due if when == at + 1])
    last = len(plan) - 1

    aligned = rows % LANES == 0 and channels % LANES == 0 and activations.shape[0] == 1
    arrived = {("layer", 0, 0): 0}
    for at, now in enumerate(plan):
        arrived.update({item: at + hops for item, _, _, hops in now})
    images = sorted(maps, key=lambda item: arrived[item])
    images.sort(
        key=lambda item: max(when for other, when in arrived.items() if other[1] == item[1])
    )
    half = len(images) // 2
    totals, early = None, []
    for batch in (images[:half], images[half:]):
        owners, pairs = [], []
        for kind, layer, pair in batch:
            owner = (fsdp_at - 2 * layer) % n_fsdp
            owners.append(owner ^ 1 if kind in ("side", "both") else owner)
            pairs.append(pair)
        if aligned:
            place = jnp.stack([factor_at ^ 1, factor_at, fsdp_at] + owners)
            totals = add_products(
                place, [maps[item] for item in batch], pairs, strips_by_pair, totals, cols, rows
            )
            early = early or [totals[3]]
            continue
        for at in range(0, len(batch), 2 * n_pair):
            part = jnp.concatenate([maps[item] for item in batch[at : at + 2 * n_pair]], axis=0)
            col_tile = tile_of_patches(part, fsdp_at * cols, cols)
            cot_tile = jnp.concatenate(
                [
                    lax.dynamic_index_in_dim(strips_by_pair[pair], owner, 0, keepdims=False)
                    for pair, owner in list(zip(pairs, owners))[at : at + 2 * n_pair]
                ],
                axis=1,
            )
            more = []
            for tile in (factor_at ^ 1, factor_at):
                row_tile = tile_of_patches(part, tile * rows, rows)
                more.append(by_rows(col_tile, row_tile))
                more.append(jnp.dot(cot_tile, row_tile, preferred_element_type=jnp.float32))
            totals = more if totals is None else [old + new for old, new in zip(totals, more)]

    g_partial = by_rows(after(own_cot, events[2]), own_cot).reshape(n_pair, 2, block, channels)
    g_pairs = lax.dynamic_index_in_dim(g_partial, core_at, 1, keepdims=False) + over_core(
        lax.dynamic_index_in_dim(g_partial, 1 - core_at, 1, keepdims=False)
    )
    g_pairs = after(g_pairs, events[last])
    g_sum = lax.dynamic_index_in_dim(g_pairs, pair_at, 0, keepdims=False)
    for step in range(1, n_pair):
        away = lax.dynamic_index_in_dim(g_pairs, (pair_at + step) % n_pair, 0, keepdims=False)
        g_sum = g_sum + over_pair(away, step)
    weight_part = after(weight, events[1])
    near_parts = [lax.dynamic_slice_in_dim(weight_part, factor_at * block, block, 1)]
    g_steps, distance, at = [g_sum], 2, 2
    while distance < n_fsdp:
        both = after(jnp.stack(near_parts), events[min(at, last)])
        both = moved(both, "fsdp", lambda to, d=distance: to ^ d)
        near_parts = near_parts + [both[k] for k in range(len(near_parts))]
        g_sum = after(g_sum, events[last] if distance == 2 else events[last + 1] + early)
        g_sum = g_sum + moved(g_sum, "fsdp", lambda to, d=distance: to ^ d)
        g_steps.append(g_sum)
        distance, at = 2 * distance, at + 2
    far_parts = over_side(after(jnp.stack(near_parts), events[last + 1] + early))
    parts = [
        part for k in range(len(near_parts)) for part in (near_parts[k], far_parts[k])
    ]

    theirs = after(totals[1], [far_parts, g_steps[-1]])
    grad_own = totals[3] + over_core(theirs)
    pixel_total = float(
        activations.shape[0] * activations.shape[1] * activations.shape[2] * n_fsdp * n_factor
    )

    exponent = jnp.floor(jnp.log2(jnp.maximum(jnp.max(jnp.abs(grad_own)), 1e-30))) - 14.0
    packed = (grad_own * jnp.exp2(-exponent)).astype(jnp.float16)
    exponent = jnp.full((strip, LANES), exponent, jnp.float16)
    packed = jnp.concatenate([packed, exponent], axis=1)
    near_packed = [packed] + [over_layer(packed, step) for step in range(1, n_layer)]
    far_packed = [over_side(array) for array in near_packed]
    strips_of_grad = [
        array[:, :rows].astype(jnp.float32) * jnp.exp2(array[:, rows : rows + 1].astype(jnp.float32))
        for array in near_packed + far_packed
    ]
    cov_own = totals[2] + over_core(after(totals[0], near_packed[1:2]))
    a_factor = 0.5 * a_factor_old + (0.5 / pixel_total) * cov_own.T
    came_from = [(fsdp_at - 2 * step) % n_fsdp for step in range(n_layer)]
    came_from = came_from + [at ^ 1 for at in came_from]
    order = [
        2 * ((pair_at + step) % n_pair) + (core_at + other) % 2
        for other in (1, 0)
        for step in range(n_pair)
    ]
    near_images = [activations] + [maps["pair", 0, step] for step in range(1, n_pair)]
    other_images = after(near_images, events[last] + [near_parts[0]])
    group = near_images + [over_core(image) for image in other_images]
    part_order = [fsdp_at ^ at for at in range(n_fsdp)]
    if aligned and block % LANES == 0:
        group_out = convolve(jnp.stack(part_order), group, parts)
    else:
        kernel = jnp.stack(parts)
        kernel = jnp.concatenate(
            [lax.dynamic_index_in_dim(kernel, at, 0, keepdims=False) for at in part_order]
        ).reshape(3, 3, channels, block)
        group_out = lax.conv_general_dilated(
            jnp.concatenate(group),
            kernel,
            (1, 1),
            "SAME",
            dimension_numbers=("NHWC", "HWIO", "NHWC"),
            preferred_element_type=jnp.float32,
        ).astype(jnp.bfloat16)
        group_out = jnp.split(group_out, n_factor)

    if aligned and block % LANES == 0:
        away, kept = tail_products(
            jnp.stack(came_from + order), after(a_inverse, group_out), g_inverse, strips_of_grad, block
        )
    else:
        inverse = jnp.concatenate(
            [lax.dynamic_slice_in_dim(g_inverse, at * block, block, 1) for at in order], axis=1
        )
        inverse = jnp.concatenate(
            [lax.dynamic_slice_in_dim(inverse, at * strip, strip, 0) for at in came_from]
        )
        partial = lax.dot_general(
            a_inverse,
            jnp.concatenate(strips_of_grad),
            (((1,), (1,)), ((), ())),
            precision=lax.Precision.HIGH,
            preferred_element_type=jnp.float32,
        )
        partial = jnp.dot(
            partial, inverse, precision=lax.Precision.HIGH, preferred_element_type=jnp.float32
        )
        away, kept = partial[:, : channels // 2], partial[:, channels // 2 :]
    by_pair = kept + over_core(away)
    result = by_pair[:, :block]
    for step in range(1, n_pair):
        back = over_pair(by_pair[:, step * block : (step + 1) * block], step)
        result = result + after(back, a_factor)
    natural_grad = result.astype(jnp.bfloat16)


    own_maps, block_order = [], []
    for other in range(2):
        for pair in range(n_pair):
            out = group_out[other * n_pair + pair]
            if pair + other:
                out = moved(out, "factor", lambda at, o=other, p=pair: (at ^ o) - 2 * p)
            own_maps.append(out)
            block_order.append(2 * ((pair_at + pair) % n_pair) + (core_at + other) % 2)
    own_maps = after(own_maps, by_pair)
    if aligned and block % LANES == 0:
        conv_out = side_by_side(jnp.stack(block_order), own_maps)
    else:
        stacked = jnp.zeros((n_factor,) + own_maps[0].shape, jnp.bfloat16)
        for at, out in zip(block_order, own_maps):
            stacked = lax.dynamic_update_index_in_dim(stacked, out, at, 0)
        conv_out = jnp.concatenate(jnp.split(stacked, n_factor), axis=4)[0]

    g_back = over_side(after(g_steps[-1], strips_of_grad[1:2]))
    g_factor_sum = g_steps[-1] + after(g_back, by_pair)
    g_factor = 0.5 * g_factor_old + 0.5 * g_factor_sum
    return (conv_out, a_factor, g_factor, natural_grad)


def solution(mesh):
    images = P(("fsdp", "factor"), None, None, None)
    return jax.shard_map(
        per_device,
        mesh=mesh,
        in_specs=(
            images,
            images,
            P("fsdp", None),
            P("factor", "fsdp"),
            P("factor", None),
            P("fsdp", "factor"),
            P(),
        ),
        out_specs=(
            images,
            P("factor", "fsdp"),
            P("factor", None),
            P("fsdp", "factor"),
        ),
        check_vma=False,
    )
```

```python
import jax
import jax.numpy as jnp
from jax import lax
from jax.experimental import pallas as pl
from jax.experimental.pallas import tpu as pltpu
from jax.sharding import PartitionSpec as P

LANES = 128


def by_rows(first_op, second_op):
    return lax.dot_general(
        first_op, second_op, (((0,), (0,)), ((), ())), preferred_element_type=jnp.float32
    )


def moved(array, axis, target):
    count = lax.axis_size(axis)
    return lax.ppermute(array, axis, [(at, target(at) % count) for at in range(count)])


def tile_of_patches(images, start, width):
    side, channels = images.shape[1], images.shape[3]
    padded = jnp.pad(images, ((0, 0), (1, 1), (1, 1), (0, 0)))
    first_tap, offset = start // channels, start % channels
    rolled = lax.dynamic_slice_in_dim(
        jnp.concatenate([padded, padded], axis=3), offset, channels, 3
    )
    lane = lax.broadcasted_iota(jnp.int32, (1, 1, 1, channels), 3)

    def tap(index):
        index = jnp.minimum(index, 8)
        return lax.dynamic_slice(
            rolled, (0, index // 3, index % 3, 0), (images.shape[0], side, side, channels)
        )

    pieces = []
    for at in range(0, width, channels):
        step = at // channels
        piece = jnp.where(lane < channels - offset, tap(first_tap + step), tap(first_tap + step + 1))
        pieces.append(piece[..., : min(channels, width - at)])
    return jnp.concatenate(pieces, axis=3).reshape(-1, width)


def fill_shifted(shifted, arrivals):
    n_images, tall, side, channels = shifted.shape[1:]
    spots = side * side
    spot = lax.broadcasted_iota(jnp.int32, (spots, LANES), 0) % side
    empty = jnp.zeros((side, channels), jnp.bfloat16)
    for at in range(n_images):
        for col_off in range(3):
            shifted[col_off, at, 0] = empty
            shifted[col_off, at, tall - 1] = empty
    for at, arrival in enumerate(arrivals):
        arrival.wait()
        for lane in range(0, channels, LANES):
            part = shifted[1, at, 1 : side + 1, :, lane : lane + LANES]
            part = part.reshape(spots, LANES).astype(jnp.float32)
            before_it = jnp.where(spot == 0, 0.0, pltpu.roll(part, 1, 0))
            after_it = jnp.where(spot == side - 1, 0.0, pltpu.roll(part, spots - 1, 0))
            for col_off, moved_part in ((0, before_it), (2, after_it)):
                shifted[col_off, at, 1 : side + 1, :, lane : lane + LANES] = moved_part.astype(
                    jnp.bfloat16
                ).reshape(side, side, LANES)


def fetch(sources, targets, sems):
    copies = [
        pltpu.make_async_copy(source, target, sems.at[at])
        for at, (source, target) in enumerate(zip(sources, targets))
    ]
    for copy in copies:
        copy.start()
    return copies


def products_kernel(owners, pairs, n_pair, first, *refs):
    image_refs, strip_refs = refs[: len(pairs)], refs[len(pairs) : len(pairs) + n_pair]
    refs = refs[len(pairs) + n_pair :]
    before, refs = (None, refs) if first else (refs[:4], refs[4:])
    out_refs, totals, (shifted, turned, left, strips, sems) = refs[:4], refs[4:8], refs[8:]
    n_images, side, channels = len(image_refs), image_refs[0].shape[1], image_refs[0].shape[3]
    spots = side * side
    cols, rows = totals[0].shape
    strip = totals[1].shape[0]
    n_fsdp = strip_refs[0].shape[0]
    fsdp_at, factor_at = lax.axis_index("fsdp"), lax.axis_index("factor")

    arrivals = fetch(
        [ref.at[0] for ref in image_refs],
        [shifted.at[1, at, pl.ds(1, side)] for at in range(n_images)],
        sems.at[0],
    )
    strip_copies = fetch(strip_refs, [strips.at[at] for at in range(n_pair)], sems.at[1])
    if not first:
        total_copies = fetch(before, totals, sems.at[2])
    fill_shifted(shifted, arrivals)

    def lanes_of_tap(tap, lane):
        piece = shifted[tap % 3, :, pl.ds(tap // 3, side), :, pl.ds(pl.multiple_of(lane, LANES), LANES)]
        return piece.reshape(n_images * spots, LANES)

    start = fsdp_at * cols
    inside = start % LANES
    for at in range(0, turned.shape[0], LANES):
        lane = start - inside + at
        tap = jnp.minimum(lane // channels, 8)
        turned[at : at + LANES, :] = lanes_of_tap(tap, lane % channels).T
    left[:cols, :] = turned[pl.ds(pl.multiple_of(inside, strip), cols), :]
    for copy in strip_copies:
        copy.wait()
    for at, pair in enumerate(pairs):
        layer, other = owners[at]
        owner = (fsdp_at + n_fsdp - 2 * layer) % n_fsdp
        owner = owner + other * (1 - 2 * (owner % 2))
        left[cols : cols + strip, at * spots : (at + 1) * spots] = strips[pair, owner]
    if not first:
        for copy in total_copies:
            copy.wait()

    tiles_per = rows // LANES
    other_tile = factor_at + 1 - 2 * (factor_at % 2)

    def lanes_at(index):
        whose = jnp.where(index >= tiles_per, 1, 0)
        tile = jnp.where(index >= tiles_per, factor_at, other_tile)
        start = (tile * tiles_per + index - whose * tiles_per) * LANES
        return lanes_of_tap(start // channels, start % channels)

    def product(first_index, count):
        right = jnp.concatenate([lanes_at(first_index + k) for k in range(count)], axis=1)
        return jnp.dot(left[...], right, preferred_element_type=jnp.float32)

    def keep(whose, lane, count, value):
        at = pl.ds(pl.multiple_of(lane, LANES), count * LANES)
        for kind, part in ((0, value[:cols]), (1, value[cols:])):
            if not first:
                part = part + totals[2 * whose + kind][:, at]
            totals[2 * whose + kind][:, at] = part

    half = tiles_per // 2
    odd = tiles_per % 2

    @pl.loop(0, half)
    def _(step):
        keep(0, step * 2 * LANES, 2, product(2 * step, 2))

    if odd:
        both = product(2 * half, 2)
        keep(0, 2 * half * LANES, 1, both[:, :LANES])
        keep(1, 0, 1, both[:, LANES:])
    theirs_out = fetch(totals[:2], out_refs[:2], sems.at[3])

    @pl.loop(0, half)
    def _(step):
        keep(1, (odd + 2 * step) * LANES, 2, product(tiles_per + odd + 2 * step, 2))

    mine_out = fetch(totals[2:], out_refs[2:], sems.at[4])
    for copy in theirs_out + mine_out:
        copy.wait()


def add_products(owners, images, pairs, strips, before, cols, rows):
    n_images, side, channels, strip = len(images), images[0].shape[1], images[0].shape[3], strips[0].shape[1]
    spots = side * side
    shapes = [(height, rows) for height in (cols, strip)] * 2
    operands = [*images, *strips, *(before or [])]
    n_front = n_images + len(strips)
    return pl.pallas_call(
        lambda *refs: products_kernel(owners, pairs, len(strips), before is None, *refs),
        out_shape=[jax.ShapeDtypeStruct(shape, jnp.float32) for shape in shapes],
        in_specs=[pl.BlockSpec(memory_space=pl.ANY)] * len(operands),
        out_specs=[pl.BlockSpec(memory_space=pl.ANY)] * 4,
        scratch_shapes=[pltpu.VMEM(shape, jnp.float32) for shape in shapes]
        + [
            pltpu.VMEM((3, n_images, side + 2, side, channels), jnp.bfloat16),
            pltpu.VMEM(((cols + strip + LANES - 1) // LANES * LANES, n_images * spots), jnp.bfloat16),
            pltpu.VMEM((cols + strip, n_images * spots), jnp.bfloat16),
            pltpu.VMEM((len(strips),) + strips[0].shape, jnp.bfloat16),
            pltpu.SemaphoreType.DMA((5, max(4, n_images))),
        ],
        input_output_aliases={} if before is None else {n_front + k: k for k in range(4)},
        compiler_params=pltpu.CompilerParams(vmem_limit_bytes=26 * 1024 * 1024),
        cost_estimate=pl.CostEstimate(
            flops=4 * (cols + strip) * rows * n_images * spots,
            bytes_accessed=16 * (cols + strip) * rows,
            transcendentals=0,
        ),
    )(*operands)


def tail_kernel(strip, block, layers, *refs):
    a_any, g_any = refs[:2]
    strip_refs, (away_ref, kept_ref) = refs[2:-8], refs[-8:-6]
    a_tile, g_whole, columns, inverse, away_vmem, sems = refs[-6:]
    channels = g_any.shape[0]
    n_fsdp, n_factor = lax.axis_size("fsdp"), lax.axis_size("factor")
    fsdp_at, factor_at = lax.axis_index("fsdp"), lax.axis_index("factor")
    core_at, pair_at = factor_at % 2, factor_at // 2
    copies = fetch([a_any, g_any], [a_tile, g_whole], sems.at[0])
    strip_copies = fetch(
        strip_refs,
        [columns.at[pl.ds(at * strip, strip)] for at in range(len(strip_refs))],
        sems.at[1],
    )
    copies[1].wait()
    for at, (layer, other) in enumerate(layers):
        owner = (fsdp_at + n_fsdp - 2 * layer) % n_fsdp
        owner = owner + other * (1 - 2 * (owner % 2))
        rows = pl.ds(pl.multiple_of(owner * strip, strip), strip)
        for to in range(n_factor):
            away, step = 1 - to // (n_factor // 2), to % (n_factor // 2)
            place = 2 * ((pair_at + step) % (n_factor // 2)) + (core_at + away) % 2
            lanes = pl.ds(pl.multiple_of(place * block, block), block)
            inverse[at * strip : (at + 1) * strip, to * block : (to + 1) * block] = g_whole[rows, lanes]
    copies[0].wait()
    for copy in strip_copies:
        copy.wait()
    first = lax.dot_general(
        a_tile[...],
        columns[...],
        (((1,), (1,)), ((), ())),
        precision=lax.Precision.HIGH,
        preferred_element_type=jnp.float32,
    )
    away_vmem[...] = jnp.dot(
        first,
        inverse[:, : channels // 2],
        precision=lax.Precision.HIGH,
        preferred_element_type=jnp.float32,
    )
    away_out = fetch([away_vmem], [away_ref], sems.at[2])
    kept_ref[...] = jnp.dot(
        first,
        inverse[:, channels // 2 :],
        precision=lax.Precision.HIGH,
        preferred_element_type=jnp.float32,
    )
    away_out[0].wait()


def tail_products(a_inverse, g_inverse, strips, layers, block):
    channels, strip = g_inverse.shape[0], strips[0].shape[0]
    rows, depth = a_inverse.shape
    half = (rows, channels // 2)
    return pl.pallas_call(
        lambda *refs: tail_kernel(strip, block, layers, *refs),
        out_shape=[jax.ShapeDtypeStruct(half, jnp.float32)] * 2,
        in_specs=[pl.BlockSpec(memory_space=pl.ANY)] * (2 + len(strips)),
        out_specs=[pl.BlockSpec(memory_space=pl.ANY), pl.BlockSpec(memory_space=pltpu.VMEM)],
        scratch_shapes=[
            pltpu.VMEM((rows, depth), jnp.float32),
            pltpu.VMEM((channels, channels), jnp.float32),
            pltpu.VMEM((channels, depth), jnp.float32),
            pltpu.VMEM((channels, channels), jnp.float32),
            pltpu.VMEM(half, jnp.float32),
            pltpu.SemaphoreType.DMA((3, max(2, len(strips)))),
        ],
        compiler_params=pltpu.CompilerParams(vmem_limit_bytes=26 * 1024 * 1024),
        cost_estimate=pl.CostEstimate(
            flops=6 * rows * channels * (depth + channels),
            bytes_accessed=4 * rows * (depth + channels),
            transcendentals=0,
        ),
    )(a_inverse, g_inverse, *strips)


def conv_kernel(n_images, *refs):
    image_refs, part_refs = refs[:n_images], refs[n_images : n_images + 2]
    out_refs, (shifted, parts, weight, sems) = refs[n_images + 2 : -4], refs[-4:]
    side, channels = image_refs[0].shape[1], image_refs[0].shape[3]
    n_near, depth, block = part_refs[0].shape
    fsdp_at = lax.axis_index("fsdp")
    arrivals = fetch(
        [ref.at[0] for ref in image_refs],
        [shifted.at[1, at, pl.ds(1, side)] for at in range(n_images)],
        sems.at[0],
    )
    part_copies = fetch(part_refs, [parts.at[at] for at in range(2)], sems.at[1])
    fill_shifted(shifted, arrivals)
    for copy in part_copies:
        copy.wait()
    for near in range(n_near):
        for far in range(2):
            owner = (fsdp_at ^ (2 * near + far)) * depth
            weight[pl.ds(pl.multiple_of(owner, 64), depth), :] = parts[far, near]
    for at, ref in enumerate(out_refs):
        total = jnp.zeros((side * side, block), jnp.float32)
        for tap in range(9):
            left = shifted[tap % 3, at, tap // 3 : tap // 3 + side].reshape(side * side, channels)
            total += jnp.dot(
                left,
                weight[tap * channels : (tap + 1) * channels, :],
                preferred_element_type=jnp.float32,
            )
        ref[0] = total.astype(jnp.bfloat16).reshape(side, side, block)


def convolve(images, near_parts, far_parts):
    n_images, (_, side, _, channels) = len(images), images[0].shape
    block = near_parts.shape[2]
    return pl.pallas_call(
        lambda *refs: conv_kernel(n_images, *refs),
        out_shape=[jax.ShapeDtypeStruct((1, side, side, block), jnp.bfloat16)] * n_images,
        in_specs=[pl.BlockSpec(memory_space=pl.ANY)] * (n_images + 2),
        out_specs=[pl.BlockSpec(memory_space=pltpu.VMEM)] * n_images,
        scratch_shapes=[
            pltpu.VMEM((3, n_images, side + 2, side, channels), jnp.bfloat16),
            pltpu.VMEM((2,) + near_parts.shape, jnp.bfloat16),
            pltpu.VMEM((9 * channels, block), jnp.bfloat16),
            pltpu.SemaphoreType.DMA((2, n_images)),
        ],
        compiler_params=pltpu.CompilerParams(vmem_limit_bytes=16 * 1024 * 1024),
        cost_estimate=pl.CostEstimate(
            flops=36 * n_images * side * side * channels * block,
            bytes_accessed=2 * (9 * channels * block + n_images * side * side * channels),
            transcendentals=0,
        ),
    )(*images, near_parts, far_parts)


def side_by_side_kernel(*refs):
    block, n_factor = refs[0].shape[3], lax.axis_size("factor")
    factor_at, n_pair = lax.axis_index("factor"), n_factor // 2
    for at, ref in enumerate(refs[:-1]):
        place = 2 * ((factor_at // 2 + at % n_pair) % n_pair) + (factor_at + at // n_pair) % 2
        refs[-1][:, :, :, pl.ds(pl.multiple_of(place * block, LANES), block)] = ref[...]


def side_by_side(blocks):
    whole = pl.BlockSpec(memory_space=pltpu.VMEM)
    shape = blocks[0].shape[:3] + (len(blocks) * blocks[0].shape[3],)
    return pl.pallas_call(
        side_by_side_kernel,
        out_shape=jax.ShapeDtypeStruct(shape, blocks[0].dtype),
        in_specs=[whole] * len(blocks),
        out_specs=whole,
        compiler_params=pltpu.CompilerParams(vmem_limit_bytes=4 * 1024 * 1024),
    )(*blocks)


def gather_plan(n_layer, n_pair):
    far_layers = sorted(range(1, n_layer), key=lambda step: min(step, n_layer - step))
    by_side, by_pair = [], []
    for turn, layer in enumerate([0] + far_layers):
        by_side.append((("side", layer, 0), ("layer", layer, 0)))
        for pair in range(1, n_pair):
            by_pair.append((("pair", layer, pair), ("layer", layer, 0)))
            if turn % 2 == 0:
                by_pair.append((("both", layer, pair), ("side", layer, 0)))
            else:
                by_side.append((("both", layer, pair), ("pair", layer, pair)))
    by_layer = [(("layer", layer, 0), None) for layer in far_layers]
    for link in (by_side, by_pair):
        link.sort(key=lambda item: item[0][0] == "both")
    here, due, rounds = {None, ("layer", 0, 0)}, {}, []
    while by_layer or by_side or by_pair:
        here |= {item for item, when in due.items() if when <= len(rounds)}
        due = {item: when for item, when in due.items() if when > len(rounds)}
        now = []
        for link in (by_layer, by_side, by_pair):
            free = [item for item in link if item[1] in here]
            for chosen in free[: 2 if link is by_layer and rounds else 1]:
                link.remove(chosen)
                item, source = chosen
                hops = min(item[1], n_layer - item[1]) if item[0] == "layer" else 1
                due[item] = len(rounds) + hops
                now.append((item, source, "pair" if link is by_pair else item[0], hops))
        rounds.append(now)
    return rounds


def per_device(activations, cotangent, weight, a_factor_old, g_factor_old, a_inverse, g_inverse):
    channels = activations.shape[3]
    n_fsdp, n_factor = lax.axis_size("fsdp"), lax.axis_size("factor")
    n_layer, n_pair = n_fsdp // 2, n_factor // 2
    fsdp_at, factor_at = lax.axis_index("fsdp"), lax.axis_index("factor")
    core_at, pair_at = factor_at % 2, factor_at // 2
    rows, cols = a_factor_old.shape
    strip = channels // n_fsdp
    block = channels // n_factor

    def over_layer(array, step):
        return moved(array, "fsdp", lambda at: at + 2 * step)

    def over_side(array):
        return moved(array, "fsdp", lambda at: at ^ 1)

    def over_pair(array, step):
        return moved(array, "factor", lambda at: at + 2 * step)

    def over_core(array):
        return moved(array, "factor", lambda at: at ^ 1)

    def after(arrays, events):
        return lax.optimization_barrier((arrays, events))[0]

    def transfer(array, item, how):
        if how == "layer":
            return over_layer(array, item[1])
        if how == "pair":
            return over_pair(array, item[2])
        return over_side(array)

    own_cot = cotangent.reshape(-1, channels)
    maps = {("layer", 0, 0): activations}
    plan = gather_plan(n_layer, n_pair)
    events, due = [[]], []
    strips_by_pair = []
    for at, now in enumerate(plan):
        if at == 1:
            strips = after(own_cot, events[1]).T.reshape(n_fsdp, strip, own_cot.shape[0])
            strips_by_pair.append(lax.all_to_all(strips, "fsdp", split_axis=0, concat_axis=0))
        if at == 3:
            strips = after(strips_by_pair[0], events[3])
            strips_by_pair += [over_pair(strips, step) for step in range(1, n_pair)]
            due += [(4, strips) for strips in strips_by_pair]
        sources = [activations if source is None else maps[source] for _, source, _, _ in now]
        sources = after(sources, events[at])
        for array, (item, _, how, hops) in zip(sources, now):
            maps[item] = transfer(array, item, how)
            due.append((at + hops, maps[item]))
        events.append([array for when, array in due if when == at + 1])
    last = len(plan) - 1

    aligned = rows % LANES == 0 and channels % LANES == 0 and activations.shape[0] == 1
    arrived = {("layer", 0, 0): 0}
    for at, now in enumerate(plan):
        arrived.update({item: at + hops for item, _, _, hops in now})
    images = sorted(maps, key=lambda item: arrived[item])
    images.sort(
        key=lambda item: max(when for other, when in arrived.items() if other[1] == item[1])
    )
    half = len(images) // 2
    totals, early = None, []
    for batch in (images[:half], images[half:]):
        owners, pairs = [], []
        for kind, layer, pair in batch:
            owner = (fsdp_at - 2 * layer) % n_fsdp
            owners.append(owner ^ 1 if kind in ("side", "both") else owner)
            pairs.append(pair)
        if aligned:
            totals = add_products(
                [(layer, int(kind in ("side", "both"))) for kind, layer, _ in batch],
                [maps[item] for item in batch], pairs, strips_by_pair, totals, cols, rows
            )
            early = early or [totals[3]]
            continue
        for at in range(0, len(batch), 2 * n_pair):
            part = jnp.concatenate([maps[item] for item in batch[at : at + 2 * n_pair]], axis=0)
            col_tile = tile_of_patches(part, fsdp_at * cols, cols)
            cot_tile = jnp.concatenate(
                [
                    lax.dynamic_index_in_dim(strips_by_pair[pair], owner, 0, keepdims=False)
                    for pair, owner in list(zip(pairs, owners))[at : at + 2 * n_pair]
                ],
                axis=1,
            )
            more = []
            for tile in (factor_at ^ 1, factor_at):
                row_tile = tile_of_patches(part, tile * rows, rows)
                more.append(by_rows(col_tile, row_tile))
                more.append(jnp.dot(cot_tile, row_tile, preferred_element_type=jnp.float32))
            totals = more if totals is None else [old + new for old, new in zip(totals, more)]

    g_partial = by_rows(own_cot, own_cot).reshape(n_pair, 2, block, channels)
    g_pairs = lax.dynamic_index_in_dim(g_partial, core_at, 1, keepdims=False) + over_core(
        lax.dynamic_index_in_dim(g_partial, 1 - core_at, 1, keepdims=False)
    )
    g_pairs = after(g_pairs, events[last])
    g_sum = lax.dynamic_index_in_dim(g_pairs, pair_at, 0, keepdims=False)
    for step in range(1, n_pair):
        away = lax.dynamic_index_in_dim(g_pairs, (pair_at + step) % n_pair, 0, keepdims=False)
        g_sum = g_sum + over_pair(away, step)
    weight_part = after(weight, events[1])
    near_parts = [lax.dynamic_slice_in_dim(weight_part, factor_at * block, block, 1)]
    distance, at = 2, 2
    while distance < n_fsdp:
        both = after(jnp.stack(near_parts), events[min(at, last)])
        both = moved(both, "fsdp", lambda to, d=distance: to ^ d)
        near_parts = near_parts + [both[k] for k in range(len(near_parts))]
        distance, at = 2 * distance, at + 2
    near_stack = jnp.stack(near_parts)
    far_parts = over_side(after(near_stack, events[last + 1] + early))

    g_sum = after(g_sum, events[last + 1] + early)
    g_sum = g_sum + moved(g_sum, "fsdp", lambda to: to ^ 2)
    near_images = [activations] + [maps["pair", 0, step] for step in range(1, n_pair)]
    group = near_images + [over_core(image) for image in after(near_images, events[last])]
    theirs = after(totals[1], [far_parts, g_sum] + group)
    grad_own = totals[3] + over_core(theirs)
    pixel_total = float(
        activations.shape[0] * activations.shape[1] * activations.shape[2] * n_fsdp * n_factor
    )

    exponent = jnp.floor(jnp.log2(jnp.maximum(jnp.max(jnp.abs(grad_own)), 1e-30))) - 14.0
    packed = (grad_own * jnp.exp2(-exponent)).astype(jnp.float16)
    exponent = jnp.full((strip, LANES), exponent, jnp.float16)
    packed = jnp.concatenate([packed, exponent], axis=1)
    near_packed = [packed] + [over_layer(packed, step) for step in range(1, n_layer)]
    far_packed = [over_side(array) for array in near_packed]
    strips_of_grad = [
        array[:, :rows].astype(jnp.float32) * jnp.exp2(array[:, rows : rows + 1].astype(jnp.float32))
        for array in near_packed + far_packed
    ]
    cov_own = totals[2] + over_core(after(totals[0], [packed]))
    a_factor = 0.5 * a_factor_old + (0.5 / pixel_total) * cov_own.T
    came_from = [(fsdp_at - 2 * step) % n_fsdp for step in range(n_layer)]
    came_from = came_from + [at ^ 1 for at in came_from]
    order = [
        2 * ((pair_at + step) % n_pair) + (core_at + other) % 2
        for other in (1, 0)
        for step in range(n_pair)
    ]
    g_sum = after(g_sum, near_packed[1:2])
    g_sum = g_sum + over_side(g_sum)
    group = after(group, near_packed[1:2])
    part_order = [fsdp_at ^ at for at in range(n_fsdp)]
    if aligned and block % LANES == 0:
        group_out = convolve(group, near_stack, far_parts)
    else:
        kernel = jnp.stack([part for pair in zip(near_stack, far_parts) for part in pair])
        kernel = jnp.concatenate(
            [lax.dynamic_index_in_dim(kernel, at, 0, keepdims=False) for at in part_order]
        ).reshape(3, 3, channels, block)
        group_out = lax.conv_general_dilated(
            jnp.concatenate(group),
            kernel,
            (1, 1),
            "SAME",
            dimension_numbers=("NHWC", "HWIO", "NHWC"),
            preferred_element_type=jnp.float32,
        ).astype(jnp.bfloat16)
        group_out = jnp.split(group_out, n_factor)

    if aligned and block % LANES == 0:
        away, kept = tail_products(
            after(a_inverse, [*group_out, a_factor, g_sum]),
            g_inverse,
            strips_of_grad,
            [(step, other) for other in range(2) for step in range(n_layer)],
            block,
        )
    else:
        inverse = jnp.concatenate(
            [lax.dynamic_slice_in_dim(g_inverse, at * block, block, 1) for at in order], axis=1
        )
        inverse = jnp.concatenate(
            [lax.dynamic_slice_in_dim(inverse, at * strip, strip, 0) for at in came_from]
        )
        partial = lax.dot_general(
            a_inverse,
            jnp.concatenate(strips_of_grad),
            (((1,), (1,)), ((), ())),
            precision=lax.Precision.HIGH,
            preferred_element_type=jnp.float32,
        )
        partial = jnp.dot(
            partial, inverse, precision=lax.Precision.HIGH, preferred_element_type=jnp.float32
        )
        away, kept = partial[:, : channels // 2], partial[:, channels // 2 :]
    by_pair = kept + over_core(away)
    result = by_pair[:, :block]
    for step in range(1, n_pair):
        back = over_pair(by_pair[:, step * block : (step + 1) * block], step)
        result = result + back
    natural_grad = result.astype(jnp.bfloat16)


    own_maps, block_order = [], []
    for other in range(2):
        for pair in range(n_pair):
            out = group_out[other * n_pair + pair]
            if pair + other:
                out = moved(out, "factor", lambda at, o=other, p=pair: (at ^ o) - 2 * p)
            own_maps.append(out)
            block_order.append(2 * ((pair_at + pair) % n_pair) + (core_at + other) % 2)
    own_maps = after(own_maps, by_pair)
    if aligned and block % LANES == 0:
        conv_out = side_by_side(own_maps)
    else:
        stacked = jnp.zeros((n_factor,) + own_maps[0].shape, jnp.bfloat16)
        for at, out in zip(block_order, own_maps):
            stacked = lax.dynamic_update_index_in_dim(stacked, out, at, 0)
        conv_out = jnp.concatenate(jnp.split(stacked, n_factor), axis=4)[0]

    distance = 4
    while distance < n_fsdp:
        g_sum = after(g_sum, strips_of_grad[:n_layer])
        g_sum = g_sum + moved(g_sum, "fsdp", lambda to, d=distance: to ^ d)
        distance *= 2
    g_factor_sum = g_sum
    g_factor = 0.5 * g_factor_old + 0.5 * g_factor_sum
    return (conv_out, a_factor, g_factor, natural_grad)


def solution(mesh):
    images = P(("fsdp", "factor"), None, None, None)
    return jax.shard_map(
        per_device,
        mesh=mesh,
        in_specs=(
            images,
            images,
            P("fsdp", None),
            P("factor", "fsdp"),
            P("factor", None),
            P("fsdp", "factor"),
            P(),
        ),
        out_specs=(
            images,
            P("factor", "fsdp"),
            P("factor", None),
            P("fsdp", "factor"),
        ),
        check_vma=False,
    )
```

```python
import jax
import jax.numpy as jnp
from jax import lax
from jax.experimental import pallas as pl
from jax.experimental.pallas import tpu as pltpu
from jax.sharding import PartitionSpec as P

LANES = 128


def by_rows(first_op, second_op):
    return lax.dot_general(
        first_op, second_op, (((0,), (0,)), ((), ())), preferred_element_type=jnp.float32
    )


def moved(array, axis, target):
    count = lax.axis_size(axis)
    return lax.ppermute(array, axis, [(at, target(at) % count) for at in range(count)])


def tile_of_patches(images, start, width):
    side, channels = images.shape[1], images.shape[3]
    padded = jnp.pad(images, ((0, 0), (1, 1), (1, 1), (0, 0)))
    first_tap, offset = start // channels, start % channels
    rolled = lax.dynamic_slice_in_dim(
        jnp.concatenate([padded, padded], axis=3), offset, channels, 3
    )
    lane = lax.broadcasted_iota(jnp.int32, (1, 1, 1, channels), 3)

    def tap(index):
        index = jnp.minimum(index, 8)
        return lax.dynamic_slice(
            rolled, (0, index // 3, index % 3, 0), (images.shape[0], side, side, channels)
        )

    pieces = []
    for at in range(0, width, channels):
        step = at // channels
        piece = jnp.where(lane < channels - offset, tap(first_tap + step), tap(first_tap + step + 1))
        pieces.append(piece[..., : min(channels, width - at)])
    return jnp.concatenate(pieces, axis=3).reshape(-1, width)


def fill_shifted(shifted, arrivals):
    n_images, tall, side, channels = shifted.shape[1:]
    spots = side * side
    spot = lax.broadcasted_iota(jnp.int32, (spots, LANES), 0) % side
    empty = jnp.zeros((side, channels), jnp.bfloat16)
    for at in range(n_images):
        for col_off in range(3):
            shifted[col_off, at, 0] = empty
            shifted[col_off, at, tall - 1] = empty
    for at, arrival in enumerate(arrivals):
        arrival.wait()
        for lane in range(0, channels, LANES):
            part = shifted[1, at, 1 : side + 1, :, lane : lane + LANES]
            part = part.reshape(spots, LANES).astype(jnp.float32)
            before_it = jnp.where(spot == 0, 0.0, pltpu.roll(part, 1, 0))
            after_it = jnp.where(spot == side - 1, 0.0, pltpu.roll(part, spots - 1, 0))
            for col_off, moved_part in ((0, before_it), (2, after_it)):
                shifted[col_off, at, 1 : side + 1, :, lane : lane + LANES] = moved_part.astype(
                    jnp.bfloat16
                ).reshape(side, side, LANES)


def fetch(sources, targets, sems):
    copies = [
        pltpu.make_async_copy(source, target, sems.at[at])
        for at, (source, target) in enumerate(zip(sources, targets))
    ]
    for copy in copies:
        copy.start()
    return copies


def products_kernel(owners, pairs, n_pair, first, *refs):
    image_refs, strip_refs = refs[: len(pairs)], refs[len(pairs) : len(pairs) + n_pair]
    refs = refs[len(pairs) + n_pair :]
    before, refs = (None, refs) if first else (refs[:4], refs[4:])
    out_refs, totals, (shifted, turned, left, strips, sems) = refs[:4], refs[4:8], refs[8:]
    n_images, side, channels = len(image_refs), image_refs[0].shape[1], image_refs[0].shape[3]
    spots = side * side
    cols, rows = totals[0].shape
    strip = totals[1].shape[0]
    n_fsdp = strip_refs[0].shape[0]
    fsdp_at, factor_at = lax.axis_index("fsdp"), lax.axis_index("factor")

    arrivals = fetch(
        [ref.at[0] for ref in image_refs],
        [shifted.at[1, at, pl.ds(1, side)] for at in range(n_images)],
        sems.at[0],
    )
    strip_copies = fetch(strip_refs, [strips.at[at] for at in range(n_pair)], sems.at[1])
    if not first:
        total_copies = fetch(before, totals, sems.at[2])
    fill_shifted(shifted, arrivals)

    def lanes_of_tap(tap, lane):
        piece = shifted[tap % 3, :, pl.ds(tap // 3, side), :, pl.ds(pl.multiple_of(lane, LANES), LANES)]
        return piece.reshape(n_images * spots, LANES)

    start = fsdp_at * cols
    inside = start % LANES
    for at in range(0, turned.shape[0], LANES):
        lane = start - inside + at
        tap = jnp.minimum(lane // channels, 8)
        turned[at : at + LANES, :] = lanes_of_tap(tap, lane % channels).T
    left[:cols, :] = turned[pl.ds(pl.multiple_of(inside, strip), cols), :]
    for copy in strip_copies:
        copy.wait()
    for at, pair in enumerate(pairs):
        layer, other = owners[at]
        owner = (fsdp_at + n_fsdp - 2 * layer) % n_fsdp
        owner = owner + other * (1 - 2 * (owner % 2))
        left[cols : cols + strip, at * spots : (at + 1) * spots] = strips[pair, owner]
    if not first:
        for copy in total_copies:
            copy.wait()

    tiles_per = rows // LANES
    other_tile = factor_at + 1 - 2 * (factor_at % 2)

    def lanes_at(index):
        whose = jnp.where(index >= tiles_per, 1, 0)
        tile = jnp.where(index >= tiles_per, factor_at, other_tile)
        start = (tile * tiles_per + index - whose * tiles_per) * LANES
        return lanes_of_tap(start // channels, start % channels)

    def product(first_index, count):
        right = jnp.concatenate([lanes_at(first_index + k) for k in range(count)], axis=1)
        return jnp.dot(left[...], right, preferred_element_type=jnp.float32)

    def keep(whose, lane, count, value):
        at = slice(lane, lane + count * LANES)
        for kind, part in ((0, value[:cols]), (1, value[cols:])):
            if not first:
                part = part + totals[2 * whose + kind][:, at]
            totals[2 * whose + kind][:, at] = part

    keep(0, 0, tiles_per, product(0, tiles_per))
    theirs_out = fetch(totals[:2], out_refs[:2], sems.at[3])
    keep(1, 0, tiles_per, product(tiles_per, tiles_per))
    mine_out = fetch(totals[2:], out_refs[2:], sems.at[4])
    for copy in theirs_out + mine_out:
        copy.wait()


def add_products(owners, images, pairs, strips, before, cols, rows):
    n_images, side, channels, strip = len(images), images[0].shape[1], images[0].shape[3], strips[0].shape[1]
    spots = side * side
    shapes = [(height, rows) for height in (cols, strip)] * 2
    operands = [*images, *strips, *(before or [])]
    n_front = n_images + len(strips)
    return pl.pallas_call(
        lambda *refs: products_kernel(owners, pairs, len(strips), before is None, *refs),
        out_shape=[jax.ShapeDtypeStruct(shape, jnp.float32) for shape in shapes],
        in_specs=[pl.BlockSpec(memory_space=pl.ANY)] * len(operands),
        out_specs=[pl.BlockSpec(memory_space=pl.ANY)] * 4,
        scratch_shapes=[pltpu.VMEM(shape, jnp.float32) for shape in shapes]
        + [
            pltpu.VMEM((3, n_images, side + 2, side, channels), jnp.bfloat16),
            pltpu.VMEM(((cols + strip + LANES - 1) // LANES * LANES, n_images * spots), jnp.bfloat16),
            pltpu.VMEM((cols + strip, n_images * spots), jnp.bfloat16),
            pltpu.VMEM((len(strips),) + strips[0].shape, jnp.bfloat16),
            pltpu.SemaphoreType.DMA((5, max(4, n_images))),
        ],
        input_output_aliases={} if before is None else {n_front + k: k for k in range(4)},
        compiler_params=pltpu.CompilerParams(vmem_limit_bytes=58 * 1024 * 1024),
        cost_estimate=pl.CostEstimate(
            flops=4 * (cols + strip) * rows * n_images * spots,
            bytes_accessed=16 * (cols + strip) * rows,
            transcendentals=0,
        ),
    )(*operands)


def tail_kernel(strip, block, layers, *refs):
    a_any, g_any = refs[:2]
    strip_refs, (away_ref, kept_ref) = refs[2:-8], refs[-8:-6]
    a_tile, g_whole, columns, inverse, away_vmem, sems = refs[-6:]
    channels = g_any.shape[0]
    n_fsdp, n_factor = lax.axis_size("fsdp"), lax.axis_size("factor")
    fsdp_at, factor_at = lax.axis_index("fsdp"), lax.axis_index("factor")
    core_at, pair_at = factor_at % 2, factor_at // 2
    copies = fetch([a_any, g_any], [a_tile, g_whole], sems.at[0])
    strip_copies = fetch(
        strip_refs,
        [columns.at[pl.ds(at * strip, strip)] for at in range(len(strip_refs))],
        sems.at[1],
    )
    copies[1].wait()
    for at, (layer, other) in enumerate(layers):
        owner = (fsdp_at + n_fsdp - 2 * layer) % n_fsdp
        owner = owner + other * (1 - 2 * (owner % 2))
        rows = pl.ds(pl.multiple_of(owner * strip, strip), strip)
        for to in range(n_factor):
            away, step = 1 - to // (n_factor // 2), to % (n_factor // 2)
            place = 2 * ((pair_at + step) % (n_factor // 2)) + (core_at + away) % 2
            lanes = pl.ds(pl.multiple_of(place * block, block), block)
            inverse[at * strip : (at + 1) * strip, to * block : (to + 1) * block] = g_whole[rows, lanes]
    copies[0].wait()
    for copy in strip_copies:
        copy.wait()
    first = lax.dot_general(
        a_tile[...],
        columns[...],
        (((1,), (1,)), ((), ())),
        precision=lax.Precision.HIGH,
        preferred_element_type=jnp.float32,
    )
    away_vmem[...] = jnp.dot(
        first,
        inverse[:, : channels // 2],
        precision=lax.Precision.HIGH,
        preferred_element_type=jnp.float32,
    )
    away_out = fetch([away_vmem], [away_ref], sems.at[2])
    kept_ref[...] = jnp.dot(
        first,
        inverse[:, channels // 2 :],
        precision=lax.Precision.HIGH,
        preferred_element_type=jnp.float32,
    )
    away_out[0].wait()


def tail_products(a_inverse, g_inverse, strips, layers, block):
    channels, strip = g_inverse.shape[0], strips[0].shape[0]
    rows, depth = a_inverse.shape
    half = (rows, channels // 2)
    return pl.pallas_call(
        lambda *refs: tail_kernel(strip, block, layers, *refs),
        out_shape=[jax.ShapeDtypeStruct(half, jnp.float32)] * 2,
        in_specs=[pl.BlockSpec(memory_space=pl.ANY)] * (2 + len(strips)),
        out_specs=[pl.BlockSpec(memory_space=pl.ANY), pl.BlockSpec(memory_space=pltpu.VMEM)],
        scratch_shapes=[
            pltpu.VMEM((rows, depth), jnp.float32),
            pltpu.VMEM((channels, channels), jnp.float32),
            pltpu.VMEM((channels, depth), jnp.float32),
            pltpu.VMEM((channels, channels), jnp.float32),
            pltpu.VMEM(half, jnp.float32),
            pltpu.SemaphoreType.DMA((3, max(2, len(strips)))),
        ],
        compiler_params=pltpu.CompilerParams(vmem_limit_bytes=26 * 1024 * 1024),
        cost_estimate=pl.CostEstimate(
            flops=6 * rows * channels * (depth + channels),
            bytes_accessed=4 * rows * (depth + channels),
            transcendentals=0,
        ),
    )(a_inverse, g_inverse, *strips)


def conv_kernel(n_images, *refs):
    image_refs, part_refs = refs[:n_images], refs[n_images : n_images + 2]
    out_refs, (shifted, parts, weight, sems) = refs[n_images + 2 : -4], refs[-4:]
    side, channels = image_refs[0].shape[1], image_refs[0].shape[3]
    n_near, depth, block = part_refs[0].shape
    fsdp_at = lax.axis_index("fsdp")
    arrivals = fetch(
        [ref.at[0] for ref in image_refs],
        [shifted.at[1, at, pl.ds(1, side)] for at in range(n_images)],
        sems.at[0],
    )
    part_copies = fetch(part_refs, [parts.at[at] for at in range(2)], sems.at[1])
    fill_shifted(shifted, arrivals)
    for copy in part_copies:
        copy.wait()
    for near in range(n_near):
        for far in range(2):
            owner = (fsdp_at ^ (2 * near + far)) * depth
            weight[pl.ds(pl.multiple_of(owner, 64), depth), :] = parts[far, near]
    for at, ref in enumerate(out_refs):
        total = jnp.zeros((side * side, block), jnp.float32)
        for tap in range(9):
            left = shifted[tap % 3, at, tap // 3 : tap // 3 + side].reshape(side * side, channels)
            total += jnp.dot(
                left,
                weight[tap * channels : (tap + 1) * channels, :],
                preferred_element_type=jnp.float32,
            )
        ref[0] = total.astype(jnp.bfloat16).reshape(side, side, block)


def convolve(images, near_parts, far_parts):
    n_images, (_, side, _, channels) = len(images), images[0].shape
    block = near_parts.shape[2]
    return pl.pallas_call(
        lambda *refs: conv_kernel(n_images, *refs),
        out_shape=[jax.ShapeDtypeStruct((1, side, side, block), jnp.bfloat16)] * n_images,
        in_specs=[pl.BlockSpec(memory_space=pl.ANY)] * (n_images + 2),
        out_specs=[pl.BlockSpec(memory_space=pltpu.VMEM)] * n_images,
        scratch_shapes=[
            pltpu.VMEM((3, n_images, side + 2, side, channels), jnp.bfloat16),
            pltpu.VMEM((2,) + near_parts.shape, jnp.bfloat16),
            pltpu.VMEM((9 * channels, block), jnp.bfloat16),
            pltpu.SemaphoreType.DMA((2, n_images)),
        ],
        compiler_params=pltpu.CompilerParams(vmem_limit_bytes=58 * 1024 * 1024),
        cost_estimate=pl.CostEstimate(
            flops=36 * n_images * side * side * channels * block,
            bytes_accessed=2 * (9 * channels * block + n_images * side * side * channels),
            transcendentals=0,
        ),
    )(*images, near_parts, far_parts)


def side_by_side_kernel(*refs):
    block, n_factor = refs[0].shape[3], lax.axis_size("factor")
    factor_at, n_pair = lax.axis_index("factor"), n_factor // 2
    for at, ref in enumerate(refs[:-1]):
        place = 2 * ((factor_at // 2 + at % n_pair) % n_pair) + (factor_at + at // n_pair) % 2
        refs[-1][:, :, :, pl.ds(pl.multiple_of(place * block, LANES), block)] = ref[...]


def side_by_side(blocks):
    whole = pl.BlockSpec(memory_space=pltpu.VMEM)
    shape = blocks[0].shape[:3] + (len(blocks) * blocks[0].shape[3],)
    return pl.pallas_call(
        side_by_side_kernel,
        out_shape=jax.ShapeDtypeStruct(shape, blocks[0].dtype),
        in_specs=[whole] * len(blocks),
        out_specs=whole,
        compiler_params=pltpu.CompilerParams(vmem_limit_bytes=4 * 1024 * 1024),
    )(*blocks)


def gather_plan(n_layer, n_pair):
    far_layers = sorted(range(1, n_layer), key=lambda step: min(step, n_layer - step))
    by_side, by_pair = [], []
    for turn, layer in enumerate([0] + far_layers):
        by_side.append((("side", layer, 0), ("layer", layer, 0)))
        for pair in range(1, n_pair):
            by_pair.append((("pair", layer, pair), ("layer", layer, 0)))
            if turn % 2 == 0:
                by_pair.append((("both", layer, pair), ("side", layer, 0)))
            else:
                by_side.append((("both", layer, pair), ("pair", layer, pair)))
    by_layer = [(("layer", layer, 0), None) for layer in far_layers]
    for link in (by_side, by_pair):
        link.sort(key=lambda item: item[0][0] == "both")
    here, due, rounds = {None, ("layer", 0, 0)}, {}, []
    while by_layer or by_side or by_pair:
        here |= {item for item, when in due.items() if when <= len(rounds)}
        due = {item: when for item, when in due.items() if when > len(rounds)}
        now = []
        for link in (by_layer, by_side, by_pair):
            free = [item for item in link if item[1] in here]
            for chosen in free[: 2 if link is by_layer and rounds else 1]:
                link.remove(chosen)
                item, source = chosen
                hops = min(item[1], n_layer - item[1]) if item[0] == "layer" else 1
                due[item] = len(rounds) + hops
                now.append((item, source, "pair" if link is by_pair else item[0], hops))
        rounds.append(now)
    return rounds


def per_device(activations, cotangent, weight, a_factor_old, g_factor_old, a_inverse, g_inverse):
    channels = activations.shape[3]
    n_fsdp, n_factor = lax.axis_size("fsdp"), lax.axis_size("factor")
    n_layer, n_pair = n_fsdp // 2, n_factor // 2
    fsdp_at, factor_at = lax.axis_index("fsdp"), lax.axis_index("factor")
    core_at, pair_at = factor_at % 2, factor_at // 2
    rows, cols = a_factor_old.shape
    strip = channels // n_fsdp
    block = channels // n_factor

    def over_layer(array, step):
        return moved(array, "fsdp", lambda at: at + 2 * step)

    def over_side(array):
        return moved(array, "fsdp", lambda at: at ^ 1)

    def over_pair(array, step):
        return moved(array, "factor", lambda at: at + 2 * step)

    def over_core(array):
        return moved(array, "factor", lambda at: at ^ 1)

    def after(arrays, events):
        return lax.optimization_barrier((arrays, events))[0]

    def transfer(array, item, how):
        if how == "layer":
            return over_layer(array, item[1])
        if how == "pair":
            return over_pair(array, item[2])
        return over_side(array)

    own_cot = cotangent.reshape(-1, channels)
    maps = {("layer", 0, 0): activations}
    plan = gather_plan(n_layer, n_pair)
    events, due = [[]], []
    strips_by_pair = []
    for at, now in enumerate(plan):
        if at == 1:
            strips = after(own_cot, [maps["side", 0, 0]]).T.reshape(n_fsdp, strip, own_cot.shape[0])
            strips_by_pair.append(lax.all_to_all(strips, "fsdp", split_axis=0, concat_axis=0))
        if at == 3:
            strips = after(strips_by_pair[0], events[3])
            strips_by_pair += [over_pair(strips, step) for step in range(1, n_pair)]
            due += [(4, strips) for strips in strips_by_pair]
        sources = [activations if source is None else maps[source] for _, source, _, _ in now]
        sources = after(sources, events[max(at - 1, 0)])
        for array, (item, _, how, hops) in zip(sources, now):
            maps[item] = transfer(array, item, how)
            due.append((at + hops, maps[item]))
        events.append([array for when, array in due if when == at + 1])
    last = len(plan) - 1

    aligned = rows % LANES == 0 and channels % LANES == 0 and activations.shape[0] == 1
    arrived = {("layer", 0, 0): 0}
    for at, now in enumerate(plan):
        arrived.update({item: at + hops for item, _, _, hops in now})
    images = sorted(maps, key=lambda item: arrived[item])
    images.sort(
        key=lambda item: max(when for other, when in arrived.items() if other[1] == item[1])
    )
    half = len(images) // 2
    totals, early = None, []
    for batch in (images[:half], images[half:]):
        owners, pairs = [], []
        for kind, layer, pair in batch:
            owner = (fsdp_at - 2 * layer) % n_fsdp
            owners.append(owner ^ 1 if kind in ("side", "both") else owner)
            pairs.append(pair)
        if aligned:
            totals = add_products(
                [(layer, int(kind in ("side", "both"))) for kind, layer, _ in batch],
                [maps[item] for item in batch], pairs, strips_by_pair, totals, cols, rows
            )
            early = early or [totals[3]]
            continue
        for at in range(0, len(batch), 2 * n_pair):
            part = jnp.concatenate([maps[item] for item in batch[at : at + 2 * n_pair]], axis=0)
            col_tile = tile_of_patches(part, fsdp_at * cols, cols)
            cot_tile = jnp.concatenate(
                [
                    lax.dynamic_index_in_dim(strips_by_pair[pair], owner, 0, keepdims=False)
                    for pair, owner in list(zip(pairs, owners))[at : at + 2 * n_pair]
                ],
                axis=1,
            )
            more = []
            for tile in (factor_at ^ 1, factor_at):
                row_tile = tile_of_patches(part, tile * rows, rows)
                more.append(by_rows(col_tile, row_tile))
                more.append(jnp.dot(cot_tile, row_tile, preferred_element_type=jnp.float32))
            totals = more if totals is None else [old + new for old, new in zip(totals, more)]

    g_partial = by_rows(after(own_cot, events[2]), own_cot).reshape(n_pair, 2, block, channels)
    g_pairs = lax.dynamic_index_in_dim(g_partial, core_at, 1, keepdims=False) + over_core(
        lax.dynamic_index_in_dim(g_partial, 1 - core_at, 1, keepdims=False)
    )
    g_pairs = after(g_pairs, events[last - 1])
    g_sum = lax.dynamic_index_in_dim(g_pairs, pair_at, 0, keepdims=False)
    for step in range(1, n_pair):
        away = lax.dynamic_index_in_dim(g_pairs, (pair_at + step) % n_pair, 0, keepdims=False)
        g_sum = g_sum + over_pair(away, step)
    weight_part = after(weight, events[1])
    near_parts = [lax.dynamic_slice_in_dim(weight_part, factor_at * block, block, 1)]
    distance, at = 2, 2
    while distance < n_fsdp:
        both = after(jnp.stack(near_parts), events[min(at, last)])
        both = moved(both, "fsdp", lambda to, d=distance: to ^ d)
        near_parts = near_parts + [both[k] for k in range(len(near_parts))]
        distance, at = 2 * distance, at + 2
    near_stack = jnp.stack(near_parts)
    far_parts = over_side(after(near_stack, events[last + 1] + early))

    distance = 2
    while distance < n_fsdp:
        g_sum = after(g_sum, events[last] if distance == 2 else events[last + 1] + early)
        g_sum = g_sum + moved(g_sum, "fsdp", lambda to, d=distance: to ^ d)
        distance *= 2
    near_images = [activations] + [maps["pair", 0, step] for step in range(1, n_pair)]
    group = near_images + [over_core(image) for image in after(near_images, events[last])]
    theirs = after(totals[1], [far_parts, g_sum] + group)
    grad_own = totals[3] + over_core(theirs)
    pixel_total = float(
        activations.shape[0] * activations.shape[1] * activations.shape[2] * n_fsdp * n_factor
    )

    exponent = jnp.floor(jnp.log2(jnp.maximum(jnp.max(jnp.abs(grad_own)), 1e-30))) - 14.0
    packed = (grad_own * jnp.exp2(-exponent)).astype(jnp.float16)
    exponent = jnp.full((strip, LANES), exponent, jnp.float16)
    packed = jnp.concatenate([packed, exponent], axis=1)
    near_packed = [packed] + [over_layer(packed, step) for step in range(1, n_layer)]
    far_packed, came = {0: over_side(packed)}, []
    for step in sorted(range(1, n_layer), key=lambda step: min(step, n_layer - step)):
        far_packed[step] = over_side(after(near_packed[step], came))
        came = came + [near_packed[step]]
    far_packed = [far_packed[step] for step in range(n_layer)]
    strips_of_grad = [
        array[:, :rows].astype(jnp.float32) * jnp.exp2(array[:, rows : rows + 1].astype(jnp.float32))
        for array in near_packed + far_packed
    ]
    cov_own = totals[2] + over_core(after(totals[0], [packed]))
    a_factor = 0.5 * a_factor_old + (0.5 / pixel_total) * cov_own.T
    came_from = [(fsdp_at - 2 * step) % n_fsdp for step in range(n_layer)]
    came_from = came_from + [at ^ 1 for at in came_from]
    order = [
        2 * ((pair_at + step) % n_pair) + (core_at + other) % 2
        for other in (1, 0)
        for step in range(n_pair)
    ]
    g_sum = after(g_sum, near_packed[1:2])
    g_sum = g_sum + over_side(g_sum)
    group = after(group, near_packed[1:2])
    part_order = [fsdp_at ^ at for at in range(n_fsdp)]
    if aligned and block % LANES == 0:
        group_out = convolve(group, near_stack, far_parts)
    else:
        kernel = jnp.stack([part for pair in zip(near_stack, far_parts) for part in pair])
        kernel = jnp.concatenate(
            [lax.dynamic_index_in_dim(kernel, at, 0, keepdims=False) for at in part_order]
        ).reshape(3, 3, channels, block)
        group_out = lax.conv_general_dilated(
            jnp.concatenate(group),
            kernel,
            (1, 1),
            "SAME",
            dimension_numbers=("NHWC", "HWIO", "NHWC"),
            preferred_element_type=jnp.float32,
        ).astype(jnp.bfloat16)
        group_out = jnp.split(group_out, n_factor)

    if aligned and block % LANES == 0:
        away, kept = tail_products(
            after(a_inverse, [*group_out, a_factor, g_sum]),
            g_inverse,
            strips_of_grad,
            [(step, other) for other in range(2) for step in range(n_layer)],
            block,
        )
    else:
        inverse = jnp.concatenate(
            [lax.dynamic_slice_in_dim(g_inverse, at * block, block, 1) for at in order], axis=1
        )
        inverse = jnp.concatenate(
            [lax.dynamic_slice_in_dim(inverse, at * strip, strip, 0) for at in came_from]
        )
        partial = lax.dot_general(
            a_inverse,
            jnp.concatenate(strips_of_grad),
            (((1,), (1,)), ((), ())),
            precision=lax.Precision.HIGH,
            preferred_element_type=jnp.float32,
        )
        partial = jnp.dot(
            partial, inverse, precision=lax.Precision.HIGH, preferred_element_type=jnp.float32
        )
        away, kept = partial[:, : channels // 2], partial[:, channels // 2 :]
    by_pair = kept + over_core(away)
    result = by_pair[:, :block]
    for step in range(1, n_pair):
        back = over_pair(by_pair[:, step * block : (step + 1) * block], step)
        result = result + back
    natural_grad = result.astype(jnp.bfloat16)


    own_maps, block_order = [], []
    for other in range(2):
        for pair in range(n_pair):
            out = group_out[other * n_pair + pair]
            if pair + other:
                out = moved(out, "factor", lambda at, o=other, p=pair: (at ^ o) - 2 * p)
            own_maps.append(out)
            block_order.append(2 * ((pair_at + pair) % n_pair) + (core_at + other) % 2)
    own_maps = after(own_maps, by_pair)
    if aligned and block % LANES == 0:
        conv_out = side_by_side(own_maps)
    else:
        stacked = jnp.zeros((n_factor,) + own_maps[0].shape, jnp.bfloat16)
        for at, out in zip(block_order, own_maps):
            stacked = lax.dynamic_update_index_in_dim(stacked, out, at, 0)
        conv_out = jnp.concatenate(jnp.split(stacked, n_factor), axis=4)[0]

    g_factor_sum = g_sum
    g_factor = 0.5 * g_factor_old + 0.5 * g_factor_sum
    return (conv_out, a_factor, g_factor, natural_grad)


def solution(mesh):
    images = P(("fsdp", "factor"), None, None, None)
    return jax.shard_map(
        per_device,
        mesh=mesh,
        in_specs=(
            images,
            images,
            P("fsdp", None),
            P("factor", "fsdp"),
            P("factor", None),
            P("fsdp", "factor"),
            P(),
        ),
        out_specs=(
            images,
            P("factor", "fsdp"),
            P("factor", None),
            P("fsdp", "factor"),
        ),
        check_vma=False,
    )
```

```python
import jax
import jax.numpy as jnp
from jax import lax
from jax.experimental import pallas as pl
from jax.experimental.pallas import tpu as pltpu
from jax.sharding import PartitionSpec as P

LANES = 128


def by_rows(first_op, second_op):
    return lax.dot_general(
        first_op, second_op, (((0,), (0,)), ((), ())), preferred_element_type=jnp.float32
    )


def moved(array, axis, target):
    count = lax.axis_size(axis)
    return lax.ppermute(array, axis, [(at, target(at) % count) for at in range(count)])


def tile_of_patches(images, start, width):
    side, channels = images.shape[1], images.shape[3]
    padded = jnp.pad(images, ((0, 0), (1, 1), (1, 1), (0, 0)))
    first_tap, offset = start // channels, start % channels
    rolled = lax.dynamic_slice_in_dim(
        jnp.concatenate([padded, padded], axis=3), offset, channels, 3
    )
    lane = lax.broadcasted_iota(jnp.int32, (1, 1, 1, channels), 3)

    def tap(index):
        index = jnp.minimum(index, 8)
        return lax.dynamic_slice(
            rolled, (0, index // 3, index % 3, 0), (images.shape[0], side, side, channels)
        )

    pieces = []
    for at in range(0, width, channels):
        step = at // channels
        piece = jnp.where(lane < channels - offset, tap(first_tap + step), tap(first_tap + step + 1))
        pieces.append(piece[..., : min(channels, width - at)])
    return jnp.concatenate(pieces, axis=3).reshape(-1, width)


def fill_shifted(shifted, arrivals):
    n_images, tall, side, channels = shifted.shape[1:]
    spots = side * side
    spot = lax.broadcasted_iota(jnp.int32, (spots, LANES), 0) % side
    empty = jnp.zeros((side, channels), jnp.bfloat16)
    for at in range(n_images):
        for col_off in range(3):
            shifted[col_off, at, 0] = empty
            shifted[col_off, at, tall - 1] = empty
    for at, arrival in enumerate(arrivals):
        arrival.wait()
        for lane in range(0, channels, LANES):
            part = shifted[1, at, 1 : side + 1, :, lane : lane + LANES]
            part = part.reshape(spots, LANES).astype(jnp.float32)
            before_it = jnp.where(spot == 0, 0.0, pltpu.roll(part, 1, 0))
            after_it = jnp.where(spot == side - 1, 0.0, pltpu.roll(part, spots - 1, 0))
            for col_off, moved_part in ((0, before_it), (2, after_it)):
                shifted[col_off, at, 1 : side + 1, :, lane : lane + LANES] = moved_part.astype(
                    jnp.bfloat16
                ).reshape(side, side, LANES)


def fetch(sources, targets, sems):
    copies = [
        pltpu.make_async_copy(source, target, sems.at[at])
        for at, (source, target) in enumerate(zip(sources, targets))
    ]
    for copy in copies:
        copy.start()
    return copies


def products_kernel(owners, pairs, n_pair, first, *refs):
    image_refs, strip_refs = refs[: len(pairs)], refs[len(pairs) : len(pairs) + n_pair]
    refs = refs[len(pairs) + n_pair :]
    before, refs = (None, refs) if first else (refs[:4], refs[4:])
    out_refs, totals, (shifted, turned, left, strips, sems) = refs[:4], refs[4:8], refs[8:]
    n_images, side, channels = len(image_refs), image_refs[0].shape[1], image_refs[0].shape[3]
    spots = side * side
    cols, rows = totals[0].shape
    strip = totals[1].shape[0]
    n_fsdp = strip_refs[0].shape[0]
    fsdp_at, factor_at = lax.axis_index("fsdp"), lax.axis_index("factor")

    arrivals = fetch(
        [ref.at[0] for ref in image_refs],
        [shifted.at[1, at, pl.ds(1, side)] for at in range(n_images)],
        sems.at[0],
    )
    strip_copies = fetch(strip_refs, [strips.at[at] for at in range(n_pair)], sems.at[1])
    if not first:
        total_copies = fetch(before, totals, sems.at[2])
    fill_shifted(shifted, arrivals)

    def lanes_of_tap(tap, lane):
        piece = shifted[tap % 3, :, pl.ds(tap // 3, side), :, pl.ds(pl.multiple_of(lane, LANES), LANES)]
        return piece.reshape(n_images * spots, LANES)

    start = fsdp_at * cols
    inside = start % LANES
    for at in range(0, turned.shape[0], LANES):
        lane = start - inside + at
        tap = jnp.minimum(lane // channels, 8)
        turned[at : at + LANES, :] = lanes_of_tap(tap, lane % channels).T
    left[:cols, :] = turned[pl.ds(pl.multiple_of(inside, strip), cols), :]
    for copy in strip_copies:
        copy.wait()
    for at, pair in enumerate(pairs):
        layer, other = owners[at]
        owner = (fsdp_at + n_fsdp - 2 * layer) % n_fsdp
        owner = owner + other * (1 - 2 * (owner % 2))
        left[cols : cols + strip, at * spots : (at + 1) * spots] = strips[pair, owner]
    if not first:
        for copy in total_copies:
            copy.wait()

    tiles_per = rows // LANES
    other_tile = factor_at + 1 - 2 * (factor_at % 2)

    def lanes_at(index):
        whose = jnp.where(index >= tiles_per, 1, 0)
        tile = jnp.where(index >= tiles_per, factor_at, other_tile)
        start = (tile * tiles_per + index - whose * tiles_per) * LANES
        return lanes_of_tap(start // channels, start % channels)

    def product(first_index, count):
        right = jnp.concatenate([lanes_at(first_index + k) for k in range(count)], axis=1)
        return jnp.dot(left[...], right, preferred_element_type=jnp.float32)

    def keep(whose, lane, count, value):
        at = slice(lane, lane + count * LANES)
        for kind, part in ((0, value[:cols]), (1, value[cols:])):
            if not first:
                part = part + totals[2 * whose + kind][:, at]
            totals[2 * whose + kind][:, at] = part
        grads = totals[2 * whose + 1]
        grads[:, rows:] = jnp.full((strip, LANES), jnp.max(jnp.abs(grads[:, :rows])))

    keep(0, 0, tiles_per, product(0, tiles_per))
    theirs_out = fetch(totals[:2], out_refs[:2], sems.at[3])
    keep(1, 0, tiles_per, product(tiles_per, tiles_per))
    mine_out = fetch(totals[2:], out_refs[2:], sems.at[4])
    for copy in theirs_out + mine_out:
        copy.wait()


def add_products(owners, images, pairs, strips, before, cols, rows):
    n_images, side, channels, strip = len(images), images[0].shape[1], images[0].shape[3], strips[0].shape[1]
    spots = side * side
    shapes = [(cols, rows), (strip, rows + LANES)] * 2
    operands = [*images, *strips, *(before or [])]
    n_front = n_images + len(strips)
    return pl.pallas_call(
        lambda *refs: products_kernel(owners, pairs, len(strips), before is None, *refs),
        out_shape=[jax.ShapeDtypeStruct(shape, jnp.float32) for shape in shapes],
        in_specs=[pl.BlockSpec(memory_space=pl.ANY)] * len(operands),
        out_specs=[pl.BlockSpec(memory_space=pl.ANY)] * 4,
        scratch_shapes=[pltpu.VMEM(shape, jnp.float32) for shape in shapes]
        + [
            pltpu.VMEM((3, n_images, side + 2, side, channels), jnp.bfloat16),
            pltpu.VMEM(((cols + strip + LANES - 1) // LANES * LANES, n_images * spots), jnp.bfloat16),
            pltpu.VMEM((cols + strip, n_images * spots), jnp.bfloat16),
            pltpu.VMEM((len(strips),) + strips[0].shape, jnp.bfloat16),
            pltpu.SemaphoreType.DMA((5, max(4, n_images))),
        ],
        input_output_aliases={} if before is None else {n_front + k: k for k in range(4)},
        compiler_params=pltpu.CompilerParams(vmem_limit_bytes=58 * 1024 * 1024),
        cost_estimate=pl.CostEstimate(
            flops=4 * (cols + strip) * rows * n_images * spots,
            bytes_accessed=16 * (cols + strip) * rows,
            transcendentals=0,
        ),
    )(*operands)


def tail_kernel(strip, block, layers, *refs):
    a_any, g_any = refs[:2]
    strip_refs, (away_ref, kept_ref) = refs[2:-8], refs[-8:-6]
    a_tile, g_whole, columns, inverse, away_vmem, sems = refs[-6:]
    channels = g_any.shape[0]
    n_fsdp, n_factor = lax.axis_size("fsdp"), lax.axis_size("factor")
    fsdp_at, factor_at = lax.axis_index("fsdp"), lax.axis_index("factor")
    core_at, pair_at = factor_at % 2, factor_at // 2
    copies = fetch([a_any, g_any], [a_tile, g_whole], sems.at[0])
    strip_copies = fetch(
        strip_refs,
        [columns.at[pl.ds(at * strip, strip)] for at in range(len(strip_refs))],
        sems.at[1],
    )
    copies[1].wait()
    for at, (layer, other) in enumerate(layers):
        owner = (fsdp_at + n_fsdp - 2 * layer) % n_fsdp
        owner = owner + other * (1 - 2 * (owner % 2))
        rows = pl.ds(pl.multiple_of(owner * strip, strip), strip)
        for to in range(n_factor):
            away, step = 1 - to // (n_factor // 2), to % (n_factor // 2)
            place = 2 * ((pair_at + step) % (n_factor // 2)) + (core_at + away) % 2
            lanes = pl.ds(pl.multiple_of(place * block, block), block)
            inverse[at * strip : (at + 1) * strip, to * block : (to + 1) * block] = g_whole[rows, lanes]
    copies[0].wait()
    for copy in strip_copies:
        copy.wait()
    first = lax.dot_general(
        a_tile[...],
        columns[...],
        (((1,), (1,)), ((), ())),
        precision=lax.Precision.HIGH,
        preferred_element_type=jnp.float32,
    )
    away_vmem[...] = jnp.dot(
        first,
        inverse[:, : channels // 2],
        precision=lax.Precision.HIGH,
        preferred_element_type=jnp.float32,
    )
    away_out = fetch([away_vmem], [away_ref], sems.at[2])
    kept_ref[...] = jnp.dot(
        first,
        inverse[:, channels // 2 :],
        precision=lax.Precision.HIGH,
        preferred_element_type=jnp.float32,
    )
    away_out[0].wait()


def tail_products(a_inverse, g_inverse, strips, layers, block):
    channels, strip = g_inverse.shape[0], strips[0].shape[0]
    rows, depth = a_inverse.shape
    half = (rows, channels // 2)
    return pl.pallas_call(
        lambda *refs: tail_kernel(strip, block, layers, *refs),
        out_shape=[jax.ShapeDtypeStruct(half, jnp.float32)] * 2,
        in_specs=[pl.BlockSpec(memory_space=pl.ANY)] * (2 + len(strips)),
        out_specs=[pl.BlockSpec(memory_space=pl.ANY), pl.BlockSpec(memory_space=pltpu.VMEM)],
        scratch_shapes=[
            pltpu.VMEM((rows, depth), jnp.float32),
            pltpu.VMEM((channels, channels), jnp.float32),
            pltpu.VMEM((channels, depth), jnp.float32),
            pltpu.VMEM((channels, channels), jnp.float32),
            pltpu.VMEM(half, jnp.float32),
            pltpu.SemaphoreType.DMA((3, max(2, len(strips)))),
        ],
        compiler_params=pltpu.CompilerParams(vmem_limit_bytes=26 * 1024 * 1024),
        cost_estimate=pl.CostEstimate(
            flops=6 * rows * channels * (depth + channels),
            bytes_accessed=4 * rows * (depth + channels),
            transcendentals=0,
        ),
    )(a_inverse, g_inverse, *strips)


def conv_kernel(n_images, *refs):
    image_refs, part_refs = refs[:n_images], refs[n_images : n_images + 2]
    out_refs, (shifted, parts, weight, sems) = refs[n_images + 2 : -4], refs[-4:]
    side, channels = image_refs[0].shape[1], image_refs[0].shape[3]
    n_near, depth, block = part_refs[0].shape
    fsdp_at = lax.axis_index("fsdp")
    arrivals = fetch(
        [ref.at[0] for ref in image_refs],
        [shifted.at[1, at, pl.ds(1, side)] for at in range(n_images)],
        sems.at[0],
    )
    part_copies = fetch(part_refs, [parts.at[at] for at in range(2)], sems.at[1])
    fill_shifted(shifted, arrivals)
    for copy in part_copies:
        copy.wait()
    for near in range(n_near):
        for far in range(2):
            owner = (fsdp_at ^ (2 * near + far)) * depth
            weight[pl.ds(pl.multiple_of(owner, 64), depth), :] = parts[far, near]
    for at, ref in enumerate(out_refs):
        total = jnp.zeros((side * side, block), jnp.float32)
        for tap in range(9):
            left = shifted[tap % 3, at, tap // 3 : tap // 3 + side].reshape(side * side, channels)
            total += jnp.dot(
                left,
                weight[tap * channels : (tap + 1) * channels, :],
                preferred_element_type=jnp.float32,
            )
        ref[0] = total.astype(jnp.bfloat16).reshape(side, side, block)


def convolve(images, near_parts, far_parts):
    n_images, (_, side, _, channels) = len(images), images[0].shape
    block = near_parts.shape[2]
    return pl.pallas_call(
        lambda *refs: conv_kernel(n_images, *refs),
        out_shape=[jax.ShapeDtypeStruct((1, side, side, block), jnp.bfloat16)] * n_images,
        in_specs=[pl.BlockSpec(memory_space=pl.ANY)] * (n_images + 2),
        out_specs=[pl.BlockSpec(memory_space=pltpu.VMEM)] * n_images,
        scratch_shapes=[
            pltpu.VMEM((3, n_images, side + 2, side, channels), jnp.bfloat16),
            pltpu.VMEM((2,) + near_parts.shape, jnp.bfloat16),
            pltpu.VMEM((9 * channels, block), jnp.bfloat16),
            pltpu.SemaphoreType.DMA((2, n_images)),
        ],
        compiler_params=pltpu.CompilerParams(vmem_limit_bytes=58 * 1024 * 1024),
        cost_estimate=pl.CostEstimate(
            flops=36 * n_images * side * side * channels * block,
            bytes_accessed=2 * (9 * channels * block + n_images * side * side * channels),
            transcendentals=0,
        ),
    )(*images, near_parts, far_parts)


def side_by_side_kernel(*refs):
    block, n_factor = refs[0].shape[3], lax.axis_size("factor")
    factor_at, n_pair = lax.axis_index("factor"), n_factor // 2
    for at, ref in enumerate(refs[:-1]):
        place = 2 * ((factor_at // 2 + at % n_pair) % n_pair) + (factor_at + at // n_pair) % 2
        refs[-1][:, :, :, pl.ds(pl.multiple_of(place * block, LANES), block)] = ref[...]


def side_by_side(blocks):
    whole = pl.BlockSpec(memory_space=pltpu.VMEM)
    shape = blocks[0].shape[:3] + (len(blocks) * blocks[0].shape[3],)
    return pl.pallas_call(
        side_by_side_kernel,
        out_shape=jax.ShapeDtypeStruct(shape, blocks[0].dtype),
        in_specs=[whole] * len(blocks),
        out_specs=whole,
        compiler_params=pltpu.CompilerParams(vmem_limit_bytes=4 * 1024 * 1024),
    )(*blocks)


def gather_plan(n_layer, n_pair):
    far_layers = sorted(range(1, n_layer), key=lambda step: min(step, n_layer - step))
    waiting = {"layer": [(("layer", layer, 0), None) for layer in far_layers], "side": [], "pair": []}
    for turn, layer in enumerate([0] + far_layers):
        waiting["side"].append((("side", layer, 0), ("layer", layer, 0)))
        for pair in range(1, n_pair):
            waiting["pair"].append((("pair", layer, pair), ("layer", layer, 0)))
            if turn % 2 == 0:
                waiting["pair"].append((("both", layer, pair), ("side", layer, 0)))
            else:
                waiting["side"].append((("both", layer, pair), ("pair", layer, pair)))
    for link in waiting.values():
        link.sort(key=lambda entry: entry[0][0] == "both")
    ready, busy, turns = {None: 0, ("layer", 0, 0): 0}, {link: 0 for link in waiting}, {}
    order, step = [], 0
    while any(waiting.values()):
        for link, entries in waiting.items():
            free = [entry for entry in entries if ready.get(entry[1], step + 1) <= step]
            if busy[link] > step or not free:
                continue
            count = 2 if link == "layer" and step == 0 else 1
            for item, source in free[:count]:
                entries.remove((item, source))
                hops = min(item[1], n_layer - item[1]) if link == "layer" else 1
                busy[link] = step + hops * count
                ready[item] = busy[link]
                turns[link] = turns.get(link, -1) + 1
                order.append((item, source, link, turns[link]))
        step += 1
    return order, ready


def per_device(activations, cotangent, weight, a_factor_old, g_factor_old, a_inverse, g_inverse):
    channels = activations.shape[3]
    n_fsdp, n_factor = lax.axis_size("fsdp"), lax.axis_size("factor")
    n_layer, n_pair = n_fsdp // 2, n_factor // 2
    fsdp_at, factor_at = lax.axis_index("fsdp"), lax.axis_index("factor")
    core_at, pair_at = factor_at % 2, factor_at // 2
    rows, cols = a_factor_old.shape
    strip = channels // n_fsdp
    block = channels // n_factor

    def over_layer(array, step):
        return moved(array, "fsdp", lambda at: at + 2 * step)

    def over_side(array):
        return moved(array, "fsdp", lambda at: at ^ 1)

    def over_pair(array, step):
        return moved(array, "factor", lambda at: at + 2 * step)

    def over_core(array):
        return moved(array, "factor", lambda at: at ^ 1)

    def after(arrays, events):
        return lax.optimization_barrier((arrays, events))[0]

    def transfer(array, item, how):
        if how == "layer":
            return over_layer(array, item[1])
        if how == "pair":
            return over_pair(array, item[2])
        return over_side(array)

    own_cot = cotangent.reshape(-1, channels)
    maps = {("layer", 0, 0): activations}
    plan, ready = gather_plan(n_layer, n_pair)
    sent = {"layer": [], "side": [], "pair": []}
    strips_by_pair = []
    for item, source, link, turn in plan:
        array = activations if source is None else maps[source]
        events = sent[link][max(turn - 2, 0) : turn - 1]
        if link == "pair" and item == [entry[0] for entry in plan if entry[2] == "pair"][-1]:
            events = events + strips_by_pair
        maps[item] = transfer(after(array, events), item, link)
        sent[link].append(maps[item])
        if link == "side" and turn == 0:
            strips = after(own_cot, [maps[item]]).T.reshape(n_fsdp, strip, own_cot.shape[0])
            strips = lax.all_to_all(strips, "fsdp", split_axis=0, concat_axis=0)
        if link == "pair" and turn == 2:
            strips_by_pair = [strips] + [
                over_pair(after(strips, [maps[item]]), step) for step in range(1, n_pair)
            ]
    first_event, last_layer = sent["side"][:1], sent["layer"][-1:]
    near_end, at_end = sent["pair"][-2:-1], sent["pair"][-1:] + sent["side"][-1:]

    aligned = rows % LANES == 0 and channels % LANES == 0 and activations.shape[0] == 1
    images = sorted(maps, key=lambda item: ready[item])
    half = len(images) // 2
    totals, early = None, []
    for batch in (images[:half], images[half:]):
        owners, pairs = [], []
        for kind, layer, pair in batch:
            owner = (fsdp_at - 2 * layer) % n_fsdp
            owners.append(owner ^ 1 if kind in ("side", "both") else owner)
            pairs.append(pair)
        if aligned:
            totals = add_products(
                [(layer, int(kind in ("side", "both"))) for kind, layer, _ in batch],
                [maps[item] for item in batch], pairs, strips_by_pair, totals, cols, rows
            )
            early = early or [totals[3]]
            continue
        for at in range(0, len(batch), 2 * n_pair):
            part = jnp.concatenate([maps[item] for item in batch[at : at + 2 * n_pair]], axis=0)
            col_tile = tile_of_patches(part, fsdp_at * cols, cols)
            cot_tile = jnp.concatenate(
                [
                    lax.dynamic_index_in_dim(strips_by_pair[pair], owner, 0, keepdims=False)
                    for pair, owner in list(zip(pairs, owners))[at : at + 2 * n_pair]
                ],
                axis=1,
            )
            more = []
            for tile in (factor_at ^ 1, factor_at):
                row_tile = tile_of_patches(part, tile * rows, rows)
                more.append(by_rows(col_tile, row_tile))
                more.append(jnp.dot(cot_tile, row_tile, preferred_element_type=jnp.float32))
            totals = more if totals is None else [old + new for old, new in zip(totals, more)]
    if not aligned:
        for at in (1, 3):
            largest = jnp.full((strip, LANES), jnp.max(jnp.abs(totals[at])))
            totals[at] = jnp.concatenate([totals[at], largest], axis=1)

    g_partial = by_rows(after(own_cot, first_event), own_cot).reshape(n_pair, 2, block, channels)
    g_pairs = lax.dynamic_index_in_dim(g_partial, core_at, 1, keepdims=False) + over_core(
        lax.dynamic_index_in_dim(g_partial, 1 - core_at, 1, keepdims=False)
    )
    g_pairs = after(g_pairs, near_end)
    g_sum = lax.dynamic_index_in_dim(g_pairs, pair_at, 0, keepdims=False)
    for step in range(1, n_pair):
        away = lax.dynamic_index_in_dim(g_pairs, (pair_at + step) % n_pair, 0, keepdims=False)
        g_sum = g_sum + over_pair(away, step)
    weight_part = after(weight, last_layer)
    near_parts = [lax.dynamic_slice_in_dim(weight_part, factor_at * block, block, 1)]
    distance = 2
    while distance < n_fsdp:
        both = moved(jnp.stack(near_parts), "fsdp", lambda to, d=distance: to ^ d)
        near_parts = near_parts + [both[k] for k in range(len(near_parts))]
        distance *= 2
    near_stack = jnp.stack(near_parts)
    far_parts = over_side(after(near_stack, at_end + early))
    distance = n_fsdp // 2
    g_sum = after(g_sum, at_end + early)
    while distance > 2:
        g_sum = g_sum + moved(g_sum, "fsdp", lambda to, d=distance: to ^ d)
        distance //= 2
    near_images = [activations] + [maps["pair", 0, step] for step in range(1, n_pair)]
    group = near_images + [over_core(image) for image in after(near_images, near_end)]
    theirs = after(totals[1], [far_parts, g_sum] + group)
    theirs = over_core(theirs)
    pixel_total = float(
        activations.shape[0] * activations.shape[1] * activations.shape[2] * n_fsdp * n_factor
    )

    largest = totals[3][:, rows : rows + 1] + theirs[:, rows : rows + 1]
    exponent = jnp.floor(jnp.log2(jnp.maximum(largest, 1e-30))) - 14.0
    packed = ((totals[3] + theirs)[:, :rows] * jnp.exp2(-exponent)).astype(jnp.float16)
    exponent = jnp.broadcast_to(exponent.astype(jnp.float16), (strip, LANES))
    packed = jnp.concatenate([packed, exponent], axis=1)
    near_packed = [packed] + [over_layer(packed, step) for step in range(1, n_layer)]

    g_sum = g_sum + over_side(g_sum)
    group = after(group, near_packed[n_layer - 1 :] + [g_sum])
    if aligned and block % LANES == 0:
        group_out = convolve(group, near_stack, far_parts)
    else:
        kernel = jnp.stack([part for pair in zip(near_stack, far_parts) for part in pair])
        kernel = jnp.concatenate(
            [
                lax.dynamic_index_in_dim(kernel, fsdp_at ^ at, 0, keepdims=False)
                for at in range(n_fsdp)
            ]
        ).reshape(3, 3, channels, block)
        group_out = lax.conv_general_dilated(
            jnp.concatenate(group),
            kernel,
            (1, 1),
            "SAME",
            dimension_numbers=("NHWC", "HWIO", "NHWC"),
            preferred_element_type=jnp.float32,
        ).astype(jnp.bfloat16)
        group_out = jnp.split(group_out, n_factor)
    own_maps, block_order = [], []
    for other in range(2):
        for pair in range(n_pair):
            out = group_out[other * n_pair + pair]
            if pair + other:
                out = moved(out, "factor", lambda at, o=other, p=pair: (at ^ o) - 2 * p)
            own_maps.append(out)
            block_order.append(2 * ((pair_at + pair) % n_pair) + (core_at + other) % 2)

    far_packed, came = {0: over_side(packed)}, []
    for step in sorted(range(1, n_layer), key=lambda step: min(step, n_layer - step)):
        if step == n_layer // 2:
            came = came + list(group_out)
        far_packed[step] = over_side(after(near_packed[step], came))
        came = came + [near_packed[step]]
    far_packed = [far_packed[step] for step in range(n_layer)]
    g_sum = after(g_sum, near_packed)
    g_sum = g_sum + moved(g_sum, "fsdp", lambda to: to ^ 2)
    strips_of_grad = [
        array[:, :rows].astype(jnp.float32) * jnp.exp2(array[:, rows : rows + 1].astype(jnp.float32))
        for array in near_packed + far_packed
    ]
    came_from = [(fsdp_at - 2 * step) % n_fsdp for step in range(n_layer)]
    came_from = came_from + [at ^ 1 for at in came_from]
    order = [
        2 * ((pair_at + step) % n_pair) + (core_at + other) % 2
        for other in (1, 0)
        for step in range(n_pair)
    ]
    if aligned and block % LANES == 0:
        away, kept = tail_products(
            after(a_inverse, own_maps[1:n_pair] + own_maps[n_pair + 1 :]),
            g_inverse,
            strips_of_grad,
            [(step, other) for other in range(2) for step in range(n_layer)],
            block,
        )
    else:
        inverse = jnp.concatenate(
            [lax.dynamic_slice_in_dim(g_inverse, at * block, block, 1) for at in order], axis=1
        )
        inverse = jnp.concatenate(
            [lax.dynamic_slice_in_dim(inverse, at * strip, strip, 0) for at in came_from]
        )
        partial = lax.dot_general(
            a_inverse,
            jnp.concatenate(strips_of_grad),
            (((1,), (1,)), ((), ())),
            precision=lax.Precision.HIGH,
            preferred_element_type=jnp.float32,
        )
        partial = jnp.dot(
            partial, inverse, precision=lax.Precision.HIGH, preferred_element_type=jnp.float32
        )
        away, kept = partial[:, : channels // 2], partial[:, channels // 2 :]
    by_pair = kept + over_core(away)
    cov_own = totals[2] + after(over_core(after(totals[0], [packed])), by_pair)
    a_factor = 0.5 * a_factor_old + (0.5 / pixel_total) * cov_own.T
    result = by_pair[:, :block]
    for step in range(1, n_pair):
        back = over_pair(by_pair[:, step * block : (step + 1) * block], step)
        result = result + after(back, a_factor)
    natural_grad = result.astype(jnp.bfloat16)


    own_maps = after(own_maps, by_pair)
    if aligned and block % LANES == 0:
        conv_out = side_by_side(own_maps)
    else:
        stacked = jnp.zeros((n_factor,) + own_maps[0].shape, jnp.bfloat16)
        for at, out in zip(block_order, own_maps):
            stacked = lax.dynamic_update_index_in_dim(stacked, out, at, 0)
        conv_out = jnp.concatenate(jnp.split(stacked, n_factor), axis=4)[0]

    g_factor = 0.5 * g_factor_old + 0.5 * g_sum
    return (conv_out, a_factor, g_factor, natural_grad)


def solution(mesh):
    images = P(("fsdp", "factor"), None, None, None)
    return jax.shard_map(
        per_device,
        mesh=mesh,
        in_specs=(
            images,
            images,
            P("fsdp", None),
            P("factor", "fsdp"),
            P("factor", None),
            P("fsdp", "factor"),
            P(),
        ),
        out_specs=(
            images,
            P("factor", "fsdp"),
            P("factor", None),
            P("fsdp", "factor"),
        ),
        check_vma=False,
    )
```

```python
import jax
import jax.numpy as jnp
from jax import lax
from jax.experimental import pallas as pl
from jax.experimental.pallas import tpu as pltpu
from jax.sharding import PartitionSpec as P

LANES = 128


def by_rows(first_op, second_op):
    return lax.dot_general(
        first_op, second_op, (((0,), (0,)), ((), ())), preferred_element_type=jnp.float32
    )


def moved(array, axis, target):
    count = lax.axis_size(axis)
    return lax.ppermute(array, axis, [(at, target(at) % count) for at in range(count)])


def tile_of_patches(images, start, width):
    side, channels = images.shape[1], images.shape[3]
    padded = jnp.pad(images, ((0, 0), (1, 1), (1, 1), (0, 0)))
    first_tap, offset = start // channels, start % channels
    rolled = lax.dynamic_slice_in_dim(
        jnp.concatenate([padded, padded], axis=3), offset, channels, 3
    )
    lane = lax.broadcasted_iota(jnp.int32, (1, 1, 1, channels), 3)

    def tap(index):
        index = jnp.minimum(index, 8)
        return lax.dynamic_slice(
            rolled, (0, index // 3, index % 3, 0), (images.shape[0], side, side, channels)
        )

    pieces = []
    for at in range(0, width, channels):
        step = at // channels
        piece = jnp.where(lane < channels - offset, tap(first_tap + step), tap(first_tap + step + 1))
        pieces.append(piece[..., : min(channels, width - at)])
    return jnp.concatenate(pieces, axis=3).reshape(-1, width)


def fill_shifted(shifted, arrivals):
    n_images, tall, side, channels = shifted.shape[1:]
    spots = side * side
    spot = lax.broadcasted_iota(jnp.int32, (spots, LANES), 0) % side
    empty = jnp.zeros((side, channels), jnp.bfloat16)
    for at in range(n_images):
        for col_off in range(3):
            shifted[col_off, at, 0] = empty
            shifted[col_off, at, tall - 1] = empty
    for at, arrival in enumerate(arrivals):
        arrival.wait()
        for lane in range(0, channels, LANES):
            part = shifted[1, at, 1 : side + 1, :, lane : lane + LANES]
            part = part.reshape(spots, LANES).astype(jnp.float32)
            before_it = jnp.where(spot == 0, 0.0, pltpu.roll(part, 1, 0))
            after_it = jnp.where(spot == side - 1, 0.0, pltpu.roll(part, spots - 1, 0))
            for col_off, moved_part in ((0, before_it), (2, after_it)):
                shifted[col_off, at, 1 : side + 1, :, lane : lane + LANES] = moved_part.astype(
                    jnp.bfloat16
                ).reshape(side, side, LANES)


def fetch(sources, targets, sems):
    copies = [
        pltpu.make_async_copy(source, target, sems.at[at])
        for at, (source, target) in enumerate(zip(sources, targets))
    ]
    for copy in copies:
        copy.start()
    return copies


def products_kernel(owners, first, *refs):
    image_refs, strips_ref = refs[: len(owners)], refs[len(owners)]
    refs = refs[len(owners) + 1 :]
    before, refs = (None, refs) if first else (refs[:4], refs[4:])
    out_refs, totals, (shifted, turned, left, strips, sems) = refs[:4], refs[4:8], refs[8:]
    n_images, side, channels = len(image_refs), image_refs[0].shape[1], image_refs[0].shape[3]
    spots = side * side
    cols, rows = totals[0].shape
    strip = totals[1].shape[0]
    n_fsdp, n_pair = lax.axis_size("fsdp"), lax.axis_size("factor") // 2
    fsdp_at, factor_at = lax.axis_index("fsdp"), lax.axis_index("factor")

    arrivals = fetch(
        [ref.at[0] for ref in image_refs],
        [shifted.at[1, at, pl.ds(1, side)] for at in range(n_images)],
        sems.at[0],
    )
    strip_copies = fetch([strips_ref], [strips], sems.at[1])
    if not first:
        total_copies = fetch(before, totals, sems.at[2])
    fill_shifted(shifted, arrivals)

    def lanes_of_tap(tap, lane):
        piece = shifted[tap % 3, :, pl.ds(tap // 3, side), :, pl.ds(pl.multiple_of(lane, LANES), LANES)]
        return piece.reshape(n_images * spots, LANES)

    start = fsdp_at * cols
    inside = start % LANES
    for at in range(0, turned.shape[0], LANES):
        lane = start - inside + at
        tap = jnp.minimum(lane // channels, 8)
        turned[at : at + LANES, :] = lanes_of_tap(tap, lane % channels).T
    left[:cols, :] = turned[pl.ds(pl.multiple_of(inside, strip), cols), :]
    for copy in strip_copies:
        copy.wait()
    for at, (layer, other, pair) in enumerate(owners):
        owner = (fsdp_at + n_fsdp - 2 * layer) % n_fsdp
        owner = owner + other * (1 - 2 * (owner % 2))
        owner = owner * n_pair + (factor_at // 2 + n_pair - pair) % n_pair
        left[cols : cols + strip, at * spots : (at + 1) * spots] = strips[owner]
    if not first:
        for copy in total_copies:
            copy.wait()

    tiles_per = rows // LANES
    other_tile = factor_at + 1 - 2 * (factor_at % 2)

    def lanes_at(index):
        whose = jnp.where(index >= tiles_per, 1, 0)
        tile = jnp.where(index >= tiles_per, factor_at, other_tile)
        start = (tile * tiles_per + index - whose * tiles_per) * LANES
        return lanes_of_tap(start // channels, start % channels)

    def product(first_index, count):
        right = jnp.concatenate([lanes_at(first_index + k) for k in range(count)], axis=1)
        return jnp.dot(left[...], right, preferred_element_type=jnp.float32)

    def keep(whose, lane, count, value):
        at = slice(lane, lane + count * LANES)
        for kind, part in ((0, value[:cols]), (1, value[cols:])):
            if not first:
                part = part + totals[2 * whose + kind][:, at]
            totals[2 * whose + kind][:, at] = part
        grads = totals[2 * whose + 1]
        grads[:, rows:] = jnp.full((strip, LANES), jnp.max(jnp.abs(grads[:, :rows])))

    keep(0, 0, tiles_per, product(0, tiles_per))
    theirs_out = fetch(totals[:2], out_refs[:2], sems.at[3])
    keep(1, 0, tiles_per, product(tiles_per, tiles_per))
    mine_out = fetch(totals[2:], out_refs[2:], sems.at[4])
    for copy in theirs_out + mine_out:
        copy.wait()


def add_products(owners, images, strips, before, cols, rows):
    n_images, side, channels, strip = len(images), images[0].shape[1], images[0].shape[3], strips.shape[1]
    spots = side * side
    shapes = [(cols, rows), (strip, rows + LANES)] * 2
    operands = [*images, strips, *(before or [])]
    n_front = n_images + 1
    return pl.pallas_call(
        lambda *refs: products_kernel(owners, before is None, *refs),
        out_shape=[jax.ShapeDtypeStruct(shape, jnp.float32) for shape in shapes],
        in_specs=[pl.BlockSpec(memory_space=pl.ANY)] * len(operands),
        out_specs=[pl.BlockSpec(memory_space=pl.ANY)] * 4,
        scratch_shapes=[pltpu.VMEM(shape, jnp.float32) for shape in shapes]
        + [
            pltpu.VMEM((3, n_images, side + 2, side, channels), jnp.bfloat16),
            pltpu.VMEM(((cols + strip + LANES - 1) // LANES * LANES, n_images * spots), jnp.bfloat16),
            pltpu.VMEM((cols + strip, n_images * spots), jnp.bfloat16),
            pltpu.VMEM(strips.shape, jnp.bfloat16),
            pltpu.SemaphoreType.DMA((5, max(4, n_images))),
        ],
        input_output_aliases={} if before is None else {n_front + k: k for k in range(4)},
        compiler_params=pltpu.CompilerParams(vmem_limit_bytes=58 * 1024 * 1024),
        cost_estimate=pl.CostEstimate(
            flops=4 * (cols + strip) * rows * n_images * spots,
            bytes_accessed=16 * (cols + strip) * rows,
            transcendentals=0,
        ),
    )(*operands)


def scale_kernel(mine_ref, theirs_ref, out_ref):
    rows = out_ref.shape[1] - LANES
    largest = mine_ref[:, rows:] + theirs_ref[:, rows:]
    exponent = jnp.floor(jnp.log2(jnp.maximum(largest, 1e-30))) - 14.0
    scale = jnp.exp2(-exponent)
    for at in range(0, rows, LANES):
        lanes = slice(at, at + LANES)
        out_ref[:, lanes] = (mine_ref[:, lanes] + theirs_ref[:, lanes]) * scale
    out_ref[:, rows:] = exponent


def scale_strips(mine, theirs):
    return pl.pallas_call(
        scale_kernel,
        out_shape=jax.ShapeDtypeStruct(mine.shape, jnp.float32),
        in_specs=[pl.BlockSpec(memory_space=pltpu.VMEM)] * 2,
        out_specs=pl.BlockSpec(memory_space=pltpu.VMEM),
        compiler_params=pltpu.CompilerParams(vmem_limit_bytes=4 * 1024 * 1024),
    )(mine, theirs)


def tail_kernel(strip, block, layers, *refs):
    a_any, g_any = refs[:2]
    strip_refs, (away_ref, kept_ref) = refs[2:-8], refs[-8:-6]
    a_tile, g_whole, columns, inverse, away_vmem, sems = refs[-6:]
    channels = g_any.shape[0]
    n_fsdp, n_factor = lax.axis_size("fsdp"), lax.axis_size("factor")
    fsdp_at, factor_at = lax.axis_index("fsdp"), lax.axis_index("factor")
    core_at, pair_at = factor_at % 2, factor_at // 2
    copies = fetch([a_any, g_any], [a_tile, g_whole], sems.at[0])
    strip_copies = fetch(
        strip_refs,
        [columns.at[pl.ds(at * strip, strip)] for at in range(len(strip_refs))],
        sems.at[1],
    )
    copies[1].wait()
    for at, (layer, other) in enumerate(layers):
        owner = (fsdp_at + n_fsdp - 2 * layer) % n_fsdp
        owner = owner + other * (1 - 2 * (owner % 2))
        rows = pl.ds(pl.multiple_of(owner * strip, strip), strip)
        for to in range(n_factor):
            away, step = 1 - to // (n_factor // 2), to % (n_factor // 2)
            place = 2 * ((pair_at + step) % (n_factor // 2)) + (core_at + away) % 2
            lanes = pl.ds(pl.multiple_of(place * block, block), block)
            inverse[at * strip : (at + 1) * strip, to * block : (to + 1) * block] = g_whole[rows, lanes]
    copies[0].wait()
    for copy in strip_copies:
        copy.wait()
    first = lax.dot_general(
        a_tile[...],
        columns[...],
        (((1,), (1,)), ((), ())),
        precision=lax.Precision.HIGH,
        preferred_element_type=jnp.float32,
    )
    away_vmem[...] = jnp.dot(
        first,
        inverse[:, : channels // 2],
        precision=lax.Precision.HIGH,
        preferred_element_type=jnp.float32,
    )
    away_out = fetch([away_vmem], [away_ref], sems.at[2])
    kept_ref[...] = jnp.dot(
        first,
        inverse[:, channels // 2 :],
        precision=lax.Precision.HIGH,
        preferred_element_type=jnp.float32,
    )
    away_out[0].wait()


def tail_products(a_inverse, g_inverse, strips, layers, block):
    channels, strip = g_inverse.shape[0], strips[0].shape[0]
    rows, depth = a_inverse.shape
    half = (rows, channels // 2)
    return pl.pallas_call(
        lambda *refs: tail_kernel(strip, block, layers, *refs),
        out_shape=[jax.ShapeDtypeStruct(half, jnp.float32)] * 2,
        in_specs=[pl.BlockSpec(memory_space=pl.ANY)] * (2 + len(strips)),
        out_specs=[pl.BlockSpec(memory_space=pl.ANY), pl.BlockSpec(memory_space=pltpu.VMEM)],
        scratch_shapes=[
            pltpu.VMEM((rows, depth), jnp.float32),
            pltpu.VMEM((channels, channels), jnp.float32),
            pltpu.VMEM((channels, depth), jnp.float32),
            pltpu.VMEM((channels, channels), jnp.float32),
            pltpu.VMEM(half, jnp.float32),
            pltpu.SemaphoreType.DMA((3, max(2, len(strips)))),
        ],
        compiler_params=pltpu.CompilerParams(vmem_limit_bytes=26 * 1024 * 1024),
        cost_estimate=pl.CostEstimate(
            flops=6 * rows * channels * (depth + channels),
            bytes_accessed=4 * rows * (depth + channels),
            transcendentals=0,
        ),
    )(a_inverse, g_inverse, *strips)


def conv_kernel(n_images, *refs):
    image_refs, part_refs = refs[:n_images], refs[n_images : n_images + 2]
    out_refs, (shifted, parts, weight, sems) = refs[n_images + 2 : -4], refs[-4:]
    side, channels = image_refs[0].shape[1], image_refs[0].shape[3]
    n_near, depth, block = part_refs[0].shape
    fsdp_at = lax.axis_index("fsdp")
    arrivals = fetch(
        [ref.at[0] for ref in image_refs],
        [shifted.at[1, at, pl.ds(1, side)] for at in range(n_images)],
        sems.at[0],
    )
    part_copies = fetch(part_refs, [parts.at[at] for at in range(2)], sems.at[1])
    fill_shifted(shifted, arrivals)
    for copy in part_copies:
        copy.wait()
    for near in range(n_near):
        for far in range(2):
            owner = (fsdp_at ^ (2 * near + far)) * depth
            weight[pl.ds(pl.multiple_of(owner, 64), depth), :] = parts[far, near]
    for at, ref in enumerate(out_refs):
        total = jnp.zeros((side * side, block), jnp.float32)
        for tap in range(9):
            left = shifted[tap % 3, at, tap // 3 : tap // 3 + side].reshape(side * side, channels)
            total += jnp.dot(
                left,
                weight[tap * channels : (tap + 1) * channels, :],
                preferred_element_type=jnp.float32,
            )
        ref[0] = total.astype(jnp.bfloat16).reshape(side, side, block)


def convolve(images, near_parts, far_parts):
    n_images, (_, side, _, channels) = len(images), images[0].shape
    block = near_parts.shape[2]
    return pl.pallas_call(
        lambda *refs: conv_kernel(n_images, *refs),
        out_shape=[jax.ShapeDtypeStruct((1, side, side, block), jnp.bfloat16)] * n_images,
        in_specs=[pl.BlockSpec(memory_space=pl.ANY)] * (n_images + 2),
        out_specs=[pl.BlockSpec(memory_space=pltpu.VMEM)] * n_images,
        scratch_shapes=[
            pltpu.VMEM((3, n_images, side + 2, side, channels), jnp.bfloat16),
            pltpu.VMEM((2,) + near_parts.shape, jnp.bfloat16),
            pltpu.VMEM((9 * channels, block), jnp.bfloat16),
            pltpu.SemaphoreType.DMA((2, n_images)),
        ],
        compiler_params=pltpu.CompilerParams(vmem_limit_bytes=58 * 1024 * 1024),
        cost_estimate=pl.CostEstimate(
            flops=36 * n_images * side * side * channels * block,
            bytes_accessed=2 * (9 * channels * block + n_images * side * side * channels),
            transcendentals=0,
        ),
    )(*images, near_parts, far_parts)


def side_by_side_kernel(*refs):
    block, n_factor = refs[0].shape[3], lax.axis_size("factor")
    factor_at, n_pair = lax.axis_index("factor"), n_factor // 2
    for at, ref in enumerate(refs[:-1]):
        place = 2 * ((factor_at // 2 + at % n_pair) % n_pair) + (factor_at + at // n_pair) % 2
        refs[-1][:, :, :, pl.ds(pl.multiple_of(place * block, LANES), block)] = ref[...]


def side_by_side(blocks):
    whole = pl.BlockSpec(memory_space=pltpu.VMEM)
    shape = blocks[0].shape[:3] + (len(blocks) * blocks[0].shape[3],)
    return pl.pallas_call(
        side_by_side_kernel,
        out_shape=jax.ShapeDtypeStruct(shape, blocks[0].dtype),
        in_specs=[whole] * len(blocks),
        out_specs=whole,
        compiler_params=pltpu.CompilerParams(vmem_limit_bytes=4 * 1024 * 1024),
    )(*blocks)


def gather_plan(n_layer, n_pair):
    far_layers = sorted(range(1, n_layer), key=lambda step: min(step, n_layer - step))
    waiting = {"layer": [(("layer", layer, 0), None) for layer in far_layers], "side": [], "pair": []}
    for turn, layer in enumerate([0] + far_layers):
        waiting["side"].append((("side", layer, 0), ("layer", layer, 0)))
        for pair in range(1, n_pair):
            waiting["pair"].append((("pair", layer, pair), ("layer", layer, 0)))
            if turn % 2 == 0:
                waiting["pair"].append((("both", layer, pair), ("side", layer, 0)))
            else:
                waiting["side"].append((("both", layer, pair), ("pair", layer, pair)))
    for link in waiting.values():
        link.sort(key=lambda entry: entry[0][0] == "both")
    ready, busy, turns = {None: 0, ("layer", 0, 0): 0}, {link: 0 for link in waiting}, {}
    order, step = [], 0
    while any(waiting.values()):
        for link, entries in waiting.items():
            free = [entry for entry in entries if ready.get(entry[1], step + 1) <= step]
            if busy[link] > step or not free:
                continue
            count = 2 if link == "layer" and step == 0 else 1
            for item, source in free[:count]:
                entries.remove((item, source))
                hops = min(item[1], n_layer - item[1]) if link == "layer" else 1
                busy[link] = step + hops * count
                ready[item] = busy[link]
                turns[link] = turns.get(link, -1) + 1
                order.append((item, source, link, turns[link]))
        step += 1
    return order, ready


def per_device(activations, cotangent, weight, a_factor_old, g_factor_old, a_inverse, g_inverse):
    channels = activations.shape[3]
    n_fsdp, n_factor = lax.axis_size("fsdp"), lax.axis_size("factor")
    n_layer, n_pair = n_fsdp // 2, n_factor // 2
    fsdp_at, factor_at = lax.axis_index("fsdp"), lax.axis_index("factor")
    core_at, pair_at = factor_at % 2, factor_at // 2
    rows, cols = a_factor_old.shape
    strip = channels // n_fsdp
    block = channels // n_factor

    def over_layer(array, step):
        return moved(array, "fsdp", lambda at: at + 2 * step)

    def over_side(array):
        return moved(array, "fsdp", lambda at: at ^ 1)

    def over_pair(array, step):
        return moved(array, "factor", lambda at: at + 2 * step)

    def over_core(array):
        return moved(array, "factor", lambda at: at ^ 1)

    def after(arrays, events):
        return lax.optimization_barrier((arrays, events))[0]

    def transfer(array, item, how):
        if how == "layer":
            return over_layer(array, item[1])
        if how == "pair":
            return over_pair(array, item[2])
        return over_side(array)

    own_cot = cotangent.reshape(-1, channels)
    maps = {("layer", 0, 0): activations}
    plan, ready = gather_plan(n_layer, n_pair)
    images = sorted((item for item in ready if item), key=lambda item: ready[item])
    half = len(images) // 2
    aligned = rows % LANES == 0 and channels % LANES == 0 and activations.shape[0] == 1

    def products(batch, totals):
        owners = [(layer, int(kind in ("side", "both")), pair) for kind, layer, pair in batch]
        if aligned:
            arrays = [maps[item] for item in batch]
            return add_products(owners, arrays, strips, totals, cols, rows)
        for at in range(0, len(batch), 2 * n_pair):
            part = jnp.concatenate([maps[item] for item in batch[at : at + 2 * n_pair]], axis=0)
            col_tile = tile_of_patches(part, fsdp_at * cols, cols)
            cot_list = []
            for layer, other, pair in owners[at : at + 2 * n_pair]:
                owner = ((fsdp_at - 2 * layer) % n_fsdp ^ other) * n_pair + (pair_at - pair) % n_pair
                cot_list.append(lax.dynamic_index_in_dim(strips, owner, 0, keepdims=False))
            more = []
            for tile in (factor_at ^ 1, factor_at):
                row_tile = tile_of_patches(part, tile * rows, rows)
                more.append(by_rows(col_tile, row_tile))
                more.append(
                    jnp.dot(
                        jnp.concatenate(cot_list, axis=1),
                        row_tile,
                        preferred_element_type=jnp.float32,
                    )
                )
            totals = more if totals is None else [old + new for old, new in zip(totals, more)]
        return totals

    sent = {"layer": [], "side": [], "pair": []}
    for item, source, link, turn in plan:
        if item == plan[-1][0]:
            totals = products(images[:half], None)
            early = [totals[3]]
        array = activations if source is None else maps[source]
        events = [] if link == "layer" else sent[link][max(turn - 2, 0) : turn - 1]
        maps[item] = transfer(after(array, events + (early if item == plan[-1][0] else [])), item, link)
        sent[link].append(maps[item])
        if link == "side" and turn == 0:
            strips = after(own_cot, [maps[item]]).T.reshape(n_fsdp, 1, strip, own_cot.shape[0])
            strips = jnp.broadcast_to(strips, (n_fsdp, n_pair) + strips.shape[2:])
            groups = [
                [at * n_factor + 2 * pair + core for at in range(n_fsdp) for pair in range(n_pair)]
                for core in range(2)
            ]
            strips = lax.all_to_all(
                strips.reshape((n_fsdp * n_pair,) + strips.shape[2:]),
                ("fsdp", "factor"),
                split_axis=0,
                concat_axis=0,
                axis_index_groups=groups,
            )
    first_event, last_layer = sent["side"][:1], sent["layer"][-1:]
    near_end = sent["pair"][-2:-1]
    at_end = [maps[plan[-1][0]]] + sent["pair"][-1:]
    totals = list(products(images[half:], totals))
    if not aligned:
        for at in (1, 3):
            largest = jnp.full((strip, LANES), jnp.max(jnp.abs(totals[at])))
            totals[at] = jnp.concatenate([totals[at], largest], axis=1)

    g_partial = by_rows(after(own_cot, first_event), own_cot).reshape(n_pair, 2, block, channels)
    g_pairs = lax.dynamic_index_in_dim(g_partial, core_at, 1, keepdims=False) + over_core(
        lax.dynamic_index_in_dim(g_partial, 1 - core_at, 1, keepdims=False)
    )
    g_pairs = after(g_pairs, early)
    g_sum = lax.dynamic_index_in_dim(g_pairs, pair_at, 0, keepdims=False)
    for step in range(1, n_pair):
        away = lax.dynamic_index_in_dim(g_pairs, (pair_at + step) % n_pair, 0, keepdims=False)
        g_sum = g_sum + over_pair(away, step)
    weight_part = after(weight, last_layer)
    near_parts = [lax.dynamic_slice_in_dim(weight_part, factor_at * block, block, 1)]
    distance = 2
    while distance < n_fsdp:
        both = after(jnp.stack(near_parts), near_end if distance > 2 else [])
        both = moved(both, "fsdp", lambda to, d=distance: to ^ d)
        both = after(both, early) if distance > 2 else both
        near_parts = near_parts + [both[k] for k in range(len(near_parts))]
        distance *= 2
    near_stack = jnp.stack(near_parts)
    far_parts = over_side(after(near_stack, at_end))
    distance = n_fsdp // 2
    g_sum = after(g_sum, at_end)
    while distance > 2:
        g_sum = g_sum + moved(g_sum, "fsdp", lambda to, d=distance: to ^ d)
        distance //= 2
    near_images = [activations] + [maps["pair", 0, step] for step in range(1, n_pair)]
    group = near_images + [over_core(image) for image in after(near_images, near_end)]
    theirs = after(totals[1], [far_parts, g_sum] + group)
    theirs = over_core(theirs)
    pixel_total = float(
        activations.shape[0] * activations.shape[1] * activations.shape[2] * n_fsdp * n_factor
    )

    if aligned:
        packed = scale_strips(totals[3], theirs).astype(jnp.float16)
    else:
        largest = totals[3][:, rows : rows + 1] + theirs[:, rows : rows + 1]
        exponent = jnp.floor(jnp.log2(jnp.maximum(largest, 1e-30))) - 14.0
        packed = (totals[3] + theirs)[:, :rows] * jnp.exp2(-exponent)
        exponent = jnp.broadcast_to(exponent, (strip, LANES))
        packed = jnp.concatenate([packed, exponent], axis=1).astype(jnp.float16)
    near_packed = [packed] + [over_layer(packed, step) for step in range(1, n_layer)]

    g_sum = g_sum + over_side(g_sum)
    group = after(group, near_packed[n_layer - 1 :] + [g_sum])
    if aligned and block % LANES == 0:
        group_out = convolve(group, near_stack, far_parts)
    else:
        kernel = jnp.stack([part for pair in zip(near_stack, far_parts) for part in pair])
        kernel = jnp.concatenate(
            [
                lax.dynamic_index_in_dim(kernel, fsdp_at ^ at, 0, keepdims=False)
                for at in range(n_fsdp)
            ]
        ).reshape(3, 3, channels, block)
        group_out = lax.conv_general_dilated(
            jnp.concatenate(group),
            kernel,
            (1, 1),
            "SAME",
            dimension_numbers=("NHWC", "HWIO", "NHWC"),
            preferred_element_type=jnp.float32,
        ).astype(jnp.bfloat16)
        group_out = jnp.split(group_out, n_factor)
    own_maps, block_order = [], []
    for other in range(2):
        for pair in range(n_pair):
            out = group_out[other * n_pair + pair]
            if pair + other:
                out = moved(out, "factor", lambda at, o=other, p=pair: (at ^ o) - 2 * p)
            own_maps.append(out)
            block_order.append(2 * ((pair_at + pair) % n_pair) + (core_at + other) % 2)

    far_packed, came = {0: over_side(packed)}, []
    for step in sorted(range(1, n_layer), key=lambda step: min(step, n_layer - step)):
        if step == n_layer // 2:
            came = came + list(group_out)
        far_packed[step] = over_side(after(near_packed[step], came))
        came = came + [near_packed[step]]
    far_packed = [far_packed[step] for step in range(n_layer)]
    g_sum = after(g_sum, near_packed)
    g_sum = g_sum + moved(g_sum, "fsdp", lambda to: to ^ 2)
    strips_of_grad = [
        array[:, :rows].astype(jnp.float32) * jnp.exp2(array[:, rows : rows + 1].astype(jnp.float32))
        for array in near_packed + far_packed
    ]
    came_from = [(fsdp_at - 2 * step) % n_fsdp for step in range(n_layer)]
    came_from = came_from + [at ^ 1 for at in came_from]
    order = [
        2 * ((pair_at + step) % n_pair) + (core_at + other) % 2
        for other in (1, 0)
        for step in range(n_pair)
    ]
    if aligned and block % LANES == 0:
        away, kept = tail_products(
            after(a_inverse, [*group_out, g_sum]),
            g_inverse,
            strips_of_grad,
            [(step, other) for other in range(2) for step in range(n_layer)],
            block,
        )
    else:
        inverse = jnp.concatenate(
            [lax.dynamic_slice_in_dim(g_inverse, at * block, block, 1) for at in order], axis=1
        )
        inverse = jnp.concatenate(
            [lax.dynamic_slice_in_dim(inverse, at * strip, strip, 0) for at in came_from]
        )
        partial = lax.dot_general(
            a_inverse,
            jnp.concatenate(strips_of_grad),
            (((1,), (1,)), ((), ())),
            precision=lax.Precision.HIGH,
            preferred_element_type=jnp.float32,
        )
        partial = jnp.dot(
            partial, inverse, precision=lax.Precision.HIGH, preferred_element_type=jnp.float32
        )
        away, kept = partial[:, : channels // 2], partial[:, channels // 2 :]
    by_pair = kept + over_core(away)
    cov_own = totals[2] + after(over_core(after(totals[0], far_packed)), by_pair)
    a_factor = 0.5 * a_factor_old + (0.5 / pixel_total) * cov_own.T
    result = by_pair[:, :block]
    for step in range(1, n_pair):
        back = over_pair(by_pair[:, step * block : (step + 1) * block], step)
        result = result + after(back, a_factor)
    natural_grad = result.astype(jnp.bfloat16)


    own_maps = after(own_maps, by_pair)
    if aligned and block % LANES == 0:
        conv_out = side_by_side(own_maps)
    else:
        stacked = jnp.zeros((n_factor,) + own_maps[0].shape, jnp.bfloat16)
        for at, out in zip(block_order, own_maps):
            stacked = lax.dynamic_update_index_in_dim(stacked, out, at, 0)
        conv_out = jnp.concatenate(jnp.split(stacked, n_factor), axis=4)[0]

    g_factor = 0.5 * g_factor_old + 0.5 * g_sum
    return (conv_out, a_factor, g_factor, natural_grad)


def solution(mesh):
    images = P(("fsdp", "factor"), None, None, None)
    return jax.shard_map(
        per_device,
        mesh=mesh,
        in_specs=(
            images,
            images,
            P("fsdp", None),
            P("factor", "fsdp"),
            P("factor", None),
            P("fsdp", "factor"),
            P(),
        ),
        out_specs=(
            images,
            P("factor", "fsdp"),
            P("factor", None),
            P("fsdp", "factor"),
        ),
        check_vma=False,
    )
```

```python
import jax
import jax.numpy as jnp
from jax import lax
from jax.experimental import pallas as pl
from jax.experimental.pallas import tpu as pltpu
from jax.sharding import PartitionSpec as P

LANES = 128


def by_rows(first_op, second_op):
    return lax.dot_general(
        first_op, second_op, (((0,), (0,)), ((), ())), preferred_element_type=jnp.float32
    )


def moved(array, axis, target):
    count = lax.axis_size(axis)
    return lax.ppermute(array, axis, [(at, target(at) % count) for at in range(count)])


def tile_of_patches(images, start, width):
    side, channels = images.shape[1], images.shape[3]
    padded = jnp.pad(images, ((0, 0), (1, 1), (1, 1), (0, 0)))
    first_tap, offset = start // channels, start % channels
    rolled = lax.dynamic_slice_in_dim(
        jnp.concatenate([padded, padded], axis=3), offset, channels, 3
    )
    lane = lax.broadcasted_iota(jnp.int32, (1, 1, 1, channels), 3)

    def tap(index):
        index = jnp.minimum(index, 8)
        return lax.dynamic_slice(
            rolled, (0, index // 3, index % 3, 0), (images.shape[0], side, side, channels)
        )

    pieces = []
    for at in range(0, width, channels):
        step = at // channels
        piece = jnp.where(lane < channels - offset, tap(first_tap + step), tap(first_tap + step + 1))
        pieces.append(piece[..., : min(channels, width - at)])
    return jnp.concatenate(pieces, axis=3).reshape(-1, width)


def fill_shifted(shifted, arrivals):
    n_images, tall, side, channels = shifted.shape[1:]
    spots = side * side
    spot = lax.broadcasted_iota(jnp.int32, (spots, LANES), 0) % side
    empty = jnp.zeros((side, channels), jnp.bfloat16)
    for at in range(n_images):
        for col_off in range(3):
            shifted[col_off, at, 0] = empty
            shifted[col_off, at, tall - 1] = empty
    for at, arrival in enumerate(arrivals):
        arrival.wait()
        for lane in range(0, channels, LANES):
            part = shifted[1, at, 1 : side + 1, :, lane : lane + LANES]
            part = part.reshape(spots, LANES).astype(jnp.float32)
            before_it = jnp.where(spot == 0, 0.0, pltpu.roll(part, 1, 0))
            after_it = jnp.where(spot == side - 1, 0.0, pltpu.roll(part, spots - 1, 0))
            for col_off, moved_part in ((0, before_it), (2, after_it)):
                shifted[col_off, at, 1 : side + 1, :, lane : lane + LANES] = moved_part.astype(
                    jnp.bfloat16
                ).reshape(side, side, LANES)


def fetch(sources, targets, sems):
    copies = [
        pltpu.make_async_copy(source, target, sems.at[at])
        for at, (source, target) in enumerate(zip(sources, targets))
    ]
    for copy in copies:
        copy.start()
    return copies


def products_kernel(owners, first, *refs):
    n_arrays = 1 + max(array for _, (array, _) in owners)
    image_refs = [refs[array].at[index] for _, (array, index) in owners]
    strips_ref, refs = refs[n_arrays], refs[n_arrays + 1 :]
    before, refs = (None, refs) if first else (refs[:4], refs[4:])
    out_refs, totals, (shifted, turned, left, strips, sems) = refs[:4], refs[4:8], refs[8:]
    n_images, side, channels = len(image_refs), image_refs[0].shape[0], image_refs[0].shape[2]
    spots = side * side
    cols, rows = totals[0].shape
    strip = totals[1].shape[0]
    n_fsdp, n_pair = lax.axis_size("fsdp"), lax.axis_size("factor") // 2
    fsdp_at, factor_at = lax.axis_index("fsdp"), lax.axis_index("factor")

    arrivals = fetch(
        image_refs, [shifted.at[1, at, pl.ds(1, side)] for at in range(n_images)], sems.at[0]
    )
    strip_copies = fetch([strips_ref], [strips], sems.at[1])
    if not first:
        total_copies = fetch(before, totals, sems.at[2])
    fill_shifted(shifted, arrivals)

    def lanes_of_tap(tap, lane):
        piece = shifted[tap % 3, :, pl.ds(tap // 3, side), :, pl.ds(pl.multiple_of(lane, LANES), LANES)]
        return piece.reshape(n_images * spots, LANES)

    start = fsdp_at * cols
    inside = start % LANES
    for at in range(0, turned.shape[0], LANES):
        lane = start - inside + at
        tap = jnp.minimum(lane // channels, 8)
        turned[at : at + LANES, :] = lanes_of_tap(tap, lane % channels).T
    left[:cols, :] = turned[pl.ds(pl.multiple_of(inside, strip), cols), :]
    for copy in strip_copies:
        copy.wait()
    for at, ((layer, other, pair), _) in enumerate(owners):
        owner = (fsdp_at + n_fsdp - 2 * layer) % n_fsdp
        owner = owner + other * (1 - 2 * (owner % 2))
        owner = owner * n_pair + (factor_at // 2 + n_pair - pair) % n_pair
        left[cols : cols + strip, at * spots : (at + 1) * spots] = strips[owner]
    if not first:
        for copy in total_copies:
            copy.wait()

    tiles_per = rows // LANES
    other_tile = factor_at + 1 - 2 * (factor_at % 2)

    def lanes_at(index):
        whose = jnp.where(index >= tiles_per, 1, 0)
        tile = jnp.where(index >= tiles_per, factor_at, other_tile)
        start = (tile * tiles_per + index - whose * tiles_per) * LANES
        return lanes_of_tap(start // channels, start % channels)

    def product(first_index, count):
        right = jnp.concatenate([lanes_at(first_index + k) for k in range(count)], axis=1)
        return jnp.dot(left[...], right, preferred_element_type=jnp.float32)

    def keep(whose, lane, count, value):
        at = slice(lane, lane + count * LANES)
        for kind, part in ((0, value[:cols]), (1, value[cols:])):
            if not first:
                part = part + totals[2 * whose + kind][:, at]
            totals[2 * whose + kind][:, at] = part
        grads = totals[2 * whose + 1]
        grads[:, rows:] = jnp.full((strip, LANES), jnp.max(jnp.abs(grads[:, :rows])))

    keep(0, 0, tiles_per, product(0, tiles_per))
    theirs_out = fetch(totals[:2], out_refs[:2], sems.at[3])
    keep(1, 0, tiles_per, product(tiles_per, tiles_per))
    mine_out = fetch(totals[2:], out_refs[2:], sems.at[4])
    for copy in theirs_out + mine_out:
        copy.wait()


def add_products(owners, arrays, strips, before, cols, rows):
    n_images, strip = len(owners), strips.shape[1]
    side, channels = arrays[0].shape[1], arrays[0].shape[3]
    spots = side * side
    shapes = [(cols, rows), (strip, rows + LANES)] * 2
    operands = [*arrays, strips, *(before or [])]
    n_front = len(arrays) + 1
    return pl.pallas_call(
        lambda *refs: products_kernel(owners, before is None, *refs),
        out_shape=[jax.ShapeDtypeStruct(shape, jnp.float32) for shape in shapes],
        in_specs=[pl.BlockSpec(memory_space=pl.ANY)] * len(operands),
        out_specs=[pl.BlockSpec(memory_space=pl.ANY)] * 4,
        scratch_shapes=[pltpu.VMEM(shape, jnp.float32) for shape in shapes]
        + [
            pltpu.VMEM((3, n_images, side + 2, side, channels), jnp.bfloat16),
            pltpu.VMEM(((cols + strip + LANES - 1) // LANES * LANES, n_images * spots), jnp.bfloat16),
            pltpu.VMEM((cols + strip, n_images * spots), jnp.bfloat16),
            pltpu.VMEM(strips.shape, jnp.bfloat16),
            pltpu.SemaphoreType.DMA((5, max(4, n_images))),
        ],
        input_output_aliases={} if before is None else {n_front + k: k for k in range(4)},
        compiler_params=pltpu.CompilerParams(vmem_limit_bytes=58 * 1024 * 1024),
        cost_estimate=pl.CostEstimate(
            flops=4 * (cols + strip) * rows * n_images * spots,
            bytes_accessed=16 * (cols + strip) * rows,
            transcendentals=0,
        ),
    )(*operands)


def scale_kernel(mine_ref, theirs_ref, out_ref):
    rows = out_ref.shape[1] - LANES
    largest = mine_ref[:, rows:] + theirs_ref[:, rows:]
    exponent = jnp.floor(jnp.log2(jnp.maximum(largest, 1e-30))) - 14.0
    scale = jnp.exp2(-exponent)
    for at in range(0, rows, LANES):
        lanes = slice(at, at + LANES)
        out_ref[:, lanes] = (mine_ref[:, lanes] + theirs_ref[:, lanes]) * scale
    out_ref[:, rows:] = exponent


def scale_strips(mine, theirs):
    return pl.pallas_call(
        scale_kernel,
        out_shape=jax.ShapeDtypeStruct(mine.shape, jnp.float32),
        in_specs=[pl.BlockSpec(memory_space=pltpu.VMEM)] * 2,
        out_specs=pl.BlockSpec(memory_space=pltpu.VMEM),
        compiler_params=pltpu.CompilerParams(vmem_limit_bytes=4 * 1024 * 1024),
    )(mine, theirs)


def tail_kernel(strip, block, layers, *refs):
    a_any, g_any = refs[:2]
    strip_refs, (away_ref, kept_ref) = refs[2:-8], refs[-8:-6]
    a_tile, g_whole, columns, inverse, away_vmem, sems = refs[-6:]
    channels = g_any.shape[0]
    n_fsdp, n_factor = lax.axis_size("fsdp"), lax.axis_size("factor")
    fsdp_at, factor_at = lax.axis_index("fsdp"), lax.axis_index("factor")
    core_at, pair_at = factor_at % 2, factor_at // 2
    copies = fetch([a_any, g_any], [a_tile, g_whole], sems.at[0])
    strip_copies = fetch(
        strip_refs,
        [columns.at[pl.ds(at * strip, strip)] for at in range(len(strip_refs))],
        sems.at[1],
    )
    copies[1].wait()
    for at, (layer, other) in enumerate(layers):
        owner = (fsdp_at + n_fsdp - 2 * layer) % n_fsdp
        owner = owner + other * (1 - 2 * (owner % 2))
        rows = pl.ds(pl.multiple_of(owner * strip, strip), strip)
        for to in range(n_factor):
            away, step = 1 - to // (n_factor // 2), to % (n_factor // 2)
            place = 2 * ((pair_at + step) % (n_factor // 2)) + (core_at + away) % 2
            lanes = pl.ds(pl.multiple_of(place * block, block), block)
            inverse[at * strip : (at + 1) * strip, to * block : (to + 1) * block] = g_whole[rows, lanes]
    copies[0].wait()
    for copy in strip_copies:
        copy.wait()
    first = lax.dot_general(
        a_tile[...],
        columns[...],
        (((1,), (1,)), ((), ())),
        precision=lax.Precision.HIGH,
        preferred_element_type=jnp.float32,
    )
    away_vmem[...] = jnp.dot(
        first,
        inverse[:, : channels // 2],
        precision=lax.Precision.HIGH,
        preferred_element_type=jnp.float32,
    )
    away_out = fetch([away_vmem], [away_ref], sems.at[2])
    kept_ref[...] = jnp.dot(
        first,
        inverse[:, channels // 2 :],
        precision=lax.Precision.HIGH,
        preferred_element_type=jnp.float32,
    )
    away_out[0].wait()


def tail_products(a_inverse, g_inverse, strips, layers, block):
    channels, strip = g_inverse.shape[0], strips[0].shape[0]
    rows, depth = a_inverse.shape
    half = (rows, channels // 2)
    return pl.pallas_call(
        lambda *refs: tail_kernel(strip, block, layers, *refs),
        out_shape=[jax.ShapeDtypeStruct(half, jnp.float32)] * 2,
        in_specs=[pl.BlockSpec(memory_space=pl.ANY)] * (2 + len(strips)),
        out_specs=[pl.BlockSpec(memory_space=pl.ANY), pl.BlockSpec(memory_space=pltpu.VMEM)],
        scratch_shapes=[
            pltpu.VMEM((rows, depth), jnp.float32),
            pltpu.VMEM((channels, channels), jnp.float32),
            pltpu.VMEM((channels, depth), jnp.float32),
            pltpu.VMEM((channels, channels), jnp.float32),
            pltpu.VMEM(half, jnp.float32),
            pltpu.SemaphoreType.DMA((3, max(2, len(strips)))),
        ],
        compiler_params=pltpu.CompilerParams(vmem_limit_bytes=26 * 1024 * 1024),
        cost_estimate=pl.CostEstimate(
            flops=6 * rows * channels * (depth + channels),
            bytes_accessed=4 * rows * (depth + channels),
            transcendentals=0,
        ),
    )(a_inverse, g_inverse, *strips)


def conv_kernel(n_images, *refs):
    image_refs, part_refs = refs[:n_images], refs[n_images : n_images + 2]
    out_refs, (shifted, parts, weight, sems) = refs[n_images + 2 : -4], refs[-4:]
    side, channels = image_refs[0].shape[1], image_refs[0].shape[3]
    n_near, depth, block = part_refs[0].shape
    fsdp_at = lax.axis_index("fsdp")
    arrivals = fetch(
        [ref.at[0] for ref in image_refs],
        [shifted.at[1, at, pl.ds(1, side)] for at in range(n_images)],
        sems.at[0],
    )
    part_copies = fetch(part_refs, [parts.at[at] for at in range(2)], sems.at[1])
    fill_shifted(shifted, arrivals)
    for copy in part_copies:
        copy.wait()
    for near in range(n_near):
        for far in range(2):
            owner = (fsdp_at ^ (2 * near + far)) * depth
            weight[pl.ds(pl.multiple_of(owner, 64), depth), :] = parts[far, near]
    for at in range(n_images):
        total = jnp.zeros((side * side, block), jnp.float32)
        for tap in range(9):
            left = shifted[tap % 3, at, tap // 3 : tap // 3 + side].reshape(side * side, channels)
            total += jnp.dot(
                left,
                weight[tap * channels : (tap + 1) * channels, :],
                preferred_element_type=jnp.float32,
            )
        half = n_images // 2
        out_refs[at // half][at % half] = total.astype(jnp.bfloat16).reshape(side, side, block)


def convolve(images, near_parts, far_parts):
    n_images, (_, side, _, channels) = len(images), images[0].shape
    block = near_parts.shape[2]
    return pl.pallas_call(
        lambda *refs: conv_kernel(n_images, *refs),
        out_shape=[jax.ShapeDtypeStruct((n_images // 2, side, side, block), jnp.bfloat16)] * 2,
        in_specs=[pl.BlockSpec(memory_space=pl.ANY)] * (n_images + 2),
        out_specs=[pl.BlockSpec(memory_space=pltpu.VMEM)] * 2,
        scratch_shapes=[
            pltpu.VMEM((3, n_images, side + 2, side, channels), jnp.bfloat16),
            pltpu.VMEM((2,) + near_parts.shape, jnp.bfloat16),
            pltpu.VMEM((9 * channels, block), jnp.bfloat16),
            pltpu.SemaphoreType.DMA((2, n_images)),
        ],
        compiler_params=pltpu.CompilerParams(vmem_limit_bytes=58 * 1024 * 1024),
        cost_estimate=pl.CostEstimate(
            flops=36 * n_images * side * side * channels * block,
            bytes_accessed=2 * (9 * channels * block + n_images * side * side * channels),
            transcendentals=0,
        ),
    )(*images, near_parts, far_parts)


def side_by_side_kernel(*refs):
    block, n_factor = refs[0].shape[3], lax.axis_size("factor")
    factor_at, n_pair = lax.axis_index("factor"), n_factor // 2
    for step, ref in enumerate(refs[:-1]):
        for other in range(2):
            place = 2 * ((factor_at // 2 + step) % n_pair) + (factor_at + other) % 2
            lanes = pl.ds(pl.multiple_of(place * block, LANES), block)
            refs[-1][0, :, :, lanes] = ref[other]


def side_by_side(blocks):
    whole = pl.BlockSpec(memory_space=pltpu.VMEM)
    shape = (1,) + blocks[0].shape[1:3] + (2 * len(blocks) * blocks[0].shape[3],)
    return pl.pallas_call(
        side_by_side_kernel,
        out_shape=jax.ShapeDtypeStruct(shape, blocks[0].dtype),
        in_specs=[whole] * len(blocks),
        out_specs=whole,
        compiler_params=pltpu.CompilerParams(vmem_limit_bytes=4 * 1024 * 1024),
    )(*blocks)


def per_device(activations, cotangent, weight, a_factor_old, g_factor_old, a_inverse, g_inverse):
    channels = activations.shape[3]
    n_fsdp, n_factor = lax.axis_size("fsdp"), lax.axis_size("factor")
    n_layer, n_pair = n_fsdp // 2, n_factor // 2
    fsdp_at, factor_at = lax.axis_index("fsdp"), lax.axis_index("factor")
    core_at, pair_at = factor_at % 2, factor_at // 2
    rows, cols = a_factor_old.shape
    strip = channels // n_fsdp
    block = channels // n_factor

    def over_layer(array, step):
        return moved(array, "fsdp", lambda at: at + 2 * step)

    def over_side(array):
        return moved(array, "fsdp", lambda at: at ^ 1)

    def over_pair(array, step):
        return moved(array, "factor", lambda at: at + 2 * step)

    def over_core(array):
        return moved(array, "factor", lambda at: at ^ 1)

    def after(arrays, events):
        return lax.optimization_barrier((arrays, events))[0]

    own_cot = cotangent.reshape(-1, channels)
    aligned = rows % LANES == 0 and channels % LANES == 0 and activations.shape[0] == 1
    far_layers = sorted(range(1, n_layer), key=lambda step: min(step, n_layer - step))
    pair_steps = range(1, n_pair)
    arrays, what = {"own": activations}, {"own": [(0, 0, 0)]}

    def add(name, array, whose):
        arrays[name], what[name] = array, whose

    add("side", over_side(activations), [(0, 1, 0)])
    for step in pair_steps:
        add(f"pair{step}", over_pair(activations, step), [(0, 0, step)])
    for layer in far_layers[:2]:
        add(f"layer{layer}", over_layer(activations, layer), [(layer, 0, 0)])
    for step in pair_steps:
        add(f"both{step}", over_pair(arrays["side"], step), [(0, 1, step)])
    for layer in far_layers[2:]:
        source = after(activations, [arrays[f"both{step}"] for step in pair_steps])
        add(f"layer{layer}", over_layer(source, layer), [(layer, 0, 0)])

    strips = after(own_cot, [arrays["side"]]).T.reshape(n_fsdp, 1, strip, own_cot.shape[0])
    strips = jnp.broadcast_to(strips, (n_fsdp, n_pair) + strips.shape[2:])
    groups = [
        [at * n_factor + 2 * pair + core for at in range(n_fsdp) for pair in range(n_pair)]
        for core in range(2)
    ]
    strips = lax.all_to_all(
        strips.reshape((n_fsdp * n_pair,) + strips.shape[2:]),
        ("fsdp", "factor"),
        split_axis=0,
        concat_axis=0,
        axis_index_groups=groups,
    )
    first_names = list(arrays)

    stacked = jnp.concatenate([arrays[f"layer{layer}"] for layer in far_layers])
    stacked = after(stacked, strips)
    add("far_side", over_side(stacked), [(layer, 1, 0) for layer in far_layers])
    for step in pair_steps:
        add(f"far_pair{step}", over_pair(stacked, step), [(layer, 0, step) for layer in far_layers])
    second_names = [name for name in arrays if name not in first_names]
    cut = (2 * len(far_layers) + 1) // 3
    for step in pair_steps:
        by_side = over_side(arrays[f"far_pair{step}"][:cut])
        by_pair = over_pair(arrays["far_side"][cut:], step)
        add(f"far_both_side{step}", by_side, [(layer, 1, step) for layer in far_layers[:cut]])
        add(f"far_both_pair{step}", by_pair, [(layer, 1, step) for layer in far_layers[cut:]])
    third_names = [name for name in arrays if name not in first_names + second_names]

    def products(names, totals, events):
        own_strips = after(strips, events)
        owners = [
            (whose, (at, index))
            for at, name in enumerate(names)
            for index, whose in enumerate(what[name])
        ]
        batch = [arrays[name] for name in names]
        if aligned:
            return add_products(owners, batch, own_strips, totals, cols, rows)
        batch = [array[index : index + 1] for array in batch for index in range(array.shape[0])]
        owners = [whose for whose, _ in owners]
        for at in range(0, len(batch), 2 * n_pair):
            part = jnp.concatenate(batch[at : at + 2 * n_pair], axis=0)
            col_tile = tile_of_patches(part, fsdp_at * cols, cols)
            cot_list = []
            for layer, other, pair in owners[at : at + 2 * n_pair]:
                owner = ((fsdp_at - 2 * layer) % n_fsdp ^ other) * n_pair + (pair_at - pair) % n_pair
                cot_list.append(lax.dynamic_index_in_dim(own_strips, owner, 0, keepdims=False))
            more = []
            for tile in (factor_at ^ 1, factor_at):
                row_tile = tile_of_patches(part, tile * rows, rows)
                more.append(by_rows(col_tile, row_tile))
                more.append(
                    jnp.dot(
                        jnp.concatenate(cot_list, axis=1),
                        row_tile,
                        preferred_element_type=jnp.float32,
                    )
                )
            totals = more if totals is None else [old + new for old, new in zip(totals, more)]
        return totals

    layer_end = [arrays[f"layer{layer}"] for layer in far_layers]
    weight_part = after(weight, layer_end)
    near_parts = [lax.dynamic_slice_in_dim(weight_part, factor_at * block, block, 1)]
    distance = 2
    while distance < n_fsdp:
        both = moved(jnp.stack(near_parts), "fsdp", lambda to, d=distance: to ^ d)
        near_parts = near_parts + [both[k] for k in range(len(near_parts))]
        distance *= 2

    g_partial = by_rows(after(own_cot, layer_end), own_cot).reshape(n_pair, 2, block, channels)
    g_pairs = lax.dynamic_index_in_dim(g_partial, core_at, 1, keepdims=False) + over_core(
        lax.dynamic_index_in_dim(g_partial, 1 - core_at, 1, keepdims=False)
    )
    totals = products(first_names, None, [])
    early = [totals[3]]
    g_pairs = after(g_pairs, early)
    g_sum = lax.dynamic_index_in_dim(g_pairs, pair_at, 0, keepdims=False)
    for step in pair_steps:
        away = lax.dynamic_index_in_dim(g_pairs, (pair_at + step) % n_pair, 0, keepdims=False)
        g_sum = g_sum + over_pair(away, step)
    totals = products(second_names, totals, [g_sum, near_parts[-1]])
    middle = [totals[3]]
    distance = n_fsdp // 2
    while distance > 2:
        g_sum = g_sum + moved(g_sum, "fsdp", lambda to, d=distance: to ^ d)
        distance //= 2
    totals = list(products(third_names, totals, [g_sum]))
    if not aligned:
        for at in (1, 3):
            largest = jnp.full((strip, LANES), jnp.max(jnp.abs(totals[at])))
            totals[at] = jnp.concatenate([totals[at], largest], axis=1)

    near_stack = jnp.stack(near_parts)
    far_parts = over_side(after(near_stack, [arrays[name] for name in third_names] + middle))
    near_images = [activations] + [arrays[f"pair{step}"] for step in pair_steps]
    group = near_images + [over_core(image) for image in after(near_images, early)]
    theirs = after(totals[1], group)
    theirs = over_core(theirs)
    g_sum = g_sum + moved(g_sum, "fsdp", lambda to: to ^ 2)
    pixel_total = float(
        activations.shape[0] * activations.shape[1] * activations.shape[2] * n_fsdp * n_factor
    )

    if aligned:
        packed = scale_strips(totals[3], theirs).astype(jnp.float16)
    else:
        largest = totals[3][:, rows : rows + 1] + theirs[:, rows : rows + 1]
        exponent = jnp.floor(jnp.log2(jnp.maximum(largest, 1e-30))) - 14.0
        packed = (totals[3] + theirs)[:, :rows] * jnp.exp2(-exponent)
        exponent = jnp.broadcast_to(exponent, (strip, LANES))
        packed = jnp.concatenate([packed, exponent], axis=1).astype(jnp.float16)
    packed = after(packed, far_parts)
    near_packed = [packed] + [over_layer(packed, step) for step in range(1, n_layer)]

    far_packed, came = {0: over_side(packed)}, []
    for step in far_layers:
        far_packed[step] = over_side(after(near_packed[step], came))
        came = came + [near_packed[step]]
    far_packed = [far_packed[step] for step in range(n_layer)]
    group = after(group, [far_packed[far_layers[0]], g_sum])
    if aligned and block % LANES == 0:
        group_out = convolve(group, near_stack, far_parts)
    else:
        kernel = jnp.stack([part for pair in zip(near_stack, far_parts) for part in pair])
        kernel = jnp.concatenate(
            [
                lax.dynamic_index_in_dim(kernel, fsdp_at ^ at, 0, keepdims=False)
                for at in range(n_fsdp)
            ]
        ).reshape(3, 3, channels, block)
        group_out = lax.conv_general_dilated(
            jnp.concatenate(group),
            kernel,
            (1, 1),
            "SAME",
            dimension_numbers=("NHWC", "HWIO", "NHWC"),
            preferred_element_type=jnp.float32,
        ).astype(jnp.bfloat16)
        group_out = jnp.split(group_out, 2)
    swapped = over_core(group_out[1])
    own_maps, block_order = [], []
    images_each = activations.shape[0]
    for step in range(n_pair):
        places = slice(step * images_each, (step + 1) * images_each)
        both = jnp.concatenate([group_out[0][places], swapped[places]])
        own_maps.append(over_pair(both, n_pair - step) if step else both)
        block_order += [2 * ((pair_at + step) % n_pair) + (core_at + other) % 2 for other in range(2)]
    g_back = over_side(after(g_sum, far_packed))
    far_packed[far_layers[-1]] = after(far_packed[far_layers[-1]], group_out)
    strips_of_grad = [
        array[:, :rows].astype(jnp.float32) * jnp.exp2(array[:, rows : rows + 1].astype(jnp.float32))
        for array in near_packed + far_packed
    ]
    came_from = [(fsdp_at - 2 * step) % n_fsdp for step in range(n_layer)]
    came_from = came_from + [at ^ 1 for at in came_from]
    order = [
        2 * ((pair_at + step) % n_pair) + (core_at + other) % 2
        for other in (1, 0)
        for step in range(n_pair)
    ]
    if aligned and block % LANES == 0:
        away, kept = tail_products(
            after(a_inverse, own_maps),
            g_inverse,
            strips_of_grad,
            [(step, other) for other in range(2) for step in range(n_layer)],
            block,
        )
    else:
        inverse = jnp.concatenate(
            [lax.dynamic_slice_in_dim(g_inverse, at * block, block, 1) for at in order], axis=1
        )
        inverse = jnp.concatenate(
            [lax.dynamic_slice_in_dim(inverse, at * strip, strip, 0) for at in came_from]
        )
        partial = lax.dot_general(
            a_inverse,
            jnp.concatenate(strips_of_grad),
            (((1,), (1,)), ((), ())),
            precision=lax.Precision.HIGH,
            preferred_element_type=jnp.float32,
        )
        partial = jnp.dot(
            partial, inverse, precision=lax.Precision.HIGH, preferred_element_type=jnp.float32
        )
        away, kept = partial[:, : channels // 2], partial[:, channels // 2 :]
    by_pair = kept + over_core(away)
    cov_own = totals[2] + after(over_core(after(totals[0], far_packed)), by_pair)
    a_factor = 0.5 * a_factor_old + (0.5 / pixel_total) * cov_own.T
    result = by_pair[:, :block]
    for step in range(1, n_pair):
        back = over_pair(by_pair[:, step * block : (step + 1) * block], step)
        result = result + after(back, a_factor)
    natural_grad = result.astype(jnp.bfloat16)


    own_maps = after(own_maps, by_pair)
    if aligned and block % LANES == 0:
        conv_out = side_by_side(own_maps)
    else:
        stacked = jnp.zeros((n_factor,) + activations.shape[:3] + (block,), jnp.bfloat16)
        out_list = [out for both in own_maps for out in jnp.split(both, 2)]
        for at, out in zip(block_order, out_list):
            stacked = lax.dynamic_update_index_in_dim(stacked, out, at, 0)
        conv_out = jnp.concatenate(jnp.split(stacked, n_factor), axis=4)[0]
    g_sum = g_sum + after(g_back, by_pair)
    g_factor = 0.5 * g_factor_old + 0.5 * g_sum
    return (conv_out, a_factor, g_factor, natural_grad)


def solution(mesh):
    images = P(("fsdp", "factor"), None, None, None)
    return jax.shard_map(
        per_device,
        mesh=mesh,
        in_specs=(
            images,
            images,
            P("fsdp", None),
            P("factor", "fsdp"),
            P("factor", None),
            P("fsdp", "factor"),
            P(),
        ),
        out_specs=(
            images,
            P("factor", "fsdp"),
            P("factor", None),
            P("fsdp", "factor"),
        ),
        check_vma=False,
    )
```

```python
import jax
import jax.numpy as jnp
from jax import lax
from jax.experimental import pallas as pl
from jax.experimental.pallas import tpu as pltpu
from jax.sharding import PartitionSpec as P

LANES = 128


def by_rows(first_op, second_op):
    return lax.dot_general(
        first_op, second_op, (((0,), (0,)), ((), ())), preferred_element_type=jnp.float32
    )


def moved(array, axis, target):
    count = lax.axis_size(axis)
    return lax.ppermute(array, axis, [(at, target(at) % count) for at in range(count)])


def tile_of_patches(images, start, width):
    side, channels = images.shape[1], images.shape[3]
    padded = jnp.pad(images, ((0, 0), (1, 1), (1, 1), (0, 0)))
    first_tap, offset = start // channels, start % channels
    rolled = lax.dynamic_slice_in_dim(
        jnp.concatenate([padded, padded], axis=3), offset, channels, 3
    )
    lane = lax.broadcasted_iota(jnp.int32, (1, 1, 1, channels), 3)

    def tap(index):
        index = jnp.minimum(index, 8)
        return lax.dynamic_slice(
            rolled, (0, index // 3, index % 3, 0), (images.shape[0], side, side, channels)
        )

    pieces = []
    for at in range(0, width, channels):
        step = at // channels
        piece = jnp.where(lane < channels - offset, tap(first_tap + step), tap(first_tap + step + 1))
        pieces.append(piece[..., : min(channels, width - at)])
    return jnp.concatenate(pieces, axis=3).reshape(-1, width)


def fill_shifted(shifted, arrivals):
    n_images, tall, side, channels = shifted.shape[1:]
    spots = side * side
    spot = lax.broadcasted_iota(jnp.int32, (spots, LANES), 0) % side
    empty = jnp.zeros((side, channels), jnp.bfloat16)
    for at in range(n_images):
        for col_off in range(3):
            shifted[col_off, at, 0] = empty
            shifted[col_off, at, tall - 1] = empty
    for at, arrival in enumerate(arrivals):
        arrival.wait()
        for lane in range(0, channels, LANES):
            part = shifted[1, at, 1 : side + 1, :, lane : lane + LANES]
            part = part.reshape(spots, LANES).astype(jnp.float32)
            before_it = jnp.where(spot == 0, 0.0, pltpu.roll(part, 1, 0))
            after_it = jnp.where(spot == side - 1, 0.0, pltpu.roll(part, spots - 1, 0))
            for col_off, moved_part in ((0, before_it), (2, after_it)):
                shifted[col_off, at, 1 : side + 1, :, lane : lane + LANES] = moved_part.astype(
                    jnp.bfloat16
                ).reshape(side, side, LANES)


def fetch(sources, targets, sems):
    copies = [
        pltpu.make_async_copy(source, target, sems.at[at])
        for at, (source, target) in enumerate(zip(sources, targets))
    ]
    for copy in copies:
        copy.start()
    return copies


def products_kernel(owners, pairs, n_pair, first, *refs):
    image_refs, strip_refs = refs[: len(pairs)], refs[len(pairs) : len(pairs) + n_pair]
    refs = refs[len(pairs) + n_pair :]
    before, refs = (None, refs) if first else (refs[:4], refs[4:])
    out_refs, totals, (shifted, turned, left, strips, sems) = refs[:4], refs[4:8], refs[8:]
    n_images, side, channels = len(image_refs), image_refs[0].shape[1], image_refs[0].shape[3]
    spots = side * side
    cols, rows = totals[0].shape
    strip = totals[1].shape[0]
    n_fsdp = strip_refs[0].shape[0]
    fsdp_at, factor_at = lax.axis_index("fsdp"), lax.axis_index("factor")

    arrivals = fetch(
        [ref.at[0] for ref in image_refs],
        [shifted.at[1, at, pl.ds(1, side)] for at in range(n_images)],
        sems.at[0],
    )
    strip_copies = fetch(strip_refs, [strips.at[at] for at in range(n_pair)], sems.at[1])
    if not first:
        total_copies = fetch(before, totals, sems.at[2])
    fill_shifted(shifted, arrivals)

    def lanes_of_tap(tap, lane):
        piece = shifted[tap % 3, :, pl.ds(tap // 3, side), :, pl.ds(pl.multiple_of(lane, LANES), LANES)]
        return piece.reshape(n_images * spots, LANES)

    start = fsdp_at * cols
    inside = start % LANES
    for at in range(0, turned.shape[0], LANES):
        lane = start - inside + at
        tap = jnp.minimum(lane // channels, 8)
        turned[at : at + LANES, :] = lanes_of_tap(tap, lane % channels).T
    left[:cols, :] = turned[pl.ds(pl.multiple_of(inside, strip), cols), :]
    for copy in strip_copies:
        copy.wait()
    for at, pair in enumerate(pairs):
        layer, other = owners[at]
        owner = (fsdp_at + n_fsdp - 2 * layer) % n_fsdp
        owner = owner + other * (1 - 2 * (owner % 2))
        left[cols : cols + strip, at * spots : (at + 1) * spots] = strips[pair, owner]
    if not first:
        for copy in total_copies:
            copy.wait()

    tiles_per = rows // LANES
    other_tile = factor_at + 1 - 2 * (factor_at % 2)

    def lanes_at(index):
        whose = jnp.where(index >= tiles_per, 1, 0)
        tile = jnp.where(index >= tiles_per, factor_at, other_tile)
        start = (tile * tiles_per + index - whose * tiles_per) * LANES
        return lanes_of_tap(start // channels, start % channels)

    def product(first_index, count):
        right = jnp.concatenate([lanes_at(first_index + k) for k in range(count)], axis=1)
        return jnp.dot(left[...], right, preferred_element_type=jnp.float32)

    def keep(whose, lane, count, value):
        at = pl.ds(pl.multiple_of(lane, LANES), count * LANES)
        for kind, part in ((0, value[:cols]), (1, value[cols:])):
            if not first:
                part = part + totals[2 * whose + kind][:, at]
            totals[2 * whose + kind][:, at] = part

    def keep_largest(whose):
        grads = totals[2 * whose + 1]
        grads[:, rows:] = jnp.full((strip, LANES), jnp.max(jnp.abs(grads[:, :rows])))

    half, odd = tiles_per // 2, tiles_per % 2

    @pl.loop(0, half)
    def _(step):
        keep(0, step * 2 * LANES, 2, product(2 * step, 2))

    if odd:
        both = product(2 * half, 2)
        keep(0, 2 * half * LANES, 1, both[:, :LANES])
        keep(1, 0, 1, both[:, LANES:])
    keep_largest(0)
    theirs_out = fetch(totals[:2], out_refs[:2], sems.at[3])

    @pl.loop(0, half)
    def _(step):
        keep(1, (odd + 2 * step) * LANES, 2, product(tiles_per + odd + 2 * step, 2))

    keep_largest(1)
    mine_out = fetch(totals[2:], out_refs[2:], sems.at[4])
    for copy in theirs_out + mine_out:
        copy.wait()


def add_products(owners, images, pairs, strips, before, cols, rows):
    n_images, side, channels, strip = len(images), images[0].shape[1], images[0].shape[3], strips[0].shape[1]
    spots = side * side
    shapes = [(cols, rows), (strip, rows + LANES)] * 2
    operands = [*images, *strips, *(before or [])]
    n_front = n_images + len(strips)
    return pl.pallas_call(
        lambda *refs: products_kernel(owners, pairs, len(strips), before is None, *refs),
        out_shape=[jax.ShapeDtypeStruct(shape, jnp.float32) for shape in shapes],
        in_specs=[pl.BlockSpec(memory_space=pl.ANY)] * len(operands),
        out_specs=[pl.BlockSpec(memory_space=pl.ANY)] * 4,
        scratch_shapes=[pltpu.VMEM(shape, jnp.float32) for shape in shapes]
        + [
            pltpu.VMEM((3, n_images, side + 2, side, channels), jnp.bfloat16),
            pltpu.VMEM(((cols + strip + LANES - 1) // LANES * LANES, n_images * spots), jnp.bfloat16),
            pltpu.VMEM((cols + strip, n_images * spots), jnp.bfloat16),
            pltpu.VMEM((len(strips),) + strips[0].shape, jnp.bfloat16),
            pltpu.SemaphoreType.DMA((5, max(4, n_images))),
        ],
        input_output_aliases={} if before is None else {n_front + k: k for k in range(4)},
        compiler_params=pltpu.CompilerParams(vmem_limit_bytes=58 * 1024 * 1024),
        cost_estimate=pl.CostEstimate(
            flops=4 * (cols + strip) * rows * n_images * spots,
            bytes_accessed=16 * (cols + strip) * rows,
            transcendentals=0,
        ),
    )(*operands)


def scale_kernel(mine_ref, theirs_ref, out_ref):
    rows = out_ref.shape[1] - LANES
    largest = mine_ref[:, rows:] + theirs_ref[:, rows:]
    exponent = jnp.floor(jnp.log2(jnp.maximum(largest, 1e-30))) - 14.0
    scale = jnp.exp2(-exponent)
    for at in range(0, rows, LANES):
        lanes = slice(at, at + LANES)
        out_ref[:, lanes] = (mine_ref[:, lanes] + theirs_ref[:, lanes]) * scale
    out_ref[:, rows:] = exponent


def scale_strips(mine, theirs):
    return pl.pallas_call(
        scale_kernel,
        out_shape=jax.ShapeDtypeStruct(mine.shape, jnp.float32),
        in_specs=[pl.BlockSpec(memory_space=pltpu.VMEM)] * 2,
        out_specs=pl.BlockSpec(memory_space=pltpu.VMEM),
        compiler_params=pltpu.CompilerParams(vmem_limit_bytes=4 * 1024 * 1024),
    )(mine, theirs)


def tail_kernel(strip, block, layers, *refs):
    a_any, g_any = refs[:2]
    strip_refs, (away_ref, kept_ref) = refs[2:-8], refs[-8:-6]
    a_tile, g_whole, columns, inverse, away_vmem, sems = refs[-6:]
    channels = g_any.shape[0]
    n_fsdp, n_factor = lax.axis_size("fsdp"), lax.axis_size("factor")
    fsdp_at, factor_at = lax.axis_index("fsdp"), lax.axis_index("factor")
    core_at, pair_at = factor_at % 2, factor_at // 2
    copies = fetch([a_any, g_any], [a_tile, g_whole], sems.at[0])
    strip_copies = fetch(
        strip_refs,
        [columns.at[pl.ds(at * strip, strip)] for at in range(len(strip_refs))],
        sems.at[1],
    )
    copies[1].wait()
    for at, (layer, other) in enumerate(layers):
        owner = (fsdp_at + n_fsdp - 2 * layer) % n_fsdp
        owner = owner + other * (1 - 2 * (owner % 2))
        rows = pl.ds(pl.multiple_of(owner * strip, strip), strip)
        for to in range(n_factor):
            away, step = 1 - to // (n_factor // 2), to % (n_factor // 2)
            place = 2 * ((pair_at + step) % (n_factor // 2)) + (core_at + away) % 2
            lanes = pl.ds(pl.multiple_of(place * block, block), block)
            inverse[at * strip : (at + 1) * strip, to * block : (to + 1) * block] = g_whole[rows, lanes]
    copies[0].wait()
    for copy in strip_copies:
        copy.wait()
    first = lax.dot_general(
        a_tile[...],
        columns[...],
        (((1,), (1,)), ((), ())),
        precision=lax.Precision.HIGH,
        preferred_element_type=jnp.float32,
    )
    away_vmem[...] = jnp.dot(
        first,
        inverse[:, : channels // 2],
        precision=lax.Precision.HIGH,
        preferred_element_type=jnp.float32,
    )
    away_out = fetch([away_vmem], [away_ref], sems.at[2])
    kept_ref[...] = jnp.dot(
        first,
        inverse[:, channels // 2 :],
        precision=lax.Precision.HIGH,
        preferred_element_type=jnp.float32,
    )
    away_out[0].wait()


def tail_products(a_inverse, g_inverse, strips, layers, block):
    channels, strip = g_inverse.shape[0], strips[0].shape[0]
    rows, depth = a_inverse.shape
    half = (rows, channels // 2)
    return pl.pallas_call(
        lambda *refs: tail_kernel(strip, block, layers, *refs),
        out_shape=[jax.ShapeDtypeStruct(half, jnp.float32)] * 2,
        in_specs=[pl.BlockSpec(memory_space=pl.ANY)] * (2 + len(strips)),
        out_specs=[pl.BlockSpec(memory_space=pl.ANY), pl.BlockSpec(memory_space=pltpu.VMEM)],
        scratch_shapes=[
            pltpu.VMEM((rows, depth), jnp.float32),
            pltpu.VMEM((channels, channels), jnp.float32),
            pltpu.VMEM((channels, depth), jnp.float32),
            pltpu.VMEM((channels, channels), jnp.float32),
            pltpu.VMEM(half, jnp.float32),
            pltpu.SemaphoreType.DMA((3, max(2, len(strips)))),
        ],
        compiler_params=pltpu.CompilerParams(vmem_limit_bytes=26 * 1024 * 1024),
        cost_estimate=pl.CostEstimate(
            flops=6 * rows * channels * (depth + channels),
            bytes_accessed=4 * rows * (depth + channels),
            transcendentals=0,
        ),
    )(a_inverse, g_inverse, *strips)


def conv_kernel(n_images, *refs):
    image_refs, part_refs = refs[:n_images], refs[n_images : n_images + 2]
    out_refs, (shifted, parts, weight, sems) = refs[n_images + 2 : -4], refs[-4:]
    side, channels = image_refs[0].shape[1], image_refs[0].shape[3]
    n_near, depth, block = part_refs[0].shape
    fsdp_at = lax.axis_index("fsdp")
    arrivals = fetch(
        [ref.at[0] for ref in image_refs],
        [shifted.at[1, at, pl.ds(1, side)] for at in range(n_images)],
        sems.at[0],
    )
    part_copies = fetch(part_refs, [parts.at[at] for at in range(2)], sems.at[1])
    fill_shifted(shifted, arrivals)
    for copy in part_copies:
        copy.wait()
    for near in range(n_near):
        for far in range(2):
            owner = (fsdp_at ^ (2 * near + far)) * depth
            weight[pl.ds(pl.multiple_of(owner, 64), depth), :] = parts[far, near]
    for at, ref in enumerate(out_refs):
        total = jnp.zeros((side * side, block), jnp.float32)
        for tap in range(9):
            left = shifted[tap % 3, at, tap // 3 : tap // 3 + side].reshape(side * side, channels)
            total += jnp.dot(
                left,
                weight[tap * channels : (tap + 1) * channels, :],
                preferred_element_type=jnp.float32,
            )
        ref[0] = total.astype(jnp.bfloat16).reshape(side, side, block)


def convolve(images, near_parts, far_parts):
    n_images, (_, side, _, channels) = len(images), images[0].shape
    block = near_parts.shape[2]
    return pl.pallas_call(
        lambda *refs: conv_kernel(n_images, *refs),
        out_shape=[jax.ShapeDtypeStruct((1, side, side, block), jnp.bfloat16)] * n_images,
        in_specs=[pl.BlockSpec(memory_space=pl.ANY)] * (n_images + 2),
        out_specs=[pl.BlockSpec(memory_space=pltpu.VMEM)] * n_images,
        scratch_shapes=[
            pltpu.VMEM((3, n_images, side + 2, side, channels), jnp.bfloat16),
            pltpu.VMEM((2,) + near_parts.shape, jnp.bfloat16),
            pltpu.VMEM((9 * channels, block), jnp.bfloat16),
            pltpu.SemaphoreType.DMA((2, n_images)),
        ],
        compiler_params=pltpu.CompilerParams(vmem_limit_bytes=58 * 1024 * 1024),
        cost_estimate=pl.CostEstimate(
            flops=36 * n_images * side * side * channels * block,
            bytes_accessed=2 * (9 * channels * block + n_images * side * side * channels),
            transcendentals=0,
        ),
    )(*images, near_parts, far_parts)


def side_by_side_kernel(*refs):
    block, n_factor = refs[0].shape[3], lax.axis_size("factor")
    factor_at, n_pair = lax.axis_index("factor"), n_factor // 2
    for at, ref in enumerate(refs[:-1]):
        place = 2 * ((factor_at // 2 + at % n_pair) % n_pair) + (factor_at + at // n_pair) % 2
        refs[-1][:, :, :, pl.ds(pl.multiple_of(place * block, LANES), block)] = ref[...]


def side_by_side(blocks):
    whole = pl.BlockSpec(memory_space=pltpu.VMEM)
    shape = blocks[0].shape[:3] + (len(blocks) * blocks[0].shape[3],)
    return pl.pallas_call(
        side_by_side_kernel,
        out_shape=jax.ShapeDtypeStruct(shape, blocks[0].dtype),
        in_specs=[whole] * len(blocks),
        out_specs=whole,
        compiler_params=pltpu.CompilerParams(vmem_limit_bytes=4 * 1024 * 1024),
    )(*blocks)


def gather_plan(n_layer, n_pair):
    far_layers = sorted(range(1, n_layer), key=lambda step: min(step, n_layer - step))
    waiting = {"layer": [(("layer", layer, 0), None) for layer in far_layers], "side": [], "pair": []}
    for turn, layer in enumerate([0] + far_layers):
        waiting["side"].append((("side", layer, 0), ("layer", layer, 0)))
        for pair in range(1, n_pair):
            waiting["pair"].append((("pair", layer, pair), ("layer", layer, 0)))
            if turn % 2 == 0:
                waiting["pair"].append((("both", layer, pair), ("side", layer, 0)))
            else:
                waiting["side"].append((("both", layer, pair), ("pair", layer, pair)))
    for link in waiting.values():
        link.sort(key=lambda entry: entry[0][0] == "both")
    ready, busy, turns = {None: 0, ("layer", 0, 0): 0}, {link: 0 for link in waiting}, {}
    order, step = [], 0
    while any(waiting.values()):
        for link, entries in waiting.items():
            free = [entry for entry in entries if ready.get(entry[1], step + 1) <= step]
            if busy[link] > step or not free:
                continue
            count = 2 if link == "layer" and step == 0 else 1
            for item, source in free[:count]:
                entries.remove((item, source))
                hops = min(item[1], n_layer - item[1]) if link == "layer" else 1
                busy[link] = step + hops * count
                ready[item] = busy[link]
                turns[link] = turns.get(link, -1) + 1
                order.append((item, source, link, turns[link]))
        step += 1
    return order, ready


def per_device(activations, cotangent, weight, a_factor_old, g_factor_old, a_inverse, g_inverse):
    channels = activations.shape[3]
    n_fsdp, n_factor = lax.axis_size("fsdp"), lax.axis_size("factor")
    n_layer, n_pair = n_fsdp // 2, n_factor // 2
    fsdp_at, factor_at = lax.axis_index("fsdp"), lax.axis_index("factor")
    core_at, pair_at = factor_at % 2, factor_at // 2
    rows, cols = a_factor_old.shape
    strip = channels // n_fsdp
    block = channels // n_factor

    def over_layer(array, step):
        return moved(array, "fsdp", lambda at: at + 2 * step)

    def over_side(array):
        return moved(array, "fsdp", lambda at: at ^ 1)

    def over_pair(array, step):
        return moved(array, "factor", lambda at: at + 2 * step)

    def over_core(array):
        return moved(array, "factor", lambda at: at ^ 1)

    def after(arrays, events):
        return lax.optimization_barrier((arrays, events))[0]

    def transfer(array, item, how):
        if how == "layer":
            return over_layer(array, item[1])
        if how == "pair":
            return over_pair(array, item[2])
        return over_side(array)

    own_cot = cotangent.reshape(-1, channels)
    maps = {("layer", 0, 0): activations}
    plan, ready = gather_plan(n_layer, n_pair)
    sent = {"layer": [], "side": [], "pair": []}
    strips_by_pair = []
    for item, source, link, turn in plan:
        array = activations if source is None else maps[source]
        events = sent[link][max(turn - 2, 0) : turn - 1]
        if link == "pair" and item == [entry[0] for entry in plan if entry[2] == "pair"][-1]:
            events = events + strips_by_pair
        maps[item] = transfer(after(array, events), item, link)
        sent[link].append(maps[item])
        if link == "side" and turn == 0:
            strips = after(own_cot, [maps[item]]).T.reshape(n_fsdp, strip, own_cot.shape[0])
            strips = lax.all_to_all(strips, "fsdp", split_axis=0, concat_axis=0)
        if link == "pair" and turn == 2:
            strips_by_pair = [strips] + [
                over_pair(after(strips, [maps[item]]), step) for step in range(1, n_pair)
            ]
    first_event, last_layer = sent["side"][:1], sent["layer"][-1:]
    near_end, at_end = sent["pair"][-2:-1], sent["pair"][-1:] + sent["side"][-1:]

    aligned = rows % LANES == 0 and channels % LANES == 0 and activations.shape[0] == 1
    images = sorted(maps, key=lambda item: ready[item])
    totals = None
    for batch in (images,):
        owners, pairs = [], []
        for kind, layer, pair in batch:
            owner = (fsdp_at - 2 * layer) % n_fsdp
            owners.append(owner ^ 1 if kind in ("side", "both") else owner)
            pairs.append(pair)
        if aligned:
            totals = add_products(
                [(layer, int(kind in ("side", "both"))) for kind, layer, _ in batch],
                [maps[item] for item in batch], pairs, strips_by_pair, totals, cols, rows
            )
            continue
        for at in range(0, len(batch), 2 * n_pair):
            part = jnp.concatenate([maps[item] for item in batch[at : at + 2 * n_pair]], axis=0)
            col_tile = tile_of_patches(part, fsdp_at * cols, cols)
            cot_tile = jnp.concatenate(
                [
                    lax.dynamic_index_in_dim(strips_by_pair[pair], owner, 0, keepdims=False)
                    for pair, owner in list(zip(pairs, owners))[at : at + 2 * n_pair]
                ],
                axis=1,
            )
            more = []
            for tile in (factor_at ^ 1, factor_at):
                row_tile = tile_of_patches(part, tile * rows, rows)
                more.append(by_rows(col_tile, row_tile))
                more.append(jnp.dot(cot_tile, row_tile, preferred_element_type=jnp.float32))
            totals = more if totals is None else [old + new for old, new in zip(totals, more)]
    if not aligned:
        for at in (1, 3):
            largest = jnp.full((strip, LANES), jnp.max(jnp.abs(totals[at])))
            totals[at] = jnp.concatenate([totals[at], largest], axis=1)

    g_partial = by_rows(after(own_cot, first_event), own_cot).reshape(n_pair, 2, block, channels)
    g_pairs = lax.dynamic_index_in_dim(g_partial, core_at, 1, keepdims=False) + over_core(
        lax.dynamic_index_in_dim(g_partial, 1 - core_at, 1, keepdims=False)
    )
    g_pairs = after(g_pairs, near_end)
    g_sum = lax.dynamic_index_in_dim(g_pairs, pair_at, 0, keepdims=False)
    for step in range(1, n_pair):
        away = lax.dynamic_index_in_dim(g_pairs, (pair_at + step) % n_pair, 0, keepdims=False)
        g_sum = g_sum + over_pair(away, step)
    weight_part = after(weight, last_layer)
    near_parts = [lax.dynamic_slice_in_dim(weight_part, factor_at * block, block, 1)]
    distance = 2
    while distance < n_fsdp:
        both = moved(jnp.stack(near_parts), "fsdp", lambda to, d=distance: to ^ d)
        near_parts = near_parts + [both[k] for k in range(len(near_parts))]
        distance *= 2
    near_stack = jnp.stack(near_parts)
    far_parts = over_side(after(near_stack, at_end))
    distance = n_fsdp // 2
    g_sum = after(g_sum, at_end)
    while distance > 2:
        g_sum = g_sum + moved(g_sum, "fsdp", lambda to, d=distance: to ^ d)
        distance //= 2
    near_images = [activations] + [maps["pair", 0, step] for step in range(1, n_pair)]
    group = near_images + [over_core(image) for image in after(near_images, near_end)]
    theirs = after(totals[1], [far_parts, g_sum] + group)
    theirs = over_core(theirs)
    pixel_total = float(
        activations.shape[0] * activations.shape[1] * activations.shape[2] * n_fsdp * n_factor
    )

    if aligned:
        packed = scale_strips(totals[3], theirs).astype(jnp.float16)
    else:
        largest = totals[3][:, rows : rows + 1] + theirs[:, rows : rows + 1]
        exponent = jnp.floor(jnp.log2(jnp.maximum(largest, 1e-30))) - 14.0
        packed = (totals[3] + theirs)[:, :rows] * jnp.exp2(-exponent)
        exponent = jnp.broadcast_to(exponent, (strip, LANES))
        packed = jnp.concatenate([packed, exponent], axis=1).astype(jnp.float16)
    near_packed = [packed] + [over_layer(packed, step) for step in range(1, n_layer)]

    cov_back = over_core(after(totals[0], [packed]))
    group = after(group, [packed])
    if aligned and block % LANES == 0:
        group_out = convolve(group, near_stack, far_parts)
    else:
        kernel = jnp.stack([part for pair in zip(near_stack, far_parts) for part in pair])
        kernel = jnp.concatenate(
            [
                lax.dynamic_index_in_dim(kernel, fsdp_at ^ at, 0, keepdims=False)
                for at in range(n_fsdp)
            ]
        ).reshape(3, 3, channels, block)
        group_out = lax.conv_general_dilated(
            jnp.concatenate(group),
            kernel,
            (1, 1),
            "SAME",
            dimension_numbers=("NHWC", "HWIO", "NHWC"),
            preferred_element_type=jnp.float32,
        ).astype(jnp.bfloat16)
        group_out = jnp.split(group_out, n_factor)
    far_packed, came = {0: over_side(packed)}, list(group_out)
    for step in sorted(range(1, n_layer), key=lambda step: min(step, n_layer - step)):
        far_packed[step] = over_side(after(near_packed[step], came))
        came = came + [near_packed[step]]
    far_packed = [far_packed[step] for step in range(n_layer)]

    own_maps, block_order = [], []
    outputs = after(list(group_out), far_packed)
    for other in range(2):
        for pair in range(n_pair):
            out = outputs[other * n_pair + pair]
            if pair + other:
                out = moved(out, "factor", lambda at, o=other, p=pair: (at ^ o) - 2 * p)
            own_maps.append(out)
            block_order.append(2 * ((pair_at + pair) % n_pair) + (core_at + other) % 2)
    g_side = over_side(after(g_sum, far_packed))
    strips_of_grad = [
        array[:, :rows].astype(jnp.float32) * jnp.exp2(array[:, rows : rows + 1].astype(jnp.float32))
        for array in near_packed + far_packed
    ]
    came_from = [(fsdp_at - 2 * step) % n_fsdp for step in range(n_layer)]
    came_from = came_from + [at ^ 1 for at in came_from]
    order = [
        2 * ((pair_at + step) % n_pair) + (core_at + other) % 2
        for other in (1, 0)
        for step in range(n_pair)
    ]
    if aligned and block % LANES == 0:
        away, kept = tail_products(
            after(a_inverse, [cov_back]),
            g_inverse,
            strips_of_grad,
            [(step, other) for other in range(2) for step in range(n_layer)],
            block,
        )
    else:
        inverse = jnp.concatenate(
            [lax.dynamic_slice_in_dim(g_inverse, at * block, block, 1) for at in order], axis=1
        )
        inverse = jnp.concatenate(
            [lax.dynamic_slice_in_dim(inverse, at * strip, strip, 0) for at in came_from]
        )
        partial = lax.dot_general(
            a_inverse,
            jnp.concatenate(strips_of_grad),
            (((1,), (1,)), ((), ())),
            precision=lax.Precision.HIGH,
            preferred_element_type=jnp.float32,
        )
        partial = jnp.dot(
            partial, inverse, precision=lax.Precision.HIGH, preferred_element_type=jnp.float32
        )
        away, kept = partial[:, : channels // 2], partial[:, channels // 2 :]
    by_pair = kept + over_core(away)
    cov_own = totals[2] + after(cov_back, by_pair)
    a_factor = 0.5 * a_factor_old + (0.5 / pixel_total) * cov_own.T
    result = by_pair[:, :block]
    for step in range(1, n_pair):
        back = over_pair(by_pair[:, step * block : (step + 1) * block], step)
        result = result + after(back, a_factor)
    g_sum = g_sum + after(g_side, by_pair)
    g_sum = g_sum + after(moved(g_sum, "fsdp", lambda to: to ^ 2), back)
    natural_grad = result.astype(jnp.bfloat16)


    own_maps = after(own_maps, by_pair)
    if aligned and block % LANES == 0:
        conv_out = side_by_side(own_maps)
    else:
        stacked = jnp.zeros((n_factor,) + own_maps[0].shape, jnp.bfloat16)
        for at, out in zip(block_order, own_maps):
            stacked = lax.dynamic_update_index_in_dim(stacked, out, at, 0)
        conv_out = jnp.concatenate(jnp.split(stacked, n_factor), axis=4)[0]

    g_factor = 0.5 * g_factor_old + 0.5 * g_sum
    return (conv_out, a_factor, g_factor, natural_grad)


def solution(mesh):
    images = P(("fsdp", "factor"), None, None, None)
    return jax.shard_map(
        per_device,
        mesh=mesh,
        in_specs=(
            images,
            images,
            P("fsdp", None),
            P("factor", "fsdp"),
            P("factor", None),
            P("fsdp", "factor"),
            P(),
        ),
        out_specs=(
            images,
            P("factor", "fsdp"),
            P("factor", None),
            P("fsdp", "factor"),
        ),
        check_vma=False,
    )
```

```python
import jax
import jax.numpy as jnp
from jax import lax
from jax.experimental import pallas as pl
from jax.experimental.pallas import tpu as pltpu
from jax.sharding import PartitionSpec as P

LANES = 128


def by_rows(first_op, second_op):
    return lax.dot_general(
        first_op, second_op, (((0,), (0,)), ((), ())), preferred_element_type=jnp.float32
    )


def moved(array, axis, target):
    count = lax.axis_size(axis)
    return lax.ppermute(array, axis, [(at, target(at) % count) for at in range(count)])


def tile_of_patches(images, start, width):
    side, channels = images.shape[1], images.shape[3]
    padded = jnp.pad(images, ((0, 0), (1, 1), (1, 1), (0, 0)))
    first_tap, offset = start // channels, start % channels
    rolled = lax.dynamic_slice_in_dim(
        jnp.concatenate([padded, padded], axis=3), offset, channels, 3
    )
    lane = lax.broadcasted_iota(jnp.int32, (1, 1, 1, channels), 3)

    def tap(index):
        index = jnp.minimum(index, 8)
        return lax.dynamic_slice(
            rolled, (0, index // 3, index % 3, 0), (images.shape[0], side, side, channels)
        )

    pieces = []
    for at in range(0, width, channels):
        step = at // channels
        piece = jnp.where(lane < channels - offset, tap(first_tap + step), tap(first_tap + step + 1))
        pieces.append(piece[..., : min(channels, width - at)])
    return jnp.concatenate(pieces, axis=3).reshape(-1, width)


def fill_shifted(shifted, arrivals):
    n_images, tall, side, channels = shifted.shape[1:]
    spots = side * side
    spot = lax.broadcasted_iota(jnp.int32, (spots, LANES), 0) % side
    empty = jnp.zeros((side, channels), jnp.bfloat16)
    for at in range(n_images):
        for col_off in range(3):
            shifted[col_off, at, 0] = empty
            shifted[col_off, at, tall - 1] = empty
    for at, arrival in enumerate(arrivals):
        arrival.wait()
        for lane in range(0, channels, LANES):
            part = shifted[1, at, 1 : side + 1, :, lane : lane + LANES]
            part = part.reshape(spots, LANES).astype(jnp.float32)
            before_it = jnp.where(spot == 0, 0.0, pltpu.roll(part, 1, 0))
            after_it = jnp.where(spot == side - 1, 0.0, pltpu.roll(part, spots - 1, 0))
            for col_off, moved_part in ((0, before_it), (2, after_it)):
                shifted[col_off, at, 1 : side + 1, :, lane : lane + LANES] = moved_part.astype(
                    jnp.bfloat16
                ).reshape(side, side, LANES)


def fetch(sources, targets, sems):
    copies = [
        pltpu.make_async_copy(source, target, sems.at[at])
        for at, (source, target) in enumerate(zip(sources, targets))
    ]
    for copy in copies:
        copy.start()
    return copies


def products_kernel(owners, pairs, n_pair, first, *refs):
    image_refs, strip_refs = refs[: len(pairs)], refs[len(pairs) : len(pairs) + n_pair]
    refs = refs[len(pairs) + n_pair :]
    before, refs = (None, refs) if first else (refs[:4], refs[4:])
    out_refs, totals, (shifted, turned, left, strips, sems) = refs[:4], refs[4:8], refs[8:]
    n_images, side, channels = len(image_refs), image_refs[0].shape[1], image_refs[0].shape[3]
    spots = side * side
    cols, rows = totals[0].shape
    strip = totals[1].shape[0]
    n_fsdp = strip_refs[0].shape[0]
    fsdp_at, factor_at = lax.axis_index("fsdp"), lax.axis_index("factor")

    arrivals = fetch(
        [ref.at[0] for ref in image_refs],
        [shifted.at[1, at, pl.ds(1, side)] for at in range(n_images)],
        sems.at[0],
    )
    strip_copies = fetch(strip_refs, [strips.at[at] for at in range(n_pair)], sems.at[1])
    if not first:
        total_copies = fetch(before, totals, sems.at[2])
    fill_shifted(shifted, arrivals)

    def lanes_of_tap(tap, lane):
        piece = shifted[tap % 3, :, pl.ds(tap // 3, side), :, pl.ds(pl.multiple_of(lane, LANES), LANES)]
        return piece.reshape(n_images * spots, LANES)

    start = fsdp_at * cols
    inside = start % LANES
    for at in range(0, turned.shape[0], LANES):
        lane = start - inside + at
        tap = jnp.minimum(lane // channels, 8)
        turned[at : at + LANES, :] = lanes_of_tap(tap, lane % channels).T
    left[:cols, :] = turned[pl.ds(pl.multiple_of(inside, strip), cols), :]
    for copy in strip_copies:
        copy.wait()
    for at, pair in enumerate(pairs):
        layer, other = owners[at]
        owner = (fsdp_at + n_fsdp - 2 * layer) % n_fsdp
        owner = owner + other * (1 - 2 * (owner % 2))
        left[cols : cols + strip, at * spots : (at + 1) * spots] = strips[pair, owner]
    if not first:
        for copy in total_copies:
            copy.wait()

    tiles_per = rows // LANES
    other_tile = factor_at + 1 - 2 * (factor_at % 2)

    def lanes_at(index):
        whose = jnp.where(index >= tiles_per, 1, 0)
        tile = jnp.where(index >= tiles_per, factor_at, other_tile)
        start = (tile * tiles_per + index - whose * tiles_per) * LANES
        return lanes_of_tap(start // channels, start % channels)

    def product(first_index, count):
        right = jnp.concatenate([lanes_at(first_index + k) for k in range(count)], axis=1)
        return jnp.dot(left[...], right, preferred_element_type=jnp.float32)

    def keep(whose, lane, count, value):
        at = pl.ds(pl.multiple_of(lane, LANES), count * LANES)
        for kind, part in ((0, value[:cols]), (1, value[cols:])):
            if not first:
                part = part + totals[2 * whose + kind][:, at]
            totals[2 * whose + kind][:, at] = part

    def keep_largest(whose):
        grads = totals[2 * whose + 1]
        grads[:, rows:] = jnp.full((strip, LANES), jnp.max(jnp.abs(grads[:, :rows])))

    half, odd = tiles_per // 2, tiles_per % 2

    @pl.loop(0, half)
    def _(step):
        keep(0, step * 2 * LANES, 2, product(2 * step, 2))

    if odd:
        both = product(2 * half, 2)
        keep(0, 2 * half * LANES, 1, both[:, :LANES])
        keep(1, 0, 1, both[:, LANES:])
    keep_largest(0)
    theirs_out = fetch(totals[:2], out_refs[:2], sems.at[3])

    @pl.loop(0, half)
    def _(step):
        keep(1, (odd + 2 * step) * LANES, 2, product(tiles_per + odd + 2 * step, 2))

    keep_largest(1)
    mine_out = fetch(totals[2:], out_refs[2:], sems.at[4])
    for copy in theirs_out + mine_out:
        copy.wait()


def add_products(owners, images, pairs, strips, before, cols, rows):
    n_images, side, channels, strip = len(images), images[0].shape[1], images[0].shape[3], strips[0].shape[1]
    spots = side * side
    shapes = [(cols, rows), (strip, rows + LANES)] * 2
    operands = [*images, *strips, *(before or [])]
    n_front = n_images + len(strips)
    return pl.pallas_call(
        lambda *refs: products_kernel(owners, pairs, len(strips), before is None, *refs),
        out_shape=[jax.ShapeDtypeStruct(shape, jnp.float32) for shape in shapes],
        in_specs=[pl.BlockSpec(memory_space=pl.ANY)] * len(operands),
        out_specs=[pl.BlockSpec(memory_space=pl.ANY)] * 4,
        scratch_shapes=[pltpu.VMEM(shape, jnp.float32) for shape in shapes]
        + [
            pltpu.VMEM((3, n_images, side + 2, side, channels), jnp.bfloat16),
            pltpu.VMEM(((cols + strip + LANES - 1) // LANES * LANES, n_images * spots), jnp.bfloat16),
            pltpu.VMEM((cols + strip, n_images * spots), jnp.bfloat16),
            pltpu.VMEM((len(strips),) + strips[0].shape, jnp.bfloat16),
            pltpu.SemaphoreType.DMA((5, max(4, n_images))),
        ],
        input_output_aliases={} if before is None else {n_front + k: k for k in range(4)},
        compiler_params=pltpu.CompilerParams(vmem_limit_bytes=58 * 1024 * 1024),
        cost_estimate=pl.CostEstimate(
            flops=4 * (cols + strip) * rows * n_images * spots,
            bytes_accessed=16 * (cols + strip) * rows,
            transcendentals=0,
        ),
    )(*operands)


def scale_kernel(mine_ref, theirs_ref, out_ref):
    rows = out_ref.shape[1] - LANES
    largest = mine_ref[:, rows:] + theirs_ref[:, rows:]
    exponent = jnp.floor(jnp.log2(jnp.maximum(largest, 1e-30))) - 14.0
    scale = jnp.exp2(-exponent)
    for at in range(0, rows, LANES):
        lanes = slice(at, at + LANES)
        out_ref[:, lanes] = (mine_ref[:, lanes] + theirs_ref[:, lanes]) * scale
    out_ref[:, rows:] = exponent


def scale_strips(mine, theirs):
    return pl.pallas_call(
        scale_kernel,
        out_shape=jax.ShapeDtypeStruct(mine.shape, jnp.float32),
        in_specs=[pl.BlockSpec(memory_space=pltpu.VMEM)] * 2,
        out_specs=pl.BlockSpec(memory_space=pltpu.VMEM),
        compiler_params=pltpu.CompilerParams(vmem_limit_bytes=4 * 1024 * 1024),
    )(mine, theirs)


def tail_kernel(strip, block, layers, *refs):
    a_any, g_any = refs[:2]
    strip_refs, (away_ref, kept_ref) = refs[2:-8], refs[-8:-6]
    a_tile, g_whole, columns, inverse, away_vmem, sems = refs[-6:]
    channels = g_any.shape[0]
    n_fsdp, n_factor = lax.axis_size("fsdp"), lax.axis_size("factor")
    fsdp_at, factor_at = lax.axis_index("fsdp"), lax.axis_index("factor")
    core_at, pair_at = factor_at % 2, factor_at // 2
    copies = fetch([a_any, g_any], [a_tile, g_whole], sems.at[0])
    strip_copies = fetch(
        strip_refs,
        [columns.at[pl.ds(at * strip, strip)] for at in range(len(strip_refs))],
        sems.at[1],
    )
    copies[1].wait()
    for at, (layer, other) in enumerate(layers):
        owner = (fsdp_at + n_fsdp - 2 * layer) % n_fsdp
        owner = owner + other * (1 - 2 * (owner % 2))
        rows = pl.ds(pl.multiple_of(owner * strip, strip), strip)
        for to in range(n_factor):
            away, step = 1 - to // (n_factor // 2), to % (n_factor // 2)
            place = 2 * ((pair_at + step) % (n_factor // 2)) + (core_at + away) % 2
            lanes = pl.ds(pl.multiple_of(place * block, block), block)
            inverse[at * strip : (at + 1) * strip, to * block : (to + 1) * block] = g_whole[rows, lanes]
    copies[0].wait()
    for copy in strip_copies:
        copy.wait()
    first = lax.dot_general(
        a_tile[...],
        columns[...],
        (((1,), (1,)), ((), ())),
        precision=lax.Precision.HIGH,
        preferred_element_type=jnp.float32,
    )
    away_vmem[...] = jnp.dot(
        first,
        inverse[:, : channels // 2],
        precision=lax.Precision.HIGH,
        preferred_element_type=jnp.float32,
    )
    away_out = fetch([away_vmem], [away_ref], sems.at[2])
    kept_ref[...] = jnp.dot(
        first,
        inverse[:, channels // 2 :],
        precision=lax.Precision.HIGH,
        preferred_element_type=jnp.float32,
    )
    away_out[0].wait()


def tail_products(a_inverse, g_inverse, strips, layers, block):
    channels, strip = g_inverse.shape[0], strips[0].shape[0]
    rows, depth = a_inverse.shape
    half = (rows, channels // 2)
    return pl.pallas_call(
        lambda *refs: tail_kernel(strip, block, layers, *refs),
        out_shape=[jax.ShapeDtypeStruct(half, jnp.float32)] * 2,
        in_specs=[pl.BlockSpec(memory_space=pl.ANY)] * (2 + len(strips)),
        out_specs=[pl.BlockSpec(memory_space=pl.ANY), pl.BlockSpec(memory_space=pltpu.VMEM)],
        scratch_shapes=[
            pltpu.VMEM((rows, depth), jnp.float32),
            pltpu.VMEM((channels, channels), jnp.float32),
            pltpu.VMEM((channels, depth), jnp.float32),
            pltpu.VMEM((channels, channels), jnp.float32),
            pltpu.VMEM(half, jnp.float32),
            pltpu.SemaphoreType.DMA((3, max(2, len(strips)))),
        ],
        compiler_params=pltpu.CompilerParams(vmem_limit_bytes=26 * 1024 * 1024),
        cost_estimate=pl.CostEstimate(
            flops=6 * rows * channels * (depth + channels),
            bytes_accessed=4 * rows * (depth + channels),
            transcendentals=0,
        ),
    )(a_inverse, g_inverse, *strips)


def conv_kernel(n_images, *refs):
    image_refs, part_refs = refs[:n_images], refs[n_images : n_images + 2]
    out_refs, (shifted, parts, weight, sems) = refs[n_images + 2 : -4], refs[-4:]
    side, channels = image_refs[0].shape[1], image_refs[0].shape[3]
    n_near, depth, block = part_refs[0].shape
    fsdp_at = lax.axis_index("fsdp")
    arrivals = fetch(
        [ref.at[0] for ref in image_refs],
        [shifted.at[1, at, pl.ds(1, side)] for at in range(n_images)],
        sems.at[0],
    )
    part_copies = fetch(part_refs, [parts.at[at] for at in range(2)], sems.at[1])
    fill_shifted(shifted, arrivals)
    for copy in part_copies:
        copy.wait()
    for near in range(n_near):
        for far in range(2):
            owner = (fsdp_at ^ (2 * near + far)) * depth
            weight[pl.ds(pl.multiple_of(owner, 64), depth), :] = parts[far, near]
    for at, ref in enumerate(out_refs):
        total = jnp.zeros((side * side, block), jnp.float32)
        for tap in range(9):
            left = shifted[tap % 3, at, tap // 3 : tap // 3 + side].reshape(side * side, channels)
            total += jnp.dot(
                left,
                weight[tap * channels : (tap + 1) * channels, :],
                preferred_element_type=jnp.float32,
            )
        ref[0] = total.astype(jnp.bfloat16).reshape(side, side, block)


def convolve(images, near_parts, far_parts):
    n_images, (_, side, _, channels) = len(images), images[0].shape
    block = near_parts.shape[2]
    return pl.pallas_call(
        lambda *refs: conv_kernel(n_images, *refs),
        out_shape=[jax.ShapeDtypeStruct((1, side, side, block), jnp.bfloat16)] * n_images,
        in_specs=[pl.BlockSpec(memory_space=pl.ANY)] * (n_images + 2),
        out_specs=[pl.BlockSpec(memory_space=pltpu.VMEM)] * n_images,
        scratch_shapes=[
            pltpu.VMEM((3, n_images, side + 2, side, channels), jnp.bfloat16),
            pltpu.VMEM((2,) + near_parts.shape, jnp.bfloat16),
            pltpu.VMEM((9 * channels, block), jnp.bfloat16),
            pltpu.SemaphoreType.DMA((2, n_images)),
        ],
        compiler_params=pltpu.CompilerParams(vmem_limit_bytes=58 * 1024 * 1024),
        cost_estimate=pl.CostEstimate(
            flops=36 * n_images * side * side * channels * block,
            bytes_accessed=2 * (9 * channels * block + n_images * side * side * channels),
            transcendentals=0,
        ),
    )(*images, near_parts, far_parts)


def side_by_side_kernel(*refs):
    block, n_factor = refs[0].shape[3], lax.axis_size("factor")
    factor_at, n_pair = lax.axis_index("factor"), n_factor // 2
    for at, ref in enumerate(refs[:-1]):
        place = 2 * ((factor_at // 2 + at % n_pair) % n_pair) + (factor_at + at // n_pair) % 2
        refs[-1][:, :, :, pl.ds(pl.multiple_of(place * block, LANES), block)] = ref[...]


def side_by_side(blocks):
    whole = pl.BlockSpec(memory_space=pltpu.VMEM)
    shape = blocks[0].shape[:3] + (len(blocks) * blocks[0].shape[3],)
    return pl.pallas_call(
        side_by_side_kernel,
        out_shape=jax.ShapeDtypeStruct(shape, blocks[0].dtype),
        in_specs=[whole] * len(blocks),
        out_specs=whole,
        compiler_params=pltpu.CompilerParams(vmem_limit_bytes=4 * 1024 * 1024),
    )(*blocks)


def gather_plan(n_layer, n_pair):
    far_layers = sorted(range(1, n_layer), key=lambda step: min(step, n_layer - step))
    waiting = {"layer": [(("layer", layer, 0), None) for layer in far_layers], "side": [], "pair": []}
    for turn, layer in enumerate([0] + far_layers):
        waiting["side"].append((("side", layer, 0), ("layer", layer, 0)))
        for pair in range(1, n_pair):
            waiting["pair"].append((("pair", layer, pair), ("layer", layer, 0)))
            if turn % 2 == 0:
                waiting["pair"].append((("both", layer, pair), ("side", layer, 0)))
            else:
                waiting["side"].append((("both", layer, pair), ("pair", layer, pair)))
    for link in waiting.values():
        link.sort(key=lambda entry: entry[0][0] == "both")
    ready, busy, turns = {None: 0, ("layer", 0, 0): 0}, {link: 0 for link in waiting}, {}
    order, step = [], 0
    while any(waiting.values()):
        for link, entries in waiting.items():
            free = [entry for entry in entries if ready.get(entry[1], step + 1) <= step]
            if busy[link] > step or not free:
                continue
            count = 2 if link == "layer" and step == 0 else 1
            for item, source in free[:count]:
                entries.remove((item, source))
                hops = min(item[1], n_layer - item[1]) if link == "layer" else 1
                busy[link] = step + hops * count
                ready[item] = busy[link]
                turns[link] = turns.get(link, -1) + 1
                order.append((item, source, link, turns[link]))
        step += 1
    return order, ready


def per_device(activations, cotangent, weight, a_factor_old, g_factor_old, a_inverse, g_inverse):
    channels = activations.shape[3]
    n_fsdp, n_factor = lax.axis_size("fsdp"), lax.axis_size("factor")
    n_layer, n_pair = n_fsdp // 2, n_factor // 2
    fsdp_at, factor_at = lax.axis_index("fsdp"), lax.axis_index("factor")
    core_at, pair_at = factor_at % 2, factor_at // 2
    rows, cols = a_factor_old.shape
    strip = channels // n_fsdp
    block = channels // n_factor

    def over_layer(array, step):
        return moved(array, "fsdp", lambda at: at + 2 * step)

    def over_side(array):
        return moved(array, "fsdp", lambda at: at ^ 1)

    def over_pair(array, step):
        return moved(array, "factor", lambda at: at + 2 * step)

    def over_core(array):
        return moved(array, "factor", lambda at: at ^ 1)

    def after(arrays, events):
        return lax.optimization_barrier((arrays, events))[0]

    def transfer(array, item, how):
        if how == "layer":
            return over_layer(array, item[1])
        if how == "pair":
            return over_pair(array, item[2])
        return over_side(array)

    own_cot = cotangent.reshape(-1, channels)
    maps = {("layer", 0, 0): activations}
    plan, ready = gather_plan(n_layer, n_pair)
    sent = {"layer": [], "side": [], "pair": []}
    strips_by_pair = []
    for item, source, link, turn in plan:
        array = activations if source is None else maps[source]
        events = sent[link][max(turn - 2, 0) : turn - 1]
        if link == "pair" and item == [entry[0] for entry in plan if entry[2] == "pair"][-1]:
            events = events + strips_by_pair
        maps[item] = transfer(after(array, events), item, link)
        sent[link].append(maps[item])
        if link == "side" and turn == 0:
            strips = after(own_cot, [maps[item]]).T.reshape(n_fsdp, strip, own_cot.shape[0])
            strips = lax.all_to_all(strips, "fsdp", split_axis=0, concat_axis=0)
        if link == "pair" and turn == 2:
            strips_by_pair = [strips] + [
                over_pair(after(strips, [maps[item]]), step) for step in range(1, n_pair)
            ]
    first_event, last_layer = sent["side"][:1], sent["layer"][-1:]
    near_end, at_end = sent["pair"][-2:-1], sent["pair"][-1:] + sent["side"][-1:]

    aligned = rows % LANES == 0 and channels % LANES == 0 and activations.shape[0] == 1
    images = sorted(maps, key=lambda item: ready[item])
    totals = None
    for batch in (images,):
        owners, pairs = [], []
        for kind, layer, pair in batch:
            owner = (fsdp_at - 2 * layer) % n_fsdp
            owners.append(owner ^ 1 if kind in ("side", "both") else owner)
            pairs.append(pair)
        if aligned:
            totals = add_products(
                [(layer, int(kind in ("side", "both"))) for kind, layer, _ in batch],
                [maps[item] for item in batch], pairs, strips_by_pair, totals, cols, rows
            )
            continue
        for at in range(0, len(batch), 2 * n_pair):
            part = jnp.concatenate([maps[item] for item in batch[at : at + 2 * n_pair]], axis=0)
            col_tile = tile_of_patches(part, fsdp_at * cols, cols)
            cot_tile = jnp.concatenate(
                [
                    lax.dynamic_index_in_dim(strips_by_pair[pair], owner, 0, keepdims=False)
                    for pair, owner in list(zip(pairs, owners))[at : at + 2 * n_pair]
                ],
                axis=1,
            )
            more = []
            for tile in (factor_at ^ 1, factor_at):
                row_tile = tile_of_patches(part, tile * rows, rows)
                more.append(by_rows(col_tile, row_tile))
                more.append(jnp.dot(cot_tile, row_tile, preferred_element_type=jnp.float32))
            totals = more if totals is None else [old + new for old, new in zip(totals, more)]
    if not aligned:
        for at in (1, 3):
            largest = jnp.full((strip, LANES), jnp.max(jnp.abs(totals[at])))
            totals[at] = jnp.concatenate([totals[at], largest], axis=1)

    g_partial = by_rows(after(own_cot, first_event), own_cot).reshape(n_pair, 2, block, channels)
    g_pairs = lax.dynamic_index_in_dim(g_partial, core_at, 1, keepdims=False) + over_core(
        lax.dynamic_index_in_dim(g_partial, 1 - core_at, 1, keepdims=False)
    )
    g_pairs = after(g_pairs, near_end)
    g_sum = lax.dynamic_index_in_dim(g_pairs, pair_at, 0, keepdims=False)
    for step in range(1, n_pair):
        away = lax.dynamic_index_in_dim(g_pairs, (pair_at + step) % n_pair, 0, keepdims=False)
        g_sum = g_sum + over_pair(away, step)
    weight_part = after(weight, last_layer)
    near_parts = [lax.dynamic_slice_in_dim(weight_part, factor_at * block, block, 1)]
    distance = 2
    while distance < n_fsdp:
        both = moved(jnp.stack(near_parts), "fsdp", lambda to, d=distance: to ^ d)
        near_parts = near_parts + [both[k] for k in range(len(near_parts))]
        distance *= 2
    near_stack = jnp.stack(near_parts)
    far_parts = over_side(after(near_stack, at_end))
    distance = n_fsdp // 2
    g_sum = g_sum + moved(g_sum, "fsdp", lambda to: to ^ 2)
    g_sum = after(g_sum, at_end)
    while distance > 2:
        g_sum = g_sum + moved(g_sum, "fsdp", lambda to, d=distance: to ^ d)
        distance //= 2
    near_images = [activations] + [maps["pair", 0, step] for step in range(1, n_pair)]
    group = near_images + [over_core(image) for image in after(near_images, near_end)]
    theirs = after(totals[1], [far_parts, g_sum] + group)
    theirs = over_core(theirs)
    pixel_total = float(
        activations.shape[0] * activations.shape[1] * activations.shape[2] * n_fsdp * n_factor
    )

    if aligned:
        packed = scale_strips(totals[3], theirs).astype(jnp.float16)
    else:
        largest = totals[3][:, rows : rows + 1] + theirs[:, rows : rows + 1]
        exponent = jnp.floor(jnp.log2(jnp.maximum(largest, 1e-30))) - 14.0
        packed = (totals[3] + theirs)[:, :rows] * jnp.exp2(-exponent)
        exponent = jnp.broadcast_to(exponent, (strip, LANES))
        packed = jnp.concatenate([packed, exponent], axis=1).astype(jnp.float16)
    near_packed = [packed] + [over_layer(packed, step) for step in range(1, n_layer)]

    cov_back = over_core(after(totals[0], [packed]))
    group = after(group, [packed])
    if aligned and block % LANES == 0:
        group_out = convolve(group, near_stack, far_parts)
    else:
        kernel = jnp.stack([part for pair in zip(near_stack, far_parts) for part in pair])
        kernel = jnp.concatenate(
            [
                lax.dynamic_index_in_dim(kernel, fsdp_at ^ at, 0, keepdims=False)
                for at in range(n_fsdp)
            ]
        ).reshape(3, 3, channels, block)
        group_out = lax.conv_general_dilated(
            jnp.concatenate(group),
            kernel,
            (1, 1),
            "SAME",
            dimension_numbers=("NHWC", "HWIO", "NHWC"),
            preferred_element_type=jnp.float32,
        ).astype(jnp.bfloat16)
        group_out = jnp.split(group_out, n_factor)
    far_packed, came = {0: over_side(packed)}, list(group_out)
    for step in sorted(range(1, n_layer), key=lambda step: min(step, n_layer - step)):
        far_packed[step] = over_side(after(near_packed[step], came))
        came = came + [near_packed[step]]
    far_packed = [far_packed[step] for step in range(n_layer)]

    own_maps, block_order = [], []
    outputs = after(list(group_out), far_packed)
    for other in range(2):
        for pair in range(n_pair):
            out = outputs[other * n_pair + pair]
            if pair + other:
                out = moved(out, "factor", lambda at, o=other, p=pair: (at ^ o) - 2 * p)
            own_maps.append(out)
            block_order.append(2 * ((pair_at + pair) % n_pair) + (core_at + other) % 2)
    g_side = over_side(after(g_sum, far_packed))
    strips_of_grad = [
        array[:, :rows].astype(jnp.float32) * jnp.exp2(array[:, rows : rows + 1].astype(jnp.float32))
        for array in near_packed + far_packed
    ]
    came_from = [(fsdp_at - 2 * step) % n_fsdp for step in range(n_layer)]
    came_from = came_from + [at ^ 1 for at in came_from]
    order = [
        2 * ((pair_at + step) % n_pair) + (core_at + other) % 2
        for other in (1, 0)
        for step in range(n_pair)
    ]
    if aligned and block % LANES == 0:
        away, kept = tail_products(
            after(a_inverse, [cov_back]),
            g_inverse,
            strips_of_grad,
            [(step, other) for other in range(2) for step in range(n_layer)],
            block,
        )
    else:
        inverse = jnp.concatenate(
            [lax.dynamic_slice_in_dim(g_inverse, at * block, block, 1) for at in order], axis=1
        )
        inverse = jnp.concatenate(
            [lax.dynamic_slice_in_dim(inverse, at * strip, strip, 0) for at in came_from]
        )
        partial = lax.dot_general(
            a_inverse,
            jnp.concatenate(strips_of_grad),
            (((1,), (1,)), ((), ())),
            precision=lax.Precision.HIGH,
            preferred_element_type=jnp.float32,
        )
        partial = jnp.dot(
            partial, inverse, precision=lax.Precision.HIGH, preferred_element_type=jnp.float32
        )
        away, kept = partial[:, : channels // 2], partial[:, channels // 2 :]
    by_pair = kept + over_core(away)
    cov_own = totals[2] + after(cov_back, by_pair)
    a_factor = 0.5 * a_factor_old + (0.5 / pixel_total) * cov_own.T
    result = by_pair[:, :block]
    for step in range(1, n_pair):
        back = over_pair(by_pair[:, step * block : (step + 1) * block], step)
        result = result + after(back, a_factor)
    g_sum = g_sum + after(g_side, back)
    natural_grad = result.astype(jnp.bfloat16)


    own_maps = after(own_maps, by_pair)
    if aligned and block % LANES == 0:
        conv_out = side_by_side(own_maps)
    else:
        stacked = jnp.zeros((n_factor,) + own_maps[0].shape, jnp.bfloat16)
        for at, out in zip(block_order, own_maps):
            stacked = lax.dynamic_update_index_in_dim(stacked, out, at, 0)
        conv_out = jnp.concatenate(jnp.split(stacked, n_factor), axis=4)[0]

    g_factor = 0.5 * g_factor_old + 0.5 * g_sum
    return (conv_out, a_factor, g_factor, natural_grad)


def solution(mesh):
    images = P(("fsdp", "factor"), None, None, None)
    return jax.shard_map(
        per_device,
        mesh=mesh,
        in_specs=(
            images,
            images,
            P("fsdp", None),
            P("factor", "fsdp"),
            P("factor", None),
            P("fsdp", "factor"),
            P(),
        ),
        out_specs=(
            images,
            P("factor", "fsdp"),
            P("factor", None),
            P("fsdp", "factor"),
        ),
        check_vma=False,
    )
```

```python
import jax
import jax.numpy as jnp
from jax import lax
from jax.experimental import pallas as pl
from jax.experimental.pallas import tpu as pltpu
from jax.sharding import PartitionSpec as P

LANES = 128


def by_rows(first_op, second_op):
    return lax.dot_general(
        first_op, second_op, (((0,), (0,)), ((), ())), preferred_element_type=jnp.float32
    )


def moved(array, axis, target):
    count = lax.axis_size(axis)
    return lax.ppermute(array, axis, [(at, target(at) % count) for at in range(count)])


def tile_of_patches(images, start, width):
    side, channels = images.shape[1], images.shape[3]
    padded = jnp.pad(images, ((0, 0), (1, 1), (1, 1), (0, 0)))
    first_tap, offset = start // channels, start % channels
    rolled = lax.dynamic_slice_in_dim(
        jnp.concatenate([padded, padded], axis=3), offset, channels, 3
    )
    lane = lax.broadcasted_iota(jnp.int32, (1, 1, 1, channels), 3)

    def tap(index):
        index = jnp.minimum(index, 8)
        return lax.dynamic_slice(
            rolled, (0, index // 3, index % 3, 0), (images.shape[0], side, side, channels)
        )

    pieces = []
    for at in range(0, width, channels):
        step = at // channels
        piece = jnp.where(lane < channels - offset, tap(first_tap + step), tap(first_tap + step + 1))
        pieces.append(piece[..., : min(channels, width - at)])
    return jnp.concatenate(pieces, axis=3).reshape(-1, width)


def fill_shifted(shifted, arrivals):
    n_images, tall, side, channels = shifted.shape[1:]
    spots = side * side
    spot = lax.broadcasted_iota(jnp.int32, (spots, LANES), 0) % side
    empty = jnp.zeros((side, channels), jnp.bfloat16)
    for at in range(n_images):
        for col_off in range(3):
            shifted[col_off, at, 0] = empty
            shifted[col_off, at, tall - 1] = empty
    for at, arrival in enumerate(arrivals):
        arrival.wait()
        for lane in range(0, channels, LANES):
            part = shifted[1, at, 1 : side + 1, :, lane : lane + LANES]
            part = part.reshape(spots, LANES).astype(jnp.float32)
            before_it = jnp.where(spot == 0, 0.0, pltpu.roll(part, 1, 0))
            after_it = jnp.where(spot == side - 1, 0.0, pltpu.roll(part, spots - 1, 0))
            for col_off, moved_part in ((0, before_it), (2, after_it)):
                shifted[col_off, at, 1 : side + 1, :, lane : lane + LANES] = moved_part.astype(
                    jnp.bfloat16
                ).reshape(side, side, LANES)


def fetch(sources, targets, sems):
    copies = [
        pltpu.make_async_copy(source, target, sems.at[at])
        for at, (source, target) in enumerate(zip(sources, targets))
    ]
    for copy in copies:
        copy.start()
    return copies


def products_kernel(owners, pairs, n_pair, first, *refs):
    image_refs, strip_refs = refs[: len(pairs)], refs[len(pairs) : len(pairs) + n_pair]
    refs = refs[len(pairs) + n_pair :]
    before, refs = (None, refs) if first else (refs[:4], refs[4:])
    out_refs, totals, (shifted, turned, left, strips, sems) = refs[:4], refs[4:8], refs[8:]
    n_images, side, channels = len(image_refs), image_refs[0].shape[1], image_refs[0].shape[3]
    spots = side * side
    cols, rows = totals[0].shape
    strip = totals[1].shape[0]
    n_fsdp = strip_refs[0].shape[0]
    fsdp_at, factor_at = lax.axis_index("fsdp"), lax.axis_index("factor")

    arrivals = fetch(
        [ref.at[0] for ref in image_refs],
        [shifted.at[1, at, pl.ds(1, side)] for at in range(n_images)],
        sems.at[0],
    )
    strip_copies = fetch(strip_refs, [strips.at[at] for at in range(n_pair)], sems.at[1])
    if not first:
        total_copies = fetch(before, totals, sems.at[2])
    fill_shifted(shifted, arrivals)

    def lanes_of_tap(tap, lane):
        piece = shifted[tap % 3, :, pl.ds(tap // 3, side), :, pl.ds(pl.multiple_of(lane, LANES), LANES)]
        return piece.reshape(n_images * spots, LANES)

    start = fsdp_at * cols
    inside = start % LANES
    for at in range(0, turned.shape[0], LANES):
        lane = start - inside + at
        tap = jnp.minimum(lane // channels, 8)
        turned[at : at + LANES, :] = lanes_of_tap(tap, lane % channels).T
    left[:cols, :] = turned[pl.ds(pl.multiple_of(inside, strip), cols), :]
    for copy in strip_copies:
        copy.wait()
    for at, pair in enumerate(pairs):
        layer, other = owners[at]
        owner = (fsdp_at + n_fsdp - 2 * layer) % n_fsdp
        owner = owner + other * (1 - 2 * (owner % 2))
        left[cols : cols + strip, at * spots : (at + 1) * spots] = strips[pair, owner]
    if not first:
        for copy in total_copies:
            copy.wait()

    tiles_per = rows // LANES
    other_tile = factor_at + 1 - 2 * (factor_at % 2)

    def lanes_at(index):
        whose = jnp.where(index >= tiles_per, 1, 0)
        tile = jnp.where(index >= tiles_per, factor_at, other_tile)
        start = (tile * tiles_per + index - whose * tiles_per) * LANES
        return lanes_of_tap(start // channels, start % channels)

    def product(first_index, count):
        right = jnp.concatenate([lanes_at(first_index + k) for k in range(count)], axis=1)
        return jnp.dot(left[...], right, preferred_element_type=jnp.float32)

    def keep(whose, lane, count, value):
        at = pl.ds(pl.multiple_of(lane, LANES), count * LANES)
        for kind, part in ((0, value[:cols]), (1, value[cols:])):
            if not first:
                part = part + totals[2 * whose + kind][:, at]
            totals[2 * whose + kind][:, at] = part

    def keep_largest(whose):
        grads = totals[2 * whose + 1]
        grads[:, rows:] = jnp.full((strip, LANES), jnp.max(jnp.abs(grads[:, :rows])))

    half, odd = tiles_per // 2, tiles_per % 2

    @pl.loop(0, half)
    def _(step):
        keep(0, step * 2 * LANES, 2, product(2 * step, 2))

    if odd:
        both = product(2 * half, 2)
        keep(0, 2 * half * LANES, 1, both[:, :LANES])
        keep(1, 0, 1, both[:, LANES:])
    keep_largest(0)
    theirs_out = fetch(totals[:2], out_refs[:2], sems.at[3])

    @pl.loop(0, half)
    def _(step):
        keep(1, (odd + 2 * step) * LANES, 2, product(tiles_per + odd + 2 * step, 2))

    keep_largest(1)
    mine_out = fetch(totals[2:], out_refs[2:], sems.at[4])
    for copy in theirs_out + mine_out:
        copy.wait()


def add_products(owners, images, pairs, strips, before, cols, rows):
    n_images, side, channels, strip = len(images), images[0].shape[1], images[0].shape[3], strips[0].shape[1]
    spots = side * side
    shapes = [(cols, rows), (strip, rows + LANES)] * 2
    operands = [*images, *strips, *(before or [])]
    n_front = n_images + len(strips)
    return pl.pallas_call(
        lambda *refs: products_kernel(owners, pairs, len(strips), before is None, *refs),
        out_shape=[jax.ShapeDtypeStruct(shape, jnp.float32) for shape in shapes],
        in_specs=[pl.BlockSpec(memory_space=pl.ANY)] * len(operands),
        out_specs=[pl.BlockSpec(memory_space=pl.ANY)] * 4,
        scratch_shapes=[pltpu.VMEM(shape, jnp.float32) for shape in shapes]
        + [
            pltpu.VMEM((3, n_images, side + 2, side, channels), jnp.bfloat16),
            pltpu.VMEM(((cols + strip + LANES - 1) // LANES * LANES, n_images * spots), jnp.bfloat16),
            pltpu.VMEM((cols + strip, n_images * spots), jnp.bfloat16),
            pltpu.VMEM((len(strips),) + strips[0].shape, jnp.bfloat16),
            pltpu.SemaphoreType.DMA((5, max(4, n_images))),
        ],
        input_output_aliases={} if before is None else {n_front + k: k for k in range(4)},
        compiler_params=pltpu.CompilerParams(vmem_limit_bytes=58 * 1024 * 1024),
        cost_estimate=pl.CostEstimate(
            flops=4 * (cols + strip) * rows * n_images * spots,
            bytes_accessed=16 * (cols + strip) * rows,
            transcendentals=0,
        ),
    )(*operands)


def scale_kernel(mine_ref, theirs_ref, out_ref):
    rows = out_ref.shape[1] - LANES
    largest = mine_ref[:, rows:] + theirs_ref[:, rows:]
    exponent = jnp.floor(jnp.log2(jnp.maximum(largest, 1e-30))) - 14.0
    scale = jnp.exp2(-exponent)
    for at in range(0, rows, LANES):
        lanes = slice(at, at + LANES)
        out_ref[:, lanes] = (mine_ref[:, lanes] + theirs_ref[:, lanes]) * scale
    out_ref[:, rows:] = exponent


def scale_strips(mine, theirs):
    return pl.pallas_call(
        scale_kernel,
        out_shape=jax.ShapeDtypeStruct(mine.shape, jnp.float32),
        in_specs=[pl.BlockSpec(memory_space=pltpu.VMEM)] * 2,
        out_specs=pl.BlockSpec(memory_space=pltpu.VMEM),
        compiler_params=pltpu.CompilerParams(vmem_limit_bytes=4 * 1024 * 1024),
    )(mine, theirs)


def tail_kernel(strip, block, layers, *refs):
    a_any, g_any = refs[:2]
    strip_refs, (away_ref, kept_ref) = refs[2:-8], refs[-8:-6]
    a_tile, g_whole, columns, inverse, away_vmem, sems = refs[-6:]
    channels = g_any.shape[0]
    n_fsdp, n_factor = lax.axis_size("fsdp"), lax.axis_size("factor")
    fsdp_at, factor_at = lax.axis_index("fsdp"), lax.axis_index("factor")
    core_at, pair_at = factor_at % 2, factor_at // 2
    copies = fetch([a_any, g_any], [a_tile, g_whole], sems.at[0])
    strip_copies = fetch(
        strip_refs,
        [columns.at[pl.ds(at * strip, strip)] for at in range(len(strip_refs))],
        sems.at[1],
    )
    copies[1].wait()
    for at, (layer, other) in enumerate(layers):
        owner = (fsdp_at + n_fsdp - 2 * layer) % n_fsdp
        owner = owner + other * (1 - 2 * (owner % 2))
        rows = pl.ds(pl.multiple_of(owner * strip, strip), strip)
        for to in range(n_factor):
            away, step = 1 - to // (n_factor // 2), to % (n_factor // 2)
            place = 2 * ((pair_at + step) % (n_factor // 2)) + (core_at + away) % 2
            lanes = pl.ds(pl.multiple_of(place * block, block), block)
            inverse[at * strip : (at + 1) * strip, to * block : (to + 1) * block] = g_whole[rows, lanes]
    copies[0].wait()
    for copy in strip_copies:
        copy.wait()
    first = lax.dot_general(
        a_tile[...],
        columns[...],
        (((1,), (1,)), ((), ())),
        precision=lax.Precision.HIGH,
        preferred_element_type=jnp.float32,
    )
    away_vmem[...] = jnp.dot(
        first,
        inverse[:, : channels // 2],
        precision=lax.Precision.HIGH,
        preferred_element_type=jnp.float32,
    )
    away_out = fetch([away_vmem], [away_ref], sems.at[2])
    kept_ref[...] = jnp.dot(
        first,
        inverse[:, channels // 2 :],
        precision=lax.Precision.HIGH,
        preferred_element_type=jnp.float32,
    )
    away_out[0].wait()


def tail_products(a_inverse, g_inverse, strips, layers, block):
    channels, strip = g_inverse.shape[0], strips[0].shape[0]
    rows, depth = a_inverse.shape
    half = (rows, channels // 2)
    return pl.pallas_call(
        lambda *refs: tail_kernel(strip, block, layers, *refs),
        out_shape=[jax.ShapeDtypeStruct(half, jnp.float32)] * 2,
        in_specs=[pl.BlockSpec(memory_space=pl.ANY)] * (2 + len(strips)),
        out_specs=[pl.BlockSpec(memory_space=pl.ANY), pl.BlockSpec(memory_space=pltpu.VMEM)],
        scratch_shapes=[
            pltpu.VMEM((rows, depth), jnp.float32),
            pltpu.VMEM((channels, channels), jnp.float32),
            pltpu.VMEM((channels, depth), jnp.float32),
            pltpu.VMEM((channels, channels), jnp.float32),
            pltpu.VMEM(half, jnp.float32),
            pltpu.SemaphoreType.DMA((3, max(2, len(strips)))),
        ],
        compiler_params=pltpu.CompilerParams(vmem_limit_bytes=26 * 1024 * 1024),
        cost_estimate=pl.CostEstimate(
            flops=6 * rows * channels * (depth + channels),
            bytes_accessed=4 * rows * (depth + channels),
            transcendentals=0,
        ),
    )(a_inverse, g_inverse, *strips)


def conv_kernel(n_images, *refs):
    image_refs, part_refs = refs[:n_images], refs[n_images : n_images + 2]
    out_refs, (shifted, parts, weight, sems) = refs[n_images + 2 : -4], refs[-4:]
    side, channels = image_refs[0].shape[1], image_refs[0].shape[3]
    n_near, depth, block = part_refs[0].shape
    fsdp_at = lax.axis_index("fsdp")
    arrivals = fetch(
        [ref.at[0] for ref in image_refs],
        [shifted.at[1, at, pl.ds(1, side)] for at in range(n_images)],
        sems.at[0],
    )
    part_copies = fetch(part_refs, [parts.at[at] for at in range(2)], sems.at[1])
    fill_shifted(shifted, arrivals)
    for copy in part_copies:
        copy.wait()
    for near in range(n_near):
        for far in range(2):
            owner = (fsdp_at ^ (2 * near + far)) * depth
            weight[pl.ds(pl.multiple_of(owner, 64), depth), :] = parts[far, near]
    for at, ref in enumerate(out_refs):
        total = jnp.zeros((side * side, block), jnp.float32)
        for tap in range(9):
            left = shifted[tap % 3, at, tap // 3 : tap // 3 + side].reshape(side * side, channels)
            total += jnp.dot(
                left,
                weight[tap * channels : (tap + 1) * channels, :],
                preferred_element_type=jnp.float32,
            )
        ref[0] = total.astype(jnp.bfloat16).reshape(side, side, block)


def convolve(images, near_parts, far_parts):
    n_images, (_, side, _, channels) = len(images), images[0].shape
    block = near_parts.shape[2]
    return pl.pallas_call(
        lambda *refs: conv_kernel(n_images, *refs),
        out_shape=[jax.ShapeDtypeStruct((1, side, side, block), jnp.bfloat16)] * n_images,
        in_specs=[pl.BlockSpec(memory_space=pl.ANY)] * (n_images + 2),
        out_specs=[pl.BlockSpec(memory_space=pltpu.VMEM)] * n_images,
        scratch_shapes=[
            pltpu.VMEM((3, n_images, side + 2, side, channels), jnp.bfloat16),
            pltpu.VMEM((2,) + near_parts.shape, jnp.bfloat16),
            pltpu.VMEM((9 * channels, block), jnp.bfloat16),
            pltpu.SemaphoreType.DMA((2, n_images)),
        ],
        compiler_params=pltpu.CompilerParams(vmem_limit_bytes=58 * 1024 * 1024),
        cost_estimate=pl.CostEstimate(
            flops=36 * n_images * side * side * channels * block,
            bytes_accessed=2 * (9 * channels * block + n_images * side * side * channels),
            transcendentals=0,
        ),
    )(*images, near_parts, far_parts)


def side_by_side_kernel(*refs):
    block, n_factor = refs[0].shape[3], lax.axis_size("factor")
    factor_at, n_pair = lax.axis_index("factor"), n_factor // 2
    for at, ref in enumerate(refs[:-1]):
        place = 2 * ((factor_at // 2 + at % n_pair) % n_pair) + (factor_at + at // n_pair) % 2
        refs[-1][:, :, :, pl.ds(pl.multiple_of(place * block, LANES), block)] = ref[...]


def side_by_side(blocks):
    whole = pl.BlockSpec(memory_space=pltpu.VMEM)
    shape = blocks[0].shape[:3] + (len(blocks) * blocks[0].shape[3],)
    return pl.pallas_call(
        side_by_side_kernel,
        out_shape=jax.ShapeDtypeStruct(shape, blocks[0].dtype),
        in_specs=[whole] * len(blocks),
        out_specs=whole,
        compiler_params=pltpu.CompilerParams(vmem_limit_bytes=4 * 1024 * 1024),
    )(*blocks)


def gather_plan(n_layer, n_pair):
    far_layers = sorted(range(1, n_layer), key=lambda step: min(step, n_layer - step))
    waiting = {"layer": [(("layer", layer, 0), None) for layer in far_layers], "side": [], "pair": []}
    for turn, layer in enumerate([0] + far_layers):
        waiting["side"].append((("side", layer, 0), ("layer", layer, 0)))
        for pair in range(1, n_pair):
            waiting["pair"].append((("pair", layer, pair), ("layer", layer, 0)))
            if turn % 2 == 0:
                waiting["pair"].append((("both", layer, pair), ("side", layer, 0)))
            else:
                waiting["side"].append((("both", layer, pair), ("pair", layer, pair)))
    for link in waiting.values():
        link.sort(key=lambda entry: entry[0][0] == "both")
    ready, busy, turns = {None: 0, ("layer", 0, 0): 0}, {link: 0 for link in waiting}, {}
    order, step = [], 0
    while any(waiting.values()):
        for link, entries in waiting.items():
            free = [entry for entry in entries if ready.get(entry[1], step + 1) <= step]
            if busy[link] > step or not free:
                continue
            count = 2 if link == "layer" and step == 0 else 1
            for item, source in free[:count]:
                entries.remove((item, source))
                hops = min(item[1], n_layer - item[1]) if link == "layer" else 1
                busy[link] = step + hops * count
                ready[item] = busy[link]
                turns[link] = turns.get(link, -1) + 1
                order.append((item, source, link, turns[link]))
        step += 1
    return order, ready


def per_device(activations, cotangent, weight, a_factor_old, g_factor_old, a_inverse, g_inverse):
    channels = activations.shape[3]
    n_fsdp, n_factor = lax.axis_size("fsdp"), lax.axis_size("factor")
    n_layer, n_pair = n_fsdp // 2, n_factor // 2
    fsdp_at, factor_at = lax.axis_index("fsdp"), lax.axis_index("factor")
    core_at, pair_at = factor_at % 2, factor_at // 2
    rows, cols = a_factor_old.shape
    strip = channels // n_fsdp
    block = channels // n_factor

    def over_layer(array, step):
        return moved(array, "fsdp", lambda at: at + 2 * step)

    def over_side(array):
        return moved(array, "fsdp", lambda at: at ^ 1)

    def over_pair(array, step):
        return moved(array, "factor", lambda at: at + 2 * step)

    def over_core(array):
        return moved(array, "factor", lambda at: at ^ 1)

    def after(arrays, events):
        return lax.optimization_barrier((arrays, events))[0]

    def transfer(array, item, how):
        if how == "layer":
            return over_layer(array, item[1])
        if how == "pair":
            return over_pair(array, item[2])
        return over_side(array)

    own_cot = cotangent.reshape(-1, channels)
    maps = {("layer", 0, 0): activations}
    plan, ready = gather_plan(n_layer, n_pair)
    sent = {"layer": [], "side": [], "pair": []}
    strips_by_pair = []
    for item, source, link, turn in plan:
        array = activations if source is None else maps[source]
        events = sent[link][max(turn - 2, 0) : turn - 1]
        if link == "pair" and item == [entry[0] for entry in plan if entry[2] == "pair"][-1]:
            events = events + strips_by_pair
        maps[item] = transfer(after(array, events), item, link)
        sent[link].append(maps[item])
        if link == "side" and turn == 0:
            strips = after(own_cot, [maps[item]]).T.reshape(n_fsdp, strip, own_cot.shape[0])
            strips = lax.all_to_all(strips, "fsdp", split_axis=0, concat_axis=0)
        if link == "pair" and turn == 2:
            strips_by_pair = [strips] + [
                over_pair(after(strips, [maps[item]]), step) for step in range(1, n_pair)
            ]
    first_event, last_layer = sent["side"][:1], sent["layer"][-1:]
    near_end, at_end = sent["pair"][-2:-1], sent["pair"][-1:] + sent["side"][-1:]

    aligned = rows % LANES == 0 and channels % LANES == 0 and activations.shape[0] == 1
    images = sorted(maps, key=lambda item: ready[item])
    totals = None
    for batch in (images,):
        owners, pairs = [], []
        for kind, layer, pair in batch:
            owner = (fsdp_at - 2 * layer) % n_fsdp
            owners.append(owner ^ 1 if kind in ("side", "both") else owner)
            pairs.append(pair)
        if aligned:
            totals = add_products(
                [(layer, int(kind in ("side", "both"))) for kind, layer, _ in batch],
                [maps[item] for item in batch], pairs, strips_by_pair, totals, cols, rows
            )
            continue
        for at in range(0, len(batch), 2 * n_pair):
            part = jnp.concatenate([maps[item] for item in batch[at : at + 2 * n_pair]], axis=0)
            col_tile = tile_of_patches(part, fsdp_at * cols, cols)
            cot_tile = jnp.concatenate(
                [
                    lax.dynamic_index_in_dim(strips_by_pair[pair], owner, 0, keepdims=False)
                    for pair, owner in list(zip(pairs, owners))[at : at + 2 * n_pair]
                ],
                axis=1,
            )
            more = []
            for tile in (factor_at ^ 1, factor_at):
                row_tile = tile_of_patches(part, tile * rows, rows)
                more.append(by_rows(col_tile, row_tile))
                more.append(jnp.dot(cot_tile, row_tile, preferred_element_type=jnp.float32))
            totals = more if totals is None else [old + new for old, new in zip(totals, more)]
    if not aligned:
        for at in (1, 3):
            largest = jnp.full((strip, LANES), jnp.max(jnp.abs(totals[at])))
            totals[at] = jnp.concatenate([totals[at], largest], axis=1)

    g_partial = by_rows(after(own_cot, first_event), own_cot).reshape(n_pair, 2, block, channels)
    g_pairs = lax.dynamic_index_in_dim(g_partial, core_at, 1, keepdims=False) + over_core(
        lax.dynamic_index_in_dim(g_partial, 1 - core_at, 1, keepdims=False)
    )
    g_pairs = after(g_pairs, near_end)
    g_sum = lax.dynamic_index_in_dim(g_pairs, pair_at, 0, keepdims=False)
    for step in range(1, n_pair):
        away = lax.dynamic_index_in_dim(g_pairs, (pair_at + step) % n_pair, 0, keepdims=False)
        g_sum = g_sum + over_pair(away, step)
    weight_part = after(weight, last_layer)
    near_parts = [lax.dynamic_slice_in_dim(weight_part, factor_at * block, block, 1)]
    distance = 2
    while distance < n_fsdp:
        both = moved(jnp.stack(near_parts), "fsdp", lambda to, d=distance: to ^ d)
        near_parts = near_parts + [both[k] for k in range(len(near_parts))]
        distance *= 2
    near_stack = jnp.stack(near_parts)
    far_parts = over_side(after(near_stack, at_end))
    distance = n_fsdp // 2
    g_sum = after(g_sum, at_end)
    while distance > 2:
        g_sum = g_sum + moved(g_sum, "fsdp", lambda to, d=distance: to ^ d)
        distance //= 2
    near_images = [activations] + [maps["pair", 0, step] for step in range(1, n_pair)]
    group = near_images + [over_core(image) for image in after(near_images, near_end)]
    theirs = after(totals[1], [far_parts, g_sum] + group)
    theirs = over_core(theirs)
    pixel_total = float(
        activations.shape[0] * activations.shape[1] * activations.shape[2] * n_fsdp * n_factor
    )

    if aligned:
        packed = scale_strips(totals[3], theirs).astype(jnp.float16)
    else:
        largest = totals[3][:, rows : rows + 1] + theirs[:, rows : rows + 1]
        exponent = jnp.floor(jnp.log2(jnp.maximum(largest, 1e-30))) - 14.0
        packed = (totals[3] + theirs)[:, :rows] * jnp.exp2(-exponent)
        exponent = jnp.broadcast_to(exponent, (strip, LANES))
        packed = jnp.concatenate([packed, exponent], axis=1).astype(jnp.float16)
    near_packed = [packed] + [over_layer(packed, step) for step in range(1, n_layer)]

    cov_back = over_core(after(totals[0], [packed]))
    group = after(group, [packed])
    if aligned and block % LANES == 0:
        group_out = convolve(group, near_stack, far_parts)
    else:
        kernel = jnp.stack([part for pair in zip(near_stack, far_parts) for part in pair])
        kernel = jnp.concatenate(
            [
                lax.dynamic_index_in_dim(kernel, fsdp_at ^ at, 0, keepdims=False)
                for at in range(n_fsdp)
            ]
        ).reshape(3, 3, channels, block)
        group_out = lax.conv_general_dilated(
            jnp.concatenate(group),
            kernel,
            (1, 1),
            "SAME",
            dimension_numbers=("NHWC", "HWIO", "NHWC"),
            preferred_element_type=jnp.float32,
        ).astype(jnp.bfloat16)
        group_out = jnp.split(group_out, n_factor)
    far_packed, came = {0: over_side(packed)}, list(group_out)
    for step in sorted(range(1, n_layer), key=lambda step: min(step, n_layer - step)):
        far_packed[step] = over_side(after(near_packed[step], came))
        came = came + [near_packed[step]]
    far_packed = [far_packed[step] for step in range(n_layer)]

    own_maps, block_order = [], []
    outputs = after(list(group_out), far_packed)
    for other in range(2):
        for pair in range(n_pair):
            out = outputs[other * n_pair + pair]
            if pair + other:
                out = moved(out, "factor", lambda at, o=other, p=pair: (at ^ o) - 2 * p)
            own_maps.append(out)
            block_order.append(2 * ((pair_at + pair) % n_pair) + (core_at + other) % 2)
    g_near = moved(after(g_sum, near_packed), "fsdp", lambda to: to ^ 2)
    g_sum = g_sum + after(g_near, far_packed)
    g_side = over_side(g_sum)
    strips_of_grad = [
        array[:, :rows].astype(jnp.float32) * jnp.exp2(array[:, rows : rows + 1].astype(jnp.float32))
        for array in near_packed + far_packed
    ]
    came_from = [(fsdp_at - 2 * step) % n_fsdp for step in range(n_layer)]
    came_from = came_from + [at ^ 1 for at in came_from]
    order = [
        2 * ((pair_at + step) % n_pair) + (core_at + other) % 2
        for other in (1, 0)
        for step in range(n_pair)
    ]
    if aligned and block % LANES == 0:
        away, kept = tail_products(
            after(a_inverse, [cov_back]),
            g_inverse,
            strips_of_grad,
            [(step, other) for other in range(2) for step in range(n_layer)],
            block,
        )
    else:
        inverse = jnp.concatenate(
            [lax.dynamic_slice_in_dim(g_inverse, at * block, block, 1) for at in order], axis=1
        )
        inverse = jnp.concatenate(
            [lax.dynamic_slice_in_dim(inverse, at * strip, strip, 0) for at in came_from]
        )
        partial = lax.dot_general(
            a_inverse,
            jnp.concatenate(strips_of_grad),
            (((1,), (1,)), ((), ())),
            precision=lax.Precision.HIGH,
            preferred_element_type=jnp.float32,
        )
        partial = jnp.dot(
            partial, inverse, precision=lax.Precision.HIGH, preferred_element_type=jnp.float32
        )
        away, kept = partial[:, : channels // 2], partial[:, channels // 2 :]
    by_pair = kept + over_core(away)
    cov_own = totals[2] + after(cov_back, by_pair)
    a_factor = 0.5 * a_factor_old + (0.5 / pixel_total) * cov_own.T
    result = by_pair[:, :block]
    for step in range(1, n_pair):
        back = over_pair(by_pair[:, step * block : (step + 1) * block], step)
        result = result + after(back, a_factor)
    g_sum = g_sum + after(g_side, back)
    natural_grad = result.astype(jnp.bfloat16)


    own_maps = after(own_maps, by_pair)
    if aligned and block % LANES == 0:
        conv_out = side_by_side(own_maps)
    else:
        stacked = jnp.zeros((n_factor,) + own_maps[0].shape, jnp.bfloat16)
        for at, out in zip(block_order, own_maps):
            stacked = lax.dynamic_update_index_in_dim(stacked, out, at, 0)
        conv_out = jnp.concatenate(jnp.split(stacked, n_factor), axis=4)[0]

    g_factor = 0.5 * g_factor_old + 0.5 * g_sum
    return (conv_out, a_factor, g_factor, natural_grad)


def solution(mesh):
    images = P(("fsdp", "factor"), None, None, None)
    return jax.shard_map(
        per_device,
        mesh=mesh,
        in_specs=(
            images,
            images,
            P("fsdp", None),
            P("factor", "fsdp"),
            P("factor", None),
            P("fsdp", "factor"),
            P(),
        ),
        out_specs=(
            images,
            P("factor", "fsdp"),
            P("factor", None),
            P("fsdp", "factor"),
        ),
        check_vma=False,
    )
```
